128 devices in a mesh: blk: 16 (over y_hi, z, core), freq: 8 (over y_lo, x).
Axes of the slice: x: 4, y: 4 (y_hi: 2, y_lo: 2; y = y_hi * 2 + y_lo), z: 4, core: 2. Of those that a mesh axis runs over, the one named last changes fastest.
Arguments:
- spectra: bfloat16 [5120, 34816], P('blk', 'freq'), may hold values from -16 to 16, as said below
- labels: int32 [5120], replicated, may hold values from 0 to 7
- wedges: int32 [8, 17408], P(None, 'freq'), may hold values 0 or 1
- shells: int32 [17408], P('freq'), may hold values from 0 to 27, never falling along the last dimension, each value on 1 to 1243 neighbouring positions
- shell_weight: float32 [28], replicated, may hold values from 0.2 to 5
Outputs:
- scores: float32 [5120, 5120], P('blk', 'freq')
The draws below stay inside these ranges and needn't reach their ends.
Inputs may be any that keep to these rules, and one draw needn't show every extreme that they name: `spectra`: finite values. `shells`: never falling along the voxels; each shell has 1 to 1243 voxels.
All inputs are finite; a program needn't handle non-finite values. No bound on the sum of `wedges` on one device may be relied on, other than what follows from the above.
Results may differ from the reference program's by a relative error of at most 0.0003.
Values may be sent and summed in bfloat16 or wider, within the bound.
No kernel may reach another device: no remote copies, remote signals or barrier semaphores. Data moves between devices by JAX's collectives and lax.ppermute only.
A program may use at most 128 MiB of HBM per device.

```python
import math
import jax
import jax.numpy as jnp
import numpy as np
from jax import lax

VOX = 17408
SHELLS = 28
CLASSES = 8
P_BLK = 320
NP = 5120
N_BLK = 16


def draw_spectra(key, part):
    key = jax.random.fold_in(key, 11)
    first, second, third = jax.random.split(key, 3)
    width = 2 * VOX
    templates = jax.random.normal(first, (4, width), jnp.float32)
    mixing = jax.random.normal(second, (NP, 4), jnp.float32) * 0.5
    signal = mixing[:, 0:1] * templates[0] + mixing[:, 1:2] * templates[1]
    signal = signal + mixing[:, 2:3] * templates[2] + mixing[:, 3:4] * templates[3]
    ramp = 0.4 + 2.0 * jnp.arange(width, dtype=jnp.float32) / width
    noise = jax.random.normal(third, (NP, width), jnp.float32)
    values = signal + noise * ramp
    return jnp.clip(values, -16.0, 16.0).astype(jnp.bfloat16)


def set_ends(result, stream_key, low, high):
    spot = [jax.random.randint(jax.random.fold_in(stream_key, axis), (), 0, length) for axis, length in enumerate(result.shape)]
    longest = result.shape.index(max(result.shape))
    next_to = spot[:longest] + [(spot[longest] + 1) % result.shape[longest]] + spot[longest + 1:]
    return result.at[tuple(spot)].set(low).at[tuple(next_to)].set(high)


def rank_bounds(number_of, slope):
    portions = [(1 << 20) // math.isqrt(grade ** slope) + 1 for grade in range(1, number_of + 1)]
    deviation = 1 + sum(portions) // (1 << 30)
    return np.cumsum(np.array([max(1, weight // deviation) for weight in portions]))


def ranked(own_key, dims, amount, lean):
    listing = rank_bounds(amount, lean)
    ticket = jax.random.randint(jax.random.fold_in(own_key, 1), dims, 0, int(listing[amount - 1]))
    grade = jnp.searchsorted(jnp.asarray(listing, jnp.int32), ticket, side="right")
    return jax.random.permutation(jax.random.fold_in(own_key, 2), amount)[grade].astype(jnp.int32)


def split_up(number_of, total, limit, skew):
    portions = [(1 << 20) // math.isqrt(standing ** skew) + 1 for standing in range(2, number_of + 1)]
    surplus, counts = total - limit - (number_of - 1), [1] * (number_of - 1)
    while surplus > 0:
        movable = [i for i in range(number_of - 1) if counts[i] < limit]
        mass, remaining = sum([portions[i] for i in movable]), surplus
        for i in movable:
            more = min(limit - counts[i], max(1, remaining * portions[i] // mass), surplus)
            counts[i] = counts[i] + more
            surplus = surplus - more
    return np.array([limit] + counts)


def uneven(rng, count, total, limit, slope):
    if count == 2:
        one = jax.random.randint(rng, (), max(1, total - limit), min(limit, total - 1) + 1)
        return jnp.stack([one, total - one])
    lengths = jnp.asarray(split_up(count, total, limit, slope), jnp.int32)
    twos = (count - 1) // 2
    donor, taker = lengths[1:1 + 2 * twos:2], lengths[2:2 + 2 * twos:2]
    margin = jnp.minimum(donor - 1, limit - taker)
    moved = jax.random.randint(jax.random.fold_in(rng, 1), (twos,), 0, 1 << 20) % (margin + 1)
    lengths = lengths.at[1:1 + 2 * twos:2].set(donor - moved).at[2:2 + 2 * twos:2].set(taker + moved)
    return lengths[jax.random.permutation(jax.random.fold_in(rng, 2), count)]


def setup_inputs(seed: int = 0) -> dict:
    splits = jax.random.split(jax.random.key(seed), 6)
    return {
        "spectra": draw_spectra(jax.random.fold_in(splits[5], 71), 0),
        "labels": set_ends(ranked(splits[1], (NP,), CLASSES, 2), jax.random.fold_in(splits[1], 3), 0, CLASSES - 1).astype(jnp.int32),
        "wedges": set_ends((jax.random.randint(splits[2], (CLASSES, VOX), 0, 3) < 2).astype(jnp.int32), jax.random.fold_in(splits[2], 1), 0, 1),
        "shells": jnp.searchsorted(jnp.cumsum(uneven(splits[3], SHELLS, VOX, 2 * VOX // SHELLS, 1)), jnp.arange(VOX), side="right").astype(jnp.int32),
        "shell_weight": jnp.clip(jnp.exp(jax.random.uniform(splits[4], (SHELLS,), jnp.float32, math.log(0.2), math.log(5.0))), 0.2, 5.0),
    }


def reference(spectra, labels, wedges, shells, shell_weight):
    keep_mask = jnp.repeat(wedges[labels], 2, axis=1).astype(jnp.bfloat16)
    masked = spectra * keep_mask
    voxel_weight = shell_weight[shells]
    pair_weight = jnp.repeat(voxel_weight, 2)
    weighted = (masked.astype(jnp.float32) * pair_weight).astype(jnp.bfloat16)
    full_products = jnp.dot(weighted, masked.T, preferred_element_type=jnp.float32)
    block_ids = jnp.arange(NP, dtype=jnp.int32) // P_BLK
    offsets = (block_ids[None, :] - block_ids[:, None]) % N_BLK
    lower_rows = block_ids[:, None] < N_BLK // 2
    direct = jnp.logical_or(offsets < N_BLK // 2, jnp.logical_and(offsets == N_BLK // 2, lower_rows))
    products = jnp.where(direct, full_products, full_products.T)
    squares = masked.astype(jnp.float32) ** 2 * pair_weight
    wedge_pairs = jnp.repeat(wedges, 2, axis=1).astype(jnp.float32)
    energy = jnp.dot(squares, wedge_pairs.T, precision=lax.Precision.HIGHEST)
    row_energy = energy[:, labels]
    column_energy = row_energy.T
    return products / jnp.sqrt(row_energy * column_energy + 1e-06)
```

```python
import jax
import jax.numpy as jnp
from jax import lax
from jax.sharding import PartitionSpec as P

BOTH = ("blk", "freq")


def places():
    return [
        (yh, z, c, f) for yh in range(2) for z in range(4) for c in range(2) for f in range(8)
    ]


def place_index(yh, z, c, f):
    return (((yh % 2) * 4 + z % 4) * 2 + c % 2) * 8 + f % 8


def route(dyh, dz, dc):
    return [(place_index(yh, z, c, f), place_index(yh + dyh, z + dz, c + dc, f)) for yh, z, c, f in places()]


def send(block, dyh=0, dz=0, dc=0):
    return lax.ppermute(block, BOTH, route(dyh, dz, dc))


def per_device(spectra, labels, wedges, shells, shell_weight):
    rows, width = spectra.shape
    half = width // 2
    classes = wedges.shape[0]
    shell_count = shell_weight.shape[0]
    blk = lax.axis_index("blk")
    core, z, yh = blk % 2, (blk // 2) % 4, blk // 8
    freq = lax.axis_index("freq")
    first_core = core == 0
    class_range = jnp.arange(classes, dtype=jnp.int32)

    own_labels = lax.dynamic_slice_in_dim(labels, blk * rows, rows)
    own_hot = (own_labels[:, None] == class_range[None, :]).astype(jnp.bfloat16)
    wedge_pairs = jnp.repeat(wedges.astype(jnp.bfloat16), 2, axis=1)
    keep = jnp.dot(own_hot, wedge_pairs, preferred_element_type=jnp.float32)
    own = spectra * keep.astype(jnp.bfloat16)

    shell_hot = (shells[:, None] == jnp.arange(shell_count, dtype=jnp.int32)[None, :]).astype(jnp.float32)
    voxel_weight = jnp.dot(shell_hot, shell_weight, precision=lax.Precision.HIGHEST)
    weight = jnp.repeat(voxel_weight, 2)[None, :]

    def cols(block, which):
        return lax.dynamic_slice_in_dim(block, which * half, half, 1)

    high = z // 2
    next_high = ((z + 1) % 4) // 2
    sibling = send(own, dc=1)
    partner_a = send(cols(own, 1 - yh), dyh=1)
    following_c = send(own, dz=-1)
    previous_c = send(cols(own, next_high), dz=1)
    partner_b = send(cols(own, yh), dyh=1)
    partner_previous_c = send(partner_a, dz=1)
    partner_sibling = send(partner_a, dc=1)
    following_s = send(following_c, dc=1)
    previous_s = send(previous_c, dc=1)
    partner_previous_s = send(partner_previous_c, dc=1)

    squares = own.astype(jnp.float32) ** 2 * weight
    partial_energy = lax.dot_general(
        wedge_pairs.astype(jnp.float32), squares, (((1,), (1,)), ((), ())), precision=lax.Precision.HIGHEST
    )
    energy = lax.psum(partial_energy, "freq")
    energy_all = lax.all_gather(energy, "blk", axis=0, tiled=False)

    def scaled(block, weighted, scale):
        factor = jnp.where(weighted, scale, jnp.ones_like(scale))
        return (block.astype(jnp.float32) * factor).astype(jnp.bfloat16)

    def tile(a, b, on_b, scale):
        return lax.dot_general(
            scaled(a, jnp.logical_not(on_b), scale),
            scaled(b, on_b, scale),
            (((1,), (1,)), ((), ())),
            preferred_element_type=jnp.float32,
        )

    def in_order(mine, other, axis=0):
        return jnp.where(
            first_core,
            jnp.concatenate([mine, other], axis),
            jnp.concatenate([other, mine], axis),
        )

    def place(dyh, dz):
        return ((yh + dyh) % 2) * 4 + (z + dz) % 4

    def ahead(a, b):
        return (a - b) % 8 < 4

    scale_yh, scale_high = cols(weight, yh), cols(weight, high)
    partner_full = jnp.where(
        yh == 0,
        jnp.concatenate([partner_a, partner_b], 1),
        jnp.concatenate([partner_b, partner_a], 1),
    )
    following = in_order(following_c, following_s)
    lower_yh, lower_z = yh == 0, z < 2

    q1 = in_order(tile(own, own, False, weight), tile(sibling, own, first_core, weight))
    q2 = tile(following, own, ahead(place(0, 1), place(0, 0)), weight)
    q3 = tile(
        jnp.where(lower_z, cols(following, high), in_order(previous_c, previous_s)),
        jnp.where(lower_z, previous_c, cols(following_c, high)),
        jnp.where(lower_z, ahead(place(0, 1), place(0, -1)), ahead(place(0, -1), place(0, 1))),
        scale_high,
    )
    own_yh, sibling_yh = cols(own, yh), cols(sibling, yh)
    b4 = jnp.where(lower_yh, own_yh, partner_a)
    q4 = in_order(
        tile(jnp.where(lower_yh, partner_a, own_yh), b4, True, scale_yh),
        tile(
            jnp.where(lower_yh, partner_sibling, sibling_yh), b4, jnp.logical_not(first_core), scale_yh
        ),
    )
    q5 = tile(following, partner_full, ahead(place(0, 1), place(1, 0)), weight)
    q6 = tile(
        jnp.where(lower_yh, cols(following, yh), in_order(partner_previous_c, partner_previous_s)),
        jnp.where(lower_yh, partner_previous_c, cols(following_c, yh)),
        jnp.where(lower_yh, ahead(place(0, 1), place(1, -1)), ahead(place(1, -1), place(0, 1))),
        scale_yh,
    )
    slices = rows // 4

    def summed(tiles):
        stack = jnp.stack([t.reshape(8, slices, rows) for t in tiles], 1)
        return jnp.sum(lax.all_to_all(stack, "freq", 0, 0, tiled=True), 0)

    r1, r2, r3, r4, r5, r6 = summed([q1, q2, q3, q4, q5, q6])
    from_previous = send(jnp.stack([r2, r3, r5, r6]), dz=1)
    from_following = send(r3, dz=-1)
    from_partner = send(jnp.stack([r4, r5]), dyh=1)
    from_diagonal = send(r6, dyh=1, dz=-1)
    near = jnp.stack([r1, r2, from_previous[1] + from_following, from_previous[0]])
    far = jnp.stack([r4 + from_partner[0], from_partner[1], from_previous[3] + from_diagonal, from_previous[2]])
    near, far = (
        lax.dynamic_slice_in_dim(jnp.concatenate([part, part]), (4 - z) % 4, 4, 0) for part in (near, far)
    )
    pieces = jnp.where(lower_yh, jnp.concatenate([near, far]), jnp.concatenate([far, near]))
    found = lax.all_to_all(pieces, "freq", 0, 0, tiled=True).reshape(2 * rows, rows)
    swapped = send(lax.dynamic_slice_in_dim(found, (1 - core) * rows, rows, 0), dc=1)
    by_row = in_order(lax.dynamic_slice_in_dim(found, core * rows, rows, 0), swapped, 1)

    step_y, step_z = (freq // 4 + yh) % 2, (freq % 4 - z) % 4
    same_y = step_y == 0
    inner_z = jnp.logical_or(z == 1, z == 2)
    is_row = jnp.where(
        step_z == 0,
        jnp.logical_or(same_y, yh == 1),
        jnp.where(step_z == 1, False, jnp.where(step_z == 2, jnp.where(same_y, inner_z, yh == 0), True)),
    )
    products = jnp.where(is_row, by_row, found.T)

    column_labels = lax.dynamic_slice_in_dim(labels, freq * 2 * rows, 2 * rows)
    column_energy = lax.dynamic_slice_in_dim(energy_all, freq * 2, 2, 0)
    column_energy = jnp.concatenate([column_energy[0], column_energy[1]], 1)
    row_side = jnp.zeros_like(products)
    column_side = jnp.zeros_like(products)
    for d in range(classes):
        row_side = jnp.where(column_labels[None, :] == d, energy[d][:, None], row_side)
        column_side = jnp.where(own_labels[:, None] == d, column_energy[d][None, :], column_side)
    return products / jnp.sqrt(row_side * column_side + 1e-06)


def solution(mesh):
    placed = (P("blk", "freq"), P(), P(None, "freq"), P("freq"), P())
    return jax.shard_map(
        per_device, mesh=mesh, in_specs=placed, out_specs=P("blk", "freq"), check_vma=False
    )
```

```python
import jax
import jax.numpy as jnp
from jax import lax
from jax.experimental import pallas as pl
from jax.experimental.pallas import tpu as pltpu
from jax.sharding import PartitionSpec as P

BOTH = ("blk", "freq")
VMEM_BYTES = 60 * 1024 * 1024
LANES = 128


def places():
    return [
        (yh, z, c, f) for yh in range(2) for z in range(4) for c in range(2) for f in range(8)
    ]


def place_index(yh, z, c, f):
    return (((yh % 2) * 4 + z % 4) * 2 + c % 2) * 8 + f % 8


def route(dyh, dz, dc):
    return [(place_index(yh, z, c, f), place_index(yh + dyh, z + dz, c + dc, f)) for yh, z, c, f in places()]


def send(block, dyh=0, dz=0, dc=0):
    return lax.ppermute(block, BOTH, route(dyh, dz, dc))


def together(*arrays):
    return lax.optimization_barrier(arrays)


def scaled(block, weighted, weight):
    factor = jnp.where(jnp.full(weight.shape, weighted, jnp.int32) > 0, weight, 1.0)
    return (block.astype(jnp.float32) * factor).astype(jnp.bfloat16)


def gram(a, b):
    return lax.dot_general(a, b, (((1,), (1,)), ((), ())), preferred_element_type=jnp.float32)


CORE, YH, LOW, HIGH, NEXT_HIGH, ON_B2, ON_B3, ON_B5, ON_B6, Z = range(10)


def mask_kernel(info, shell_weight, hot, spectra, wedges, shells, own, to_partner, to_next, pairs, weight):
    half = spectra.shape[1] // 2
    step = 2 * LANES

    @pl.when(pl.program_id(0) == 0)
    def _():
        place = lax.broadcasted_iota(jnp.int32, (LANES, step), 0)
        spread = (lax.broadcasted_iota(jnp.int32, (LANES, step), 1) // 2 == place).astype(jnp.bfloat16)

        def widen(x):
            return jnp.dot(x, spread, preferred_element_type=jnp.float32)

        for j in range(spectra.shape[1] // step):
            some, wide = pl.ds(j * LANES, LANES), pl.ds(j * step, step)
            pairs[:, wide] = widen(wedges[:, some].astype(jnp.float32).astype(jnp.bfloat16)).astype(jnp.bfloat16)
            shell = shells[:, some]
            value = jnp.zeros(shell.shape, jnp.float32)
            for k in range(shell_weight.shape[0]):
                value = jnp.where(shell == k, shell_weight[k], value)
            top = value.astype(jnp.bfloat16)
            rest = value - top.astype(jnp.float32)
            middle = rest.astype(jnp.bfloat16)
            low = (rest - middle.astype(jnp.float32)).astype(jnp.bfloat16)
            weight[:, wide] = (widen(top) + widen(middle)) + widen(low)

    keep = jnp.dot(hot[...], pairs[...], preferred_element_type=jnp.float32).astype(jnp.bfloat16)
    own[...] = spectra[...] * keep
    to_partner[...] = own[:, pl.ds(pl.multiple_of((1 - info[YH]) * half, LANES), half)]
    to_next[...] = own[:, pl.ds(pl.multiple_of(info[NEXT_HIGH] * half, LANES), half)]


def masked_blocks(info, shell_weight, hot, spectra, wedges, shells):
    rows, width = spectra.shape
    classes = wedges.shape[0]
    part = rows // 4
    whole = lambda *shape: pl.BlockSpec(shape, lambda i, info: (0, 0))
    slab = lambda n: pl.BlockSpec((part, n), lambda i, info: (i, 0))
    return pl.pallas_call(
        mask_kernel,
        grid_spec=pltpu.PrefetchScalarGridSpec(
            num_scalar_prefetch=1,
            grid=(4,),
            in_specs=[
                pl.BlockSpec(memory_space=pltpu.SMEM),
                slab(classes),
                slab(width),
                whole(classes, width // 2),
                whole(1, width // 2),
            ],
            out_specs=[slab(width), slab(width // 2), slab(width // 2), whole(classes, width), whole(1, width)],
        ),
        out_shape=[
            jax.ShapeDtypeStruct((rows, width), jnp.bfloat16),
            jax.ShapeDtypeStruct((rows, width // 2), jnp.bfloat16),
            jax.ShapeDtypeStruct((rows, width // 2), jnp.bfloat16),
            jax.ShapeDtypeStruct((classes, width), jnp.bfloat16),
            jax.ShapeDtypeStruct((1, width), jnp.float32),
        ],
        compiler_params=pltpu.CompilerParams(vmem_limit_bytes=VMEM_BYTES),
    )(info, shell_weight, hot, spectra, wedges, shells)


def mine(i):
    return jnp.minimum(i, 1)


def others(i):
    return jnp.maximum(i - 2, 0)


def rank(i, info):
    return jnp.where(i < 2, info[CORE], 1 - info[CORE]) * 2 + i % 2


def first_kernel(info, a_mine, a_other, b, weight, out):
    i = pl.program_id(0)
    w = weight[...]
    slices = out.shape[1]

    def product(a, on_b):
        tile = gram(scaled(a[...], 1 - on_b, w), scaled(b[...], on_b, w))
        out[...] = tile.reshape(2, slices, tile.shape[1])

    @pl.when(i < 2)
    def _():
        product(a_mine, 0)

    @pl.when(i >= 2)
    def _():
        product(a_other, 1 - info[CORE])


def first_tiles(info, own, sibling, weight):
    rows, width = own.shape
    part = rows // 2
    return pl.pallas_call(
        first_kernel,
        grid_spec=pltpu.PrefetchScalarGridSpec(
            num_scalar_prefetch=1,
            grid=(4,),
            in_specs=[
                pl.BlockSpec((part, width), lambda i, info: (mine(i), 0)),
                pl.BlockSpec((part, width), lambda i, info: (others(i), 0)),
                pl.BlockSpec((rows, width), lambda i, info: (0, 0)),
                pl.BlockSpec((1, width), lambda i, info: (0, 0)),
            ],
            out_specs=pl.BlockSpec((2, part // 2, rows), lambda i, info: (rank(i, info), 0, 0)),
        ),
        out_shape=jax.ShapeDtypeStruct((8, part // 2, rows), jnp.float32),
        compiler_params=pltpu.CompilerParams(vmem_limit_bytes=VMEM_BYTES),
    )(info, own, sibling, own, weight)


def fourth_kernel(info, own, own_a, sibling_a, partner, partner_a, partner_sibling_a, weight, out):
    i = pl.program_id(0)
    w = weight[...]
    slices = out.shape[1]

    def product(a, b, on_b):
        tile = gram(scaled(a[...], 1 - on_b, w), scaled(b[...], on_b, w))
        out[...] = tile.reshape(2, slices, tile.shape[1])

    lower = info[YH] == 0
    for is_mine, is_lower, a, b in (
        (True, True, partner_a, own),
        (True, False, own_a, partner),
        (False, True, partner_sibling_a, own),
        (False, False, sibling_a, partner),
    ):

        @pl.when(jnp.logical_and((i < 2) == is_mine, lower == is_lower))
        def _(a=a, b=b, on_b=1 if is_mine else info[CORE]):
            product(a, b, on_b)


def fourth_tiles(info, own, sibling, partner, partner_sibling, weight):
    rows, half = partner.shape
    part = rows // 2
    return pl.pallas_call(
        fourth_kernel,
        grid_spec=pltpu.PrefetchScalarGridSpec(
            num_scalar_prefetch=1,
            grid=(4,),
            in_specs=[
                pl.BlockSpec((rows, half), lambda i, info: (0, info[YH])),
                pl.BlockSpec((part, half), lambda i, info: (mine(i), info[YH])),
                pl.BlockSpec((part, half), lambda i, info: (others(i), info[YH])),
                pl.BlockSpec((rows, half), lambda i, info: (0, 0)),
                pl.BlockSpec((part, half), lambda i, info: (mine(i), 0)),
                pl.BlockSpec((part, half), lambda i, info: (others(i), 0)),
                pl.BlockSpec((1, half), lambda i, info: (0, info[YH])),
            ],
            out_specs=pl.BlockSpec((2, part // 2, rows), lambda i, info: (rank(i, info), 0, 0)),
        ),
        out_shape=jax.ShapeDtypeStruct((8, part // 2, rows), jnp.float32),
        compiler_params=pltpu.CompilerParams(vmem_limit_bytes=VMEM_BYTES),
    )(info, own, own, sibling, partner, partner, partner_sibling, weight)


def late_kernel(
    info, own, near_half, far_half, previous, diagonal, following_high, following_yh, a_mine, a_other,
    previous_mine, previous_other, diagonal_mine, diagonal_other, weight, out, own_b, partner_b, third_b, sixth_b,
):
    i = pl.program_id(0)
    half = previous.shape[1]
    slices = out.shape[2]
    lower, low = info[YH] == 0, info[LOW] == 1

    def span(which):
        return pl.ds(pl.multiple_of(which * half, LANES), half)

    at_yh, at_other, at_high = span(info[YH]), span(1 - info[YH]), span(info[HIGH])

    @pl.when(i == 0)
    def _():
        own_b[...] = scaled(own[...], info[ON_B2], weight[...])
        partner_b[:, at_yh] = scaled(near_half[...], info[ON_B5], weight[:, at_yh])
        partner_b[:, at_other] = scaled(far_half[...], info[ON_B5], weight[:, at_other])

        @pl.when(low)
        def _():
            third_b[...] = scaled(previous[...], info[ON_B3], weight[:, at_high])

        @pl.when(jnp.logical_not(low))
        def _():
            third_b[...] = scaled(following_high[...], info[ON_B3], weight[:, at_high])

        @pl.when(lower)
        def _():
            sixth_b[...] = scaled(diagonal[...], info[ON_B6], weight[:, at_yh])

        @pl.when(jnp.logical_not(lower))
        def _():
            sixth_b[...] = scaled(following_yh[...], info[ON_B6], weight[:, at_yh])

    def put(k, a, on_b, w, b):
        tile = gram(scaled(a, 1 - on_b, w), b[...])
        out[:, k] = tile.reshape(2, slices, tile.shape[1])

    def products(a, earlier, across):
        put(0, a[...], info[ON_B2], weight[...], own_b)
        put(2, a[...], info[ON_B5], weight[...], partner_b)

        @pl.when(low)
        def _():
            put(1, a[:, at_high], info[ON_B3], weight[:, at_high], third_b)

        @pl.when(jnp.logical_not(low))
        def _():
            put(1, earlier[...], info[ON_B3], weight[:, at_high], third_b)

        @pl.when(lower)
        def _():
            put(3, a[:, at_yh], info[ON_B6], weight[:, at_yh], sixth_b)

        @pl.when(jnp.logical_not(lower))
        def _():
            put(3, across[...], info[ON_B6], weight[:, at_yh], sixth_b)

    @pl.when(i < 2)
    def _():
        products(a_mine, previous_mine, diagonal_mine)

    @pl.when(i >= 2)
    def _():
        products(a_other, previous_other, diagonal_other)


def late_tiles(info, own, near_half, far_half, previous, previous_s, diagonal, diagonal_s, following, following_s, weight):
    rows, width = own.shape
    half, part = width // 2, rows // 2
    full = lambda n, at=lambda info: 0: pl.BlockSpec((rows, n), lambda i, info: (0, at(info)))
    slab = lambda n, which: pl.BlockSpec((part, n), lambda i, info: (which(i), 0))
    return pl.pallas_call(
        late_kernel,
        grid_spec=pltpu.PrefetchScalarGridSpec(
            num_scalar_prefetch=1,
            grid=(4,),
            in_specs=[
                full(width),
                full(half),
                full(half),
                full(half),
                full(half),
                full(half, lambda info: info[HIGH]),
                full(half, lambda info: info[YH]),
                slab(width, mine),
                slab(width, others),
                slab(half, mine),
                slab(half, others),
                slab(half, mine),
                slab(half, others),
                pl.BlockSpec((1, width), lambda i, info: (0, 0)),
            ],
            out_specs=pl.BlockSpec((2, 4, part // 2, rows), lambda i, info: (rank(i, info), 0, 0, 0)),
            scratch_shapes=[
                pltpu.VMEM((rows, width), jnp.bfloat16),
                pltpu.VMEM((rows, width), jnp.bfloat16),
                pltpu.VMEM((rows, half), jnp.bfloat16),
                pltpu.VMEM((rows, half), jnp.bfloat16),
            ],
        ),
        out_shape=jax.ShapeDtypeStruct((8, 4, part // 2, rows), jnp.float32),
        compiler_params=pltpu.CompilerParams(vmem_limit_bytes=VMEM_BYTES),
    )(
        info, own, near_half, far_half, previous, diagonal, following, following, following, following_s,
        previous, previous_s, diagonal, diagonal_s, weight,
    )


def gather_kernel(info, r1, r2, r4, from_previous, from_following, from_partner, from_diagonal, out):
    yh, z = info[YH], info[Z]

    def put(dyh, dz, value):
        out[(yh + dyh) % 2 * 4 + (z + dz) % 4] = value

    put(0, 0, r1[...])
    put(0, 1, r2[...])
    put(0, 2, from_previous[1] + from_following[...])
    put(0, 3, from_previous[0])
    put(1, 0, r4[...] + from_partner[0])
    put(1, 1, from_partner[1])
    put(1, 2, from_previous[3] + from_diagonal[...])
    put(1, 3, from_previous[2])


def gathered(info, *parts):
    slices, rows = parts[0].shape
    vmem = pl.BlockSpec(memory_space=pltpu.VMEM)
    return pl.pallas_call(
        gather_kernel,
        in_specs=[pl.BlockSpec(memory_space=pltpu.SMEM)] + [vmem] * len(parts),
        out_specs=vmem,
        out_shape=jax.ShapeDtypeStruct((8, slices, rows), jnp.float32),
    )(info, *parts)


def final_kernel(info, found, swapped, root, out):
    rows = swapped.shape[0]
    core, by_row = info[0], info[1]

    for is_first in (True, False):

        @pl.when(jnp.logical_and(by_row == 1, (core == 0) == is_first))
        def _(is_first=is_first):
            kept = found[:rows] if is_first else found[rows:]
            pair = (kept, swapped[...]) if is_first else (swapped[...], kept)
            out[...] = jnp.concatenate(pair, 1) / root[...]

    @pl.when(by_row == 0)
    def _():
        out[...] = found[...].T / root[...]


def finished(info, found, swapped, root):
    vmem = pl.BlockSpec(memory_space=pltpu.VMEM)
    return pl.pallas_call(
        final_kernel,
        in_specs=[pl.BlockSpec(memory_space=pltpu.SMEM), vmem, vmem, vmem],
        out_specs=vmem,
        out_shape=jax.ShapeDtypeStruct(root.shape, jnp.float32),
    )(info, found, swapped, root)


def per_device(spectra, labels, wedges, shells, shell_weight):
    rows, width = spectra.shape
    half = width // 2
    classes = wedges.shape[0]
    blk = lax.axis_index("blk")
    core, z, yh = blk % 2, (blk // 2) % 4, blk // 8
    freq = lax.axis_index("freq")

    def place(dyh, dz):
        return ((yh + dyh) % 2) * 4 + (z + dz) % 4

    def ahead(a, b):
        return ((a - b) % 8 < 4).astype(jnp.int32)

    low, lower = z < 2, yh == 0
    info = jnp.stack(
        [
            core,
            yh,
            low.astype(jnp.int32),
            z // 2,
            ((z + 1) % 4) // 2,
            ahead(place(0, 1), place(0, 0)),
            jnp.where(low, ahead(place(0, 1), place(0, -1)), ahead(place(0, -1), place(0, 1))),
            ahead(place(0, 1), place(1, 0)),
            jnp.where(lower, ahead(place(0, 1), place(1, -1)), ahead(place(1, -1), place(0, 1))),
            z,
        ]
    ).astype(jnp.int32)

    class_range = jnp.arange(classes, dtype=jnp.int32)
    own_labels = lax.dynamic_slice_in_dim(labels, blk * rows, rows)
    hot = (own_labels[:, None] == class_range[None, :]).astype(jnp.bfloat16)
    own, to_partner, to_next, pairs, weight = masked_blocks(info, shell_weight, hot, spectra, wedges, shells[None, :])

    following = send(own, dz=-1)
    partner_a = send(to_partner, dyh=1)
    previous = send(to_next, dz=1)
    sibling = send(own, dc=1)

    squares = own.astype(jnp.float32) ** 2 * weight
    partial_energy = lax.dot_general(
        pairs.astype(jnp.float32), squares, (((1,), (1,)), ((), ())), precision=lax.Precision.HIGHEST
    )
    q1 = first_tiles(info, own, sibling, weight)
    q1 = jnp.concatenate([q1, jnp.broadcast_to(partial_energy[None], (8, classes, rows))], 1)
    r1 = jnp.sum(lax.all_to_all(q1, "freq", 0, 0, tiled=True), 0)
    energy, r1 = r1[rows // 4 :], r1[: rows // 4]
    to_partner_b = lax.dynamic_slice_in_dim(own, yh * half, half, 1)
    partner_a, previous, to_partner_b, r1, energy = together(partner_a, previous, to_partner_b, r1, energy)

    partner_b = send(to_partner_b, dyh=1)
    diagonal = send(partner_a, dz=1)
    partner_sibling = send(partner_a, dc=1)
    previous_s = send(previous, dc=1)
    q4 = fourth_tiles(info, own, sibling, partner_a, partner_sibling, weight)
    r4 = jnp.sum(lax.all_to_all(q4, "freq", 0, 0, tiled=True), 0)
    energy_all = lax.all_to_all(jnp.broadcast_to(energy[None], (16, classes, rows)), "blk", 0, 0, tiled=True)
    column_labels = lax.dynamic_slice_in_dim(labels, freq * 2 * rows, 2 * rows)
    column_energy = lax.dynamic_slice_in_dim(energy_all, freq * 2, 2, 0)
    column_energy = jnp.concatenate([column_energy[0], column_energy[1]], 1)
    row_side = jnp.zeros((rows, 2 * rows), jnp.float32)
    column_side = jnp.zeros((rows, 2 * rows), jnp.float32)
    for d in range(classes):
        row_side = jnp.where(column_labels[None, :] == d, energy[d][:, None], row_side)
        column_side = jnp.where(own_labels[:, None] == d, column_energy[d][None, :], column_side)
    root = jnp.sqrt(row_side * column_side + 1e-06)
    following, diagonal, partner_b, r4, root = together(following, diagonal, partner_b, r4, root)

    following_s = send(following, dc=1)
    diagonal_s = send(diagonal, dc=1)
    late = late_tiles(
        info, own, partner_a, partner_b, previous, previous_s, diagonal, diagonal_s, following, following_s, weight
    )
    late = jnp.sum(lax.all_to_all(late, "freq", 0, 0, tiled=True), 0)

    from_previous = send(late, dz=1)
    from_following = send(late[1], dz=-1)
    from_partner = send(jnp.stack([r4, late[2]]), dyh=1)
    from_diagonal = send(late[3], dyh=1, dz=-1)
    from_previous, from_following, from_partner, from_diagonal = together(
        from_previous, from_following, from_partner, from_diagonal
    )
    pieces = gathered(info, r1, late[0], r4, from_previous, from_following, from_partner, from_diagonal)
    found = lax.all_to_all(pieces, "freq", 0, 0, tiled=True).reshape(2 * rows, rows)
    swapped = send(lax.dynamic_slice_in_dim(found, (1 - core) * rows, rows, 0), dc=1)

    step_y, step_z = (freq // 4 + yh) % 2, (freq % 4 - z) % 4
    same_y = step_y == 0
    inner_z = jnp.logical_or(z == 1, z == 2)
    by_row = jnp.where(
        step_z == 0,
        jnp.logical_or(same_y, yh == 1),
        jnp.where(step_z == 1, False, jnp.where(step_z == 2, jnp.where(same_y, inner_z, lower), True)),
    )
    return finished(jnp.stack([core, by_row.astype(jnp.int32)]), found, swapped, root)


def solution(mesh):
    placed = (P("blk", "freq"), P(), P(None, "freq"), P("freq"), P())
    return jax.shard_map(
        per_device, mesh=mesh, in_specs=placed, out_specs=P("blk", "freq"), check_vma=False
    )
```

```python
import jax
import jax.numpy as jnp
from jax import lax
from jax.experimental import pallas as pl
from jax.experimental.pallas import tpu as pltpu
from jax.sharding import PartitionSpec as P

BOTH = ("blk", "freq")
VMEM_BYTES = 60 * 1024 * 1024
LANES = 128
PARAMS = pltpu.CompilerParams(vmem_limit_bytes=VMEM_BYTES)
VMEM = pl.BlockSpec(memory_space=pltpu.VMEM)
SMEM = pl.BlockSpec(memory_space=pltpu.SMEM)
ANY = pl.BlockSpec(memory_space=pl.ANY)


def places():
    return [
        (yh, z, c, f) for yh in range(2) for z in range(4) for c in range(2) for f in range(8)
    ]


def place_index(yh, z, c, f):
    return (((yh % 2) * 4 + z % 4) * 2 + c % 2) * 8 + f % 8


def route(dyh, dz, dc):
    return [(place_index(yh, z, c, f), place_index(yh + dyh, z + dz, c + dc, f)) for yh, z, c, f in places()]


def send(block, dyh=0, dz=0, dc=0):
    return lax.ppermute(block, BOTH, route(dyh, dz, dc))


def together(*arrays):
    return lax.optimization_barrier(arrays)


def scaled(block, weight):
    return (block.astype(jnp.float32) * weight).astype(jnp.bfloat16)


def gram(a, b):
    return lax.dot_general(a, b, (((1,), (1,)), ((), ())), preferred_element_type=jnp.float32)


CORE, YH, Z, HIGH, NEXT_HIGH, PREV_HIGH, ON_B2, ON_B3, ON_B5, ON_B6 = range(10)


def span(which, half):
    return pl.ds(pl.multiple_of(which * half, LANES), half)


def spread_pairs():
    place = lax.broadcasted_iota(jnp.int32, (LANES, 2 * LANES), 0)
    return (lax.broadcasted_iota(jnp.int32, (LANES, 2 * LANES), 1) // 2 == place).astype(jnp.bfloat16)


def mask_kernel(info, hot, spectra, wedges, own, to_partner, to_next, to_previous, pairs):
    half = spectra.shape[1] // 2

    @pl.when(pl.program_id(0) == 0)
    def _():
        spread = spread_pairs()
        for j in range(half // LANES):
            some = wedges[:, pl.ds(j * LANES, LANES)].astype(jnp.float32).astype(jnp.bfloat16)
            wide = jnp.dot(some, spread, preferred_element_type=jnp.float32)
            pairs[:, pl.ds(j * 2 * LANES, 2 * LANES)] = wide.astype(jnp.bfloat16)

    keep = jnp.dot(hot[...], pairs[...], preferred_element_type=jnp.float32).astype(jnp.bfloat16)
    own[...] = spectra[...] * keep
    to_partner[...] = own[:, span(1 - info[YH], half)]
    to_next[...] = own[:, span(info[NEXT_HIGH], half)]
    to_previous[...] = own[:, span(info[PREV_HIGH], half)]


def masked_blocks(info, hot, spectra, wedges):
    rows, width = spectra.shape
    classes = wedges.shape[0]
    part = rows // 4
    whole = lambda *shape: pl.BlockSpec(shape, lambda i, info: (0, 0))
    slab = lambda n: pl.BlockSpec((part, n), lambda i, info: (i, 0))
    half_block = jax.ShapeDtypeStruct((rows, width // 2), jnp.bfloat16)
    return pl.pallas_call(
        mask_kernel,
        grid_spec=pltpu.PrefetchScalarGridSpec(
            num_scalar_prefetch=1,
            grid=(4,),
            in_specs=[slab(classes), slab(width), whole(classes, width // 2)],
            out_specs=[slab(width), slab(width // 2), slab(width // 2), slab(width // 2), whole(classes, width)],
        ),
        out_shape=[
            jax.ShapeDtypeStruct((rows, width), jnp.bfloat16),
            half_block,
            half_block,
            half_block,
            jax.ShapeDtypeStruct((classes, width), jnp.bfloat16),
        ],
        compiler_params=PARAMS,
    )(info, hot, spectra, wedges)


def weight_kernel(shell_weight, shells, weight):
    spread = spread_pairs()

    def widen(x):
        return jnp.dot(x, spread, preferred_element_type=jnp.float32)

    for j in range(shells.shape[1] // LANES):
        shell = shells[:, pl.ds(j * LANES, LANES)]
        value = jnp.zeros(shell.shape, jnp.float32)
        for k in range(shell_weight.shape[0]):
            value = jnp.where(shell == k, shell_weight[k], value)
        top = value.astype(jnp.bfloat16)
        rest = value - top.astype(jnp.float32)
        middle = rest.astype(jnp.bfloat16)
        low = (rest - middle.astype(jnp.float32)).astype(jnp.bfloat16)
        weight[:, pl.ds(j * 2 * LANES, 2 * LANES)] = (widen(top) + widen(middle)) + widen(low)


def pair_weights(shell_weight, shells):
    return pl.pallas_call(
        weight_kernel,
        in_specs=[SMEM, VMEM],
        out_specs=VMEM,
        out_shape=jax.ShapeDtypeStruct((1, 2 * shells.shape[1]), jnp.float32),
        compiler_params=PARAMS,
    )(shell_weight, shells)


def first_kernel(info, own, sibling, weight, out, own_w):
    slices = out.shape[1]
    own_w[...] = scaled(own[...], weight[...])

    def put(core, tile):
        out[pl.ds(core * 4, 4)] = tile.reshape(4, slices, tile.shape[1])

    put(info[CORE], gram(own_w[...], own[...]))

    @pl.when(info[CORE] == 0)
    def _():
        put(1, gram(sibling[...], own_w[...]))

    @pl.when(info[CORE] == 1)
    def _():
        put(0, gram(scaled(sibling[...], weight[...]), own[...]))


def first_tiles(info, own, sibling, weight):
    rows, width = own.shape
    return pl.pallas_call(
        first_kernel,
        in_specs=[SMEM, VMEM, VMEM, VMEM],
        out_specs=[VMEM, VMEM],
        out_shape=[
            jax.ShapeDtypeStruct((8, rows // 4, rows), jnp.float32),
            jax.ShapeDtypeStruct((rows, width), jnp.bfloat16),
        ],
        compiler_params=PARAMS,
    )(info, own, sibling, weight)


def middle_kernel(
    info, own, own_w, sibling, partner, partner_s, third_a, third_a_s, third_b, weight, out, scaled_b
):
    half = partner.shape[1]
    slices = out.shape[2]
    lower, on_b3, core = info[YH] == 0, info[ON_B3] == 1, info[CORE]
    at_yh = span(info[YH], half)
    w_yh, w_high = weight[:, at_yh], weight[:, span(info[HIGH], half)]

    def put(k, owner, tile):
        out[pl.ds(owner * 4, 4), k] = tile.reshape(4, slices, tile.shape[1])

    @pl.when(on_b3)
    def _():
        scaled_b[...] = scaled(third_b[...], w_high)
        put(0, core, gram(third_a[...], scaled_b[...]))
        put(0, 1 - core, gram(third_a_s[...], scaled_b[...]))

    @pl.when(jnp.logical_not(on_b3))
    def _():
        put(0, core, gram(scaled(third_a[...], w_high), third_b[...]))
        put(0, 1 - core, gram(scaled(third_a_s[...], w_high), third_b[...]))

    @pl.when(lower)
    def _():
        put(1, core, gram(partner[...], own_w[:, at_yh]))

        @pl.when(core == 1)
        def _():
            put(1, 0, gram(partner_s[...], own_w[:, at_yh]))

        @pl.when(core == 0)
        def _():
            put(1, 1, gram(scaled(partner_s[...], w_yh), own[:, at_yh]))

    @pl.when(jnp.logical_not(lower))
    def _():
        scaled_b[...] = scaled(partner[...], w_yh)
        put(1, core, gram(own[:, at_yh], scaled_b[...]))

        @pl.when(core == 1)
        def _():
            put(1, 0, gram(sibling[:, at_yh], scaled_b[...]))

        @pl.when(core == 0)
        def _():
            put(1, 1, gram(scaled(sibling[:, at_yh], w_yh), partner[...]))


def middle_tiles(info, own, *others):
    rows, width = own.shape
    return pl.pallas_call(
        middle_kernel,
        in_specs=[SMEM] + [VMEM] * (len(others) + 1),
        out_specs=VMEM,
        out_shape=jax.ShapeDtypeStruct((8, 2, rows // 4, rows), jnp.float32),
        scratch_shapes=[pltpu.VMEM((rows, width // 2), jnp.bfloat16)],
        compiler_params=PARAMS,
    )(info, own, *others)


def late_kernel(
    is_mine, info, own, own_w, partner_a, partner_b, a_high, a_low, mine_high, mine_low, diagonal, a_diagonal,
    weight, *rest,
):
    out, a, a_w, own_b, partner, sixth_a, sixth_b, tiles, sems, out_sems = rest[-10:]
    half = partner_a.shape[1]
    slices = out.shape[2]
    lower = info[YH] == 0
    high_is_yh = info[HIGH] == info[YH]
    high, yh = info[HIGH], info[YH]

    def pick(n, dst, *choices):
        for chosen, src in choices:

            @pl.when(chosen)
            def _(src=src):
                pltpu.make_async_copy(src, dst, sems.at[n]).start()

        return pltpu.make_async_copy(choices[0][1], dst, sems.at[n])

    always = info[CORE] >= 0
    no = jnp.logical_not
    got_high = pick(0, a.at[:, span(high, half)], (always, a_high))
    got_low = pick(1, a.at[:, span(1 - high, half)], (always, a_low))
    got_own = pick(2, own_b, (info[ON_B2] == 1, own_w), (info[ON_B2] == 0, own))
    got_near = pick(3, partner.at[:, span(yh, half)], (always, partner_a))
    got_far = pick(4, partner.at[:, span(1 - yh, half)], (always, partner_b))
    got_a = pick(
        5,
        sixth_a,
        (no(lower), a_diagonal),
        (jnp.logical_and(lower, high_is_yh), a_high),
        (jnp.logical_and(lower, no(high_is_yh)), a_low),
    )
    got_b = pick(
        6,
        sixth_b,
        (lower, diagonal),
        (jnp.logical_and(no(lower), high_is_yh), mine_high),
        (jnp.logical_and(no(lower), no(high_is_yh)), mine_low),
    )
    owner = info[CORE] if is_mine else 1 - info[CORE]
    sent = []

    def put(k, tile):
        tiles[k] = tile.reshape(4, slices, tile.shape[1])

    def leave(k):
        copy = pltpu.make_async_copy(tiles.at[k], out.at[pl.ds(owner * 4, 4), k], out_sems.at[k])
        copy.start()
        sent.append(copy)

    got_high.wait()
    got_low.wait()
    a_w[...] = scaled(a[...], weight[...])
    got_own.wait()

    @pl.when(info[ON_B2] == 1)
    def _():
        put(0, gram(a[...], own_b[...]))

    @pl.when(info[ON_B2] == 0)
    def _():
        put(0, gram(a_w[...], own_b[...]))

    leave(0)
    got_near.wait()
    got_far.wait()

    @pl.when(info[ON_B5] == 1)
    def _():
        partner[...] = scaled(partner[...], weight[...])
        put(1, gram(a[...], partner[...]))

    @pl.when(info[ON_B5] == 0)
    def _():
        put(1, gram(a_w[...], partner[...]))

    leave(1)
    got_a.wait()
    got_b.wait()
    w_yh = weight[:, span(yh, half)]

    @pl.when(info[ON_B6] == 1)
    def _():
        sixth_b[...] = scaled(sixth_b[...], w_yh)

    @pl.when(info[ON_B6] == 0)
    def _():
        sixth_a[...] = scaled(sixth_a[...], w_yh)

    put(2, gram(sixth_a[...], sixth_b[...]))
    leave(2)
    for copy in sent:
        copy.wait()


def late_tiles(is_mine, info, own, own_w, partner_a, partner_b, a_high, a_low, mine_high, mine_low, diagonal,
               a_diagonal, weight, other=None):
    rows, width = own.shape
    half = width // 2
    arrays = [own, own_w, partner_a, partner_b, a_high, a_low, mine_high, mine_low, diagonal, a_diagonal, weight]
    specs = [SMEM] + [ANY] * 10 + [VMEM]
    aliases = {}
    if other is not None:
        arrays.append(other)
        specs.append(ANY)
        aliases = {len(specs) - 1: 0}
    block = lambda n: pltpu.VMEM((rows, n), jnp.bfloat16)

    def kernel(*refs):
        late_kernel(is_mine, *refs)

    return pl.pallas_call(
        kernel,
        in_specs=specs,
        out_specs=ANY,
        out_shape=jax.ShapeDtypeStruct((8, 3, rows // 4, rows), jnp.float32),
        scratch_shapes=[
            block(width),
            block(width),
            block(width),
            block(width),
            block(half),
            block(half),
            pltpu.VMEM((3, 4, rows // 4, rows), jnp.float32),
            pltpu.SemaphoreType.DMA((7,)),
            pltpu.SemaphoreType.DMA((3,)),
        ],
        input_output_aliases=aliases,
        compiler_params=PARAMS,
    )(info, *arrays)


def gather_kernel(info, r1, late, r4, from_previous, third_back, third_ahead, from_partner, fourth, from_diagonal, out):
    yh, z = info[YH], info[Z]

    def put(dyh, dz, value):
        out[(yh + dyh) % 2 * 4 + (z + dz) % 4] = value

    put(0, 0, r1[...])
    put(0, 1, late[0])
    put(0, 2, third_back[...] + third_ahead[...])
    put(0, 3, from_previous[0])
    put(1, 0, r4[...] + fourth[...])
    put(1, 1, from_partner[...])
    put(1, 2, from_previous[2] + from_diagonal[...])
    put(1, 3, from_previous[1])


def gathered(info, *parts):
    slices, rows = parts[0].shape
    return pl.pallas_call(
        gather_kernel,
        in_specs=[SMEM] + [VMEM] * len(parts),
        out_specs=VMEM,
        out_shape=jax.ShapeDtypeStruct((8, slices, rows), jnp.float32),
    )(info, *parts)


def final_kernel(info, found, swapped, root, out):
    rows = swapped.shape[0]
    core, by_row = info[0], info[1]

    for is_first in (True, False):

        @pl.when(jnp.logical_and(by_row == 1, (core == 0) == is_first))
        def _(is_first=is_first):
            kept = found[:rows] if is_first else found[rows:]
            pair = (kept, swapped[...]) if is_first else (swapped[...], kept)
            out[...] = jnp.concatenate(pair, 1) / root[...]

    @pl.when(by_row == 0)
    def _():
        out[...] = found[...].T / root[...]


def finished(info, found, swapped, root):
    return pl.pallas_call(
        final_kernel,
        in_specs=[SMEM, VMEM, VMEM, VMEM],
        out_specs=VMEM,
        out_shape=jax.ShapeDtypeStruct(root.shape, jnp.float32),
    )(info, found, swapped, root)


def per_device(spectra, labels, wedges, shells, shell_weight):
    rows, width = spectra.shape
    half = width // 2
    classes = wedges.shape[0]
    blk = lax.axis_index("blk")
    core, z, yh = blk % 2, (blk // 2) % 4, blk // 8
    freq = lax.axis_index("freq")

    def place(dyh, dz):
        return ((yh + dyh) % 2) * 4 + (z + dz) % 4

    def ahead(a, b):
        return ((a - b) % 8 < 4).astype(jnp.int32)

    def columns(block, which):
        return lax.dynamic_slice_in_dim(block, which * half, half, 1)

    def summed(tiles):
        return jnp.sum(lax.all_to_all(tiles, "freq", 0, 0, tiled=True), 0)

    low, lower = z < 2, yh == 0
    high = z // 2
    previous_high = ((z + 3) % 4) // 2
    info = jnp.stack(
        [
            core,
            yh,
            z,
            high,
            ((z + 1) % 4) // 2,
            previous_high,
            ahead(place(0, 1), place(0, 0)),
            jnp.where(low, ahead(place(0, 1), place(0, -1)), ahead(place(0, -1), place(0, 1))),
            ahead(place(0, 1), place(1, 0)),
            jnp.where(lower, ahead(place(0, 1), place(1, -1)), ahead(place(1, -1), place(0, 1))),
        ]
    ).astype(jnp.int32)

    class_range = jnp.arange(classes, dtype=jnp.int32)
    own_labels = lax.dynamic_slice_in_dim(labels, blk * rows, rows)
    hot = (own_labels[:, None] == class_range[None, :]).astype(jnp.bfloat16)
    own, to_partner, to_next, to_previous, pairs = masked_blocks(info, hot, spectra, wedges)

    following_a = send(to_previous, dz=-1)
    partner_a = send(to_partner, dyh=1)
    previous = send(to_next, dz=1)
    sibling = send(own, dc=1)

    own, shells = together(own, shells)
    weight = pair_weights(shell_weight, shells[None, :])
    squares = own.astype(jnp.float32) ** 2 * weight
    partial_energy = lax.dot_general(
        pairs.astype(jnp.float32), squares, (((1,), (1,)), ((), ())), precision=lax.Precision.HIGHEST
    )
    q1, own_w = first_tiles(info, own, sibling, weight)
    q1 = jnp.concatenate([q1, jnp.broadcast_to(partial_energy[None], (8, classes, rows))], 1)
    to_partner_b = columns(own, yh)
    to_previous_b = columns(own, 1 - previous_high)
    following_a, partner_a, previous, to_partner_b, to_previous_b, q1 = together(
        following_a, partner_a, previous, to_partner_b, to_previous_b, q1
    )

    following_b = send(to_previous_b, dz=-1)
    partner_b = send(to_partner_b, dyh=1)
    diagonal = send(partner_a, dz=1)
    partner_s = send(partner_a, dc=1)
    third_a = jnp.where(low, following_a, previous)
    third_b = jnp.where(low, previous, following_a)
    third_a_s = send(third_a, dc=1)
    r1 = summed(q1)
    energy, r1 = r1[rows // 4 :], r1[: rows // 4]
    middle = middle_tiles(info, own, own_w, sibling, partner_a, partner_s, third_a, third_a_s, third_b, weight)
    following_b, partner_b, diagonal, middle, energy, r1 = together(
        following_b, partner_b, diagonal, middle, energy, r1
    )

    following_as = send(following_a, dc=1)
    following_bs = send(following_b, dc=1)
    diagonal_s = send(diagonal, dc=1)
    middle = summed(middle)
    energy_all = lax.all_to_all(jnp.broadcast_to(energy[None], (16, classes, rows)), "blk", 0, 0, tiled=True)
    late = late_tiles(
        True, info, own, own_w, partner_a, partner_b, following_a, following_b, following_a, following_b,
        diagonal, diagonal, weight,
    )
    late, middle, following_as, following_bs, diagonal_s = together(
        late, middle, following_as, following_bs, diagonal_s
    )
    late = late_tiles(
        False, info, own, own_w, partner_a, partner_b, following_as, following_bs, following_a, following_b,
        diagonal, diagonal_s, weight, late,
    )
    late, energy_all = together(late, energy_all)
    r3, r4 = middle[0], middle[1]

    third_back = send(r3, dz=1)
    third_ahead = send(r3, dz=-1)
    fourth = send(r4, dyh=1)
    column_labels = lax.dynamic_slice_in_dim(labels, freq * 2 * rows, 2 * rows)
    column_energy = lax.dynamic_slice_in_dim(energy_all, freq * 2, 2, 0)
    column_energy = jnp.concatenate([column_energy[0], column_energy[1]], 1)
    row_side = jnp.zeros((rows, 2 * rows), jnp.float32)
    column_side = jnp.zeros((rows, 2 * rows), jnp.float32)
    for d in range(classes):
        row_side = jnp.where(column_labels[None, :] == d, energy[d][:, None], row_side)
        column_side = jnp.where(own_labels[:, None] == d, column_energy[d][None, :], column_side)
    root = jnp.sqrt(row_side * column_side + 1e-06)
    late = lax.all_to_all(late, "freq", 0, 0, tiled=True)
    late, third_back, third_ahead, fourth, root = together(late, third_back, third_ahead, fourth, root)
    late = jnp.sum(late, 0)

    from_previous = send(late, dz=1)
    from_partner = send(late[1], dyh=1)
    from_diagonal = send(late[2], dyh=1, dz=-1)
    from_previous, from_partner, from_diagonal = together(from_previous, from_partner, from_diagonal)
    pieces = gathered(
        info, r1, late, r4, from_previous, third_back, third_ahead, from_partner, fourth, from_diagonal
    )
    found = lax.all_to_all(pieces, "freq", 0, 0, tiled=True).reshape(2 * rows, rows)
    swapped = send(lax.dynamic_slice_in_dim(found, (1 - core) * rows, rows, 0), dc=1)

    step_y, step_z = (freq // 4 + yh) % 2, (freq % 4 - z) % 4
    same_y = step_y == 0
    inner_z = jnp.logical_or(z == 1, z == 2)
    by_row = jnp.where(
        step_z == 0,
        jnp.logical_or(same_y, yh == 1),
        jnp.where(step_z == 1, False, jnp.where(step_z == 2, jnp.where(same_y, inner_z, lower), True)),
    )
    return finished(jnp.stack([core, by_row.astype(jnp.int32)]), found, swapped, root)


def solution(mesh):
    placed = (P("blk", "freq"), P(), P(None, "freq"), P("freq"), P())
    return jax.shard_map(
        per_device, mesh=mesh, in_specs=placed, out_specs=P("blk", "freq"), check_vma=False
    )
```

```python
import jax
import jax.numpy as jnp
from jax import lax
from jax.experimental import pallas as pl
from jax.experimental.pallas import tpu as pltpu
from jax.sharding import PartitionSpec as P

BOTH = ("blk", "freq")
VMEM_BYTES = 60 * 1024 * 1024
LANES = 128
PARAMS = pltpu.CompilerParams(vmem_limit_bytes=VMEM_BYTES)
VMEM = pl.BlockSpec(memory_space=pltpu.VMEM)
SMEM = pl.BlockSpec(memory_space=pltpu.SMEM)
ANY = pl.BlockSpec(memory_space=pl.ANY)


def places():
    return [
        (yh, z, c, f) for yh in range(2) for z in range(4) for c in range(2) for f in range(8)
    ]


def place_index(yh, z, c, f):
    return (((yh % 2) * 4 + z % 4) * 2 + c % 2) * 8 + f % 8


def route(dyh, dz, dc, dyl):
    return [
        (place_index(yh, z, c, f), place_index(yh + dyh, z + dz, c + dc, f + 4 * dyl))
        for yh, z, c, f in places()
    ]


def send(block, dyh=0, dz=0, dc=0, dyl=0):
    return lax.ppermute(block, BOTH, route(dyh, dz, dc, dyl))


def summed_along_x(tiles):
    groups = [list(range(4)), list(range(4, 8))]
    return jnp.sum(lax.all_to_all(tiles, "freq", 0, 0, axis_index_groups=groups, tiled=True), 0)


def together(*arrays):
    return lax.optimization_barrier(arrays)


def scaled(block, weight):
    return (block.astype(jnp.float32) * weight).astype(jnp.bfloat16)


def gram(a, b):
    return lax.dot_general(a, b, (((1,), (1,)), ((), ())), preferred_element_type=jnp.float32)


CORE, YH, Z, HIGH, NEXT_HIGH, PREV_HIGH, ON_B2, ON_B3, ON_B5, ON_B6 = range(10)


def span(which, half):
    return pl.ds(pl.multiple_of(which * half, LANES), half)


def spread_pairs():
    place = lax.broadcasted_iota(jnp.int32, (LANES, 2 * LANES), 0)
    return (lax.broadcasted_iota(jnp.int32, (LANES, 2 * LANES), 1) // 2 == place).astype(jnp.bfloat16)


def mask_kernel(info, hot, spectra, wedges, own, to_partner, to_next, to_previous, pairs):
    half = spectra.shape[1] // 2

    @pl.when(pl.program_id(0) == 0)
    def _():
        spread = spread_pairs()
        for j in range(half // LANES):
            some = wedges[:, pl.ds(j * LANES, LANES)].astype(jnp.float32).astype(jnp.bfloat16)
            wide = jnp.dot(some, spread, preferred_element_type=jnp.float32)
            pairs[:, pl.ds(j * 2 * LANES, 2 * LANES)] = wide.astype(jnp.bfloat16)

    keep = jnp.dot(hot[...], pairs[...], preferred_element_type=jnp.float32).astype(jnp.bfloat16)
    own[...] = spectra[...] * keep
    to_partner[...] = own[:, span(1 - info[YH], half)]
    to_next[...] = own[:, span(info[NEXT_HIGH], half)]
    to_previous[...] = own[:, span(info[PREV_HIGH], half)]


def masked_blocks(info, hot, spectra, wedges):
    rows, width = spectra.shape
    classes = wedges.shape[0]
    part = rows // 4
    whole = lambda *shape: pl.BlockSpec(shape, lambda i, info: (0, 0))
    slab = lambda n: pl.BlockSpec((part, n), lambda i, info: (i, 0))
    half_block = jax.ShapeDtypeStruct((rows, width // 2), jnp.bfloat16)
    return pl.pallas_call(
        mask_kernel,
        grid_spec=pltpu.PrefetchScalarGridSpec(
            num_scalar_prefetch=1,
            grid=(4,),
            in_specs=[slab(classes), slab(width), whole(classes, width // 2)],
            out_specs=[slab(width), slab(width // 2), slab(width // 2), slab(width // 2), whole(classes, width)],
        ),
        out_shape=[
            jax.ShapeDtypeStruct((rows, width), jnp.bfloat16),
            half_block,
            half_block,
            half_block,
            jax.ShapeDtypeStruct((classes, width), jnp.bfloat16),
        ],
        compiler_params=PARAMS,
    )(info, hot, spectra, wedges)


def weight_kernel(shell_weight, shells, weight):
    spread = spread_pairs()

    def widen(x):
        return jnp.dot(x, spread, preferred_element_type=jnp.float32)

    for j in range(shells.shape[1] // LANES):
        shell = shells[:, pl.ds(j * LANES, LANES)]
        value = jnp.zeros(shell.shape, jnp.float32)
        for k in range(shell_weight.shape[0]):
            value = jnp.where(shell == k, shell_weight[k], value)
        top = value.astype(jnp.bfloat16)
        rest = value - top.astype(jnp.float32)
        middle = rest.astype(jnp.bfloat16)
        low = (rest - middle.astype(jnp.float32)).astype(jnp.bfloat16)
        weight[:, pl.ds(j * 2 * LANES, 2 * LANES)] = (widen(top) + widen(middle)) + widen(low)


def pair_weights(shell_weight, shells):
    return pl.pallas_call(
        weight_kernel,
        in_specs=[SMEM, VMEM],
        out_specs=VMEM,
        out_shape=jax.ShapeDtypeStruct((1, 2 * shells.shape[1]), jnp.float32),
        compiler_params=PARAMS,
    )(shell_weight, shells)


def first_kernel(info, own, sibling, weight, out, own_w):
    slices = out.shape[2]
    own_w[...] = scaled(own[...], weight[...])

    def put(core, tile):
        out[:, core] = tile.reshape(4, slices, tile.shape[1])

    put(info[CORE], gram(own_w[...], own[...]))

    @pl.when(info[CORE] == 0)
    def _():
        put(1, gram(sibling[...], own_w[...]))

    @pl.when(info[CORE] == 1)
    def _():
        put(0, gram(scaled(sibling[...], weight[...]), own[...]))


def first_tiles(info, own, sibling, weight):
    rows, width = own.shape
    return pl.pallas_call(
        first_kernel,
        in_specs=[SMEM, VMEM, VMEM, VMEM],
        out_specs=[VMEM, VMEM],
        out_shape=[
            jax.ShapeDtypeStruct((4, 2, rows // 4, rows), jnp.float32),
            jax.ShapeDtypeStruct((rows, width), jnp.bfloat16),
        ],
        compiler_params=PARAMS,
    )(info, own, sibling, weight)


def middle_kernel(
    info, own, own_w, sibling, partner, partner_s, third_a, third_a_s, third_b, energy, weight, out, scaled_b
):
    half = partner.shape[1]
    slices = own.shape[0] // 4
    for x in range(4):
        out[x, 4 * slices :] = energy[...]
    lower, on_b3, core = info[YH] == 0, info[ON_B3] == 1, info[CORE]
    at_yh = span(info[YH], half)
    w_yh, w_high = weight[:, at_yh], weight[:, span(info[HIGH], half)]

    def put(k, owner, tile):
        at = pl.ds(pl.multiple_of((2 * owner + k) * slices, 8), slices)
        out[:, at] = tile.reshape(4, slices, tile.shape[1])

    @pl.when(on_b3)
    def _():
        scaled_b[...] = scaled(third_b[...], w_high)
        put(0, core, gram(third_a[...], scaled_b[...]))
        put(0, 1 - core, gram(third_a_s[...], scaled_b[...]))

    @pl.when(jnp.logical_not(on_b3))
    def _():
        put(0, core, gram(scaled(third_a[...], w_high), third_b[...]))
        put(0, 1 - core, gram(scaled(third_a_s[...], w_high), third_b[...]))

    @pl.when(lower)
    def _():
        put(1, core, gram(partner[...], own_w[:, at_yh]))

        @pl.when(core == 1)
        def _():
            put(1, 0, gram(partner_s[...], own_w[:, at_yh]))

        @pl.when(core == 0)
        def _():
            put(1, 1, gram(scaled(partner_s[...], w_yh), own[:, at_yh]))

    @pl.when(jnp.logical_not(lower))
    def _():
        scaled_b[...] = scaled(partner[...], w_yh)
        put(1, core, gram(own[:, at_yh], scaled_b[...]))

        @pl.when(core == 1)
        def _():
            put(1, 0, gram(sibling[:, at_yh], scaled_b[...]))

        @pl.when(core == 0)
        def _():
            put(1, 1, gram(scaled(sibling[:, at_yh], w_yh), partner[...]))


def middle_tiles(info, own, *others):
    rows, width = own.shape
    classes = others[-2].shape[0]
    return pl.pallas_call(
        middle_kernel,
        in_specs=[SMEM] + [VMEM] * (len(others) + 1),
        out_specs=VMEM,
        out_shape=jax.ShapeDtypeStruct((4, rows + classes, rows), jnp.float32),
        scratch_shapes=[pltpu.VMEM((rows, width // 2), jnp.bfloat16)],
        compiler_params=PARAMS,
    )(info, own, *others)


def late_kernel(
    is_mine, info, own, own_w, partner_a, partner_b, a_high, a_low, mine_high, mine_low, diagonal, a_diagonal,
    weight, *rest,
):
    out, a, a_w, own_b, partner, sixth_a, sixth_b, tiles, sems, out_sems = rest[-10:]
    half = partner_a.shape[1]
    slices = out.shape[2]
    lower = info[YH] == 0
    high_is_yh = info[HIGH] == info[YH]
    high, yh = info[HIGH], info[YH]

    def pick(n, dst, *choices):
        for chosen, src in choices:

            @pl.when(chosen)
            def _(src=src):
                pltpu.make_async_copy(src, dst, sems.at[n]).start()

        return pltpu.make_async_copy(choices[0][1], dst, sems.at[n])

    always = info[CORE] >= 0
    no = jnp.logical_not
    got_high = pick(0, a.at[:, span(high, half)], (always, a_high))
    got_low = pick(1, a.at[:, span(1 - high, half)], (always, a_low))
    got_own = pick(2, own_b, (info[ON_B2] == 1, own_w), (info[ON_B2] == 0, own))
    got_near = pick(3, partner.at[:, span(yh, half)], (always, partner_a))
    got_far = pick(4, partner.at[:, span(1 - yh, half)], (always, partner_b))
    got_a = pick(
        5,
        sixth_a,
        (no(lower), a_diagonal),
        (jnp.logical_and(lower, high_is_yh), a_high),
        (jnp.logical_and(lower, no(high_is_yh)), a_low),
    )
    got_b = pick(
        6,
        sixth_b,
        (lower, diagonal),
        (jnp.logical_and(no(lower), high_is_yh), mine_high),
        (jnp.logical_and(no(lower), no(high_is_yh)), mine_low),
    )
    owner = info[CORE] if is_mine else 1 - info[CORE]
    sent = []

    def put(k, tile):
        tiles[k] = tile.reshape(4, slices, tile.shape[1])

    def leave(k):
        copy = pltpu.make_async_copy(tiles.at[k], out.at[pl.ds(owner * 4, 4), k], out_sems.at[k])
        copy.start()
        sent.append(copy)

    got_high.wait()
    got_low.wait()
    a_w[...] = scaled(a[...], weight[...])
    got_own.wait()

    @pl.when(info[ON_B2] == 1)
    def _():
        put(0, gram(a[...], own_b[...]))

    @pl.when(info[ON_B2] == 0)
    def _():
        put(0, gram(a_w[...], own_b[...]))

    leave(0)
    got_near.wait()
    got_far.wait()

    @pl.when(info[ON_B5] == 1)
    def _():
        partner[...] = scaled(partner[...], weight[...])
        put(1, gram(a[...], partner[...]))

    @pl.when(info[ON_B5] == 0)
    def _():
        put(1, gram(a_w[...], partner[...]))

    leave(1)
    got_a.wait()
    got_b.wait()
    w_yh = weight[:, span(yh, half)]

    @pl.when(info[ON_B6] == 1)
    def _():
        sixth_b[...] = scaled(sixth_b[...], w_yh)

    @pl.when(info[ON_B6] == 0)
    def _():
        sixth_a[...] = scaled(sixth_a[...], w_yh)

    put(2, gram(sixth_a[...], sixth_b[...]))
    leave(2)
    for copy in sent:
        copy.wait()


def late_tiles(is_mine, info, own, own_w, partner_a, partner_b, a_high, a_low, mine_high, mine_low, diagonal,
               a_diagonal, weight, other=None):
    rows, width = own.shape
    half = width // 2
    arrays = [own, own_w, partner_a, partner_b, a_high, a_low, mine_high, mine_low, diagonal, a_diagonal, weight]
    specs = [SMEM] + [ANY] * 10 + [VMEM]
    aliases = {}
    if other is not None:
        arrays.append(other)
        specs.append(ANY)
        aliases = {len(specs) - 1: 0}
    block = lambda n: pltpu.VMEM((rows, n), jnp.bfloat16)

    def kernel(*refs):
        late_kernel(is_mine, *refs)

    return pl.pallas_call(
        kernel,
        in_specs=specs,
        out_specs=ANY,
        out_shape=jax.ShapeDtypeStruct((8, 3, rows // 4, rows), jnp.float32),
        scratch_shapes=[
            block(width),
            block(width),
            block(width),
            block(width),
            block(half),
            block(half),
            pltpu.VMEM((3, 4, rows // 4, rows), jnp.float32),
            pltpu.SemaphoreType.DMA((7,)),
            pltpu.SemaphoreType.DMA((3,)),
        ],
        input_output_aliases=aliases,
        compiler_params=PARAMS,
    )(info, *arrays)


def gather_kernel(info, early, late, from_previous, third_back, third_ahead, from_partner, fourth, from_diagonal, out):
    yh, z = info[YH], info[Z]

    def put(dyh, dz, value):
        out[(yh + dyh) % 2 * 4 + (z + dz) % 4] = value

    slices = out.shape[1]
    put(0, 0, early[:slices])
    put(0, 1, late[0])
    put(0, 2, third_back[...] + third_ahead[...])
    put(0, 3, from_previous[0])
    put(1, 0, early[2 * slices : 3 * slices] + fourth[...])
    put(1, 1, from_partner[...])
    put(1, 2, from_previous[2] + from_diagonal[...])
    put(1, 3, from_previous[1])


def gathered(info, *parts):
    slices, rows = parts[1].shape[1:]
    return pl.pallas_call(
        gather_kernel,
        in_specs=[SMEM] + [VMEM] * len(parts),
        out_specs=VMEM,
        out_shape=jax.ShapeDtypeStruct((8, slices, rows), jnp.float32),
    )(info, *parts)


def final_kernel(info, found, swapped, root, out):
    rows = swapped.shape[0]
    core, by_row = info[0], info[1]

    for is_first in (True, False):

        @pl.when(jnp.logical_and(by_row == 1, (core == 0) == is_first))
        def _(is_first=is_first):
            kept = found[:rows] if is_first else found[rows:]
            pair = (kept, swapped[...]) if is_first else (swapped[...], kept)
            out[...] = jnp.concatenate(pair, 1) / root[...]

    @pl.when(by_row == 0)
    def _():
        out[...] = found[...].T / root[...]


def finished(info, found, swapped, root):
    return pl.pallas_call(
        final_kernel,
        in_specs=[SMEM, VMEM, VMEM, VMEM],
        out_specs=VMEM,
        out_shape=jax.ShapeDtypeStruct(root.shape, jnp.float32),
    )(info, found, swapped, root)


def per_device(spectra, labels, wedges, shells, shell_weight):
    rows, width = spectra.shape
    half, slices = width // 2, rows // 4
    classes = wedges.shape[0]
    blk = lax.axis_index("blk")
    core, z, yh = blk % 2, (blk // 2) % 4, blk // 8
    freq = lax.axis_index("freq")

    def place(dyh, dz):
        return ((yh + dyh) % 2) * 4 + (z + dz) % 4

    def ahead(a, b):
        return ((a - b) % 8 < 4).astype(jnp.int32)

    def columns(block, which):
        return lax.dynamic_slice_in_dim(block, which * half, half, 1)

    low, lower = z < 2, yh == 0
    high = z // 2
    previous_high = ((z + 3) % 4) // 2
    info = jnp.stack(
        [
            core,
            yh,
            z,
            high,
            ((z + 1) % 4) // 2,
            previous_high,
            ahead(place(0, 1), place(0, 0)),
            jnp.where(low, ahead(place(0, 1), place(0, -1)), ahead(place(0, -1), place(0, 1))),
            ahead(place(0, 1), place(1, 0)),
            jnp.where(lower, ahead(place(0, 1), place(1, -1)), ahead(place(1, -1), place(0, 1))),
        ]
    ).astype(jnp.int32)

    class_range = jnp.arange(classes, dtype=jnp.int32)
    own_labels = lax.dynamic_slice_in_dim(labels, blk * rows, rows)
    hot = (own_labels[:, None] == class_range[None, :]).astype(jnp.bfloat16)
    own, to_partner, to_next, to_previous, pairs = masked_blocks(info, hot, spectra, wedges)

    following_a = send(to_previous, dz=-1)
    partner_a = send(to_partner, dyh=1)
    previous = send(to_next, dz=1)
    sibling = send(own, dc=1)

    own, shells = together(own, shells)
    weight = pair_weights(shell_weight, shells[None, :])
    q1, own_w = first_tiles(info, own, sibling, weight)
    to_partner_b = columns(own, yh)
    to_previous_b = columns(own, 1 - previous_high)
    p1 = summed_along_x(q1)
    following_a, partner_a, previous, to_partner_b, to_previous_b, p1 = together(
        following_a, partner_a, previous, to_partner_b, to_previous_b, p1
    )

    following_b = send(to_previous_b, dz=-1)
    partner_b = send(to_partner_b, dyh=1)
    diagonal = send(partner_a, dz=1)
    partner_s = send(partner_a, dc=1)
    third_a = jnp.where(low, following_a, previous)
    third_b = jnp.where(low, previous, following_a)
    third_a_s = send(third_a, dc=1)
    squares = own.astype(jnp.float32) ** 2 * weight
    partial_energy = lax.dot_general(
        pairs.astype(jnp.float32), squares, (((1,), (1,)), ((), ())), precision=lax.Precision.HIGHEST
    )
    middle = middle_tiles(
        info, own, own_w, sibling, partner_a, partner_s, third_a, third_a_s, third_b, partial_energy, weight
    )
    middle = summed_along_x(middle)
    following_b, partner_b, diagonal, middle = together(following_b, partner_b, diagonal, middle)

    following_as = send(following_a, dc=1)
    following_bs = send(following_b, dc=1)
    diagonal_s = send(diagonal, dc=1)
    late = late_tiles(
        True, info, own, own_w, partner_a, partner_b, following_a, following_b, following_a, following_b,
        diagonal, diagonal, weight,
    )
    late, following_as, following_bs, diagonal_s = together(late, following_as, following_bs, diagonal_s)
    late = late_tiles(
        False, info, own, own_w, partner_a, partner_b, following_as, following_bs, following_a, following_b,
        diagonal, diagonal_s, weight, late,
    )
    late = lax.all_to_all(late, "freq", 0, 0, tiled=True)

    own_yl = freq // 4

    def halves(which):
        return [
            lax.dynamic_index_in_dim(p1, which, 0, keepdims=False),
            lax.dynamic_slice_in_dim(middle, which * 2 * slices, 2 * slices, 0),
            middle[4 * slices :],
        ]

    early = jnp.concatenate(halves(own_yl)) + send(jnp.concatenate(halves(1 - own_yl)), dyl=1)
    third, energy = early[slices : 2 * slices], early[3 * slices :]
    third_energy = jnp.concatenate([third, energy])
    back, forth, opposite = send(third_energy, dz=1), send(third_energy, dz=-1), send(energy, dz=2)
    third_back, third_ahead = back[:slices], forth[:slices]
    plane = jnp.concatenate([energy, forth[slices:], opposite, back[slices:]])
    from_other = send(jnp.concatenate([early[2 * slices : 3 * slices], plane]), dyh=1)
    fourth = from_other[:slices]
    energies = jnp.concatenate([plane, from_other[slices:]])
    energies_s = send(energies, dc=1)
    step_y, step_z = (freq // 4 + yh) % 2, (freq % 4 - z) % 4
    column_energy = [
        lax.dynamic_slice_in_dim(e, (step_y * 4 + step_z) * classes, classes, 0) for e in (energies, energies_s)
    ]
    column_energy = jnp.where(
        core == 0, jnp.concatenate(column_energy, 1), jnp.concatenate(column_energy[::-1], 1)
    )
    column_labels = lax.dynamic_slice_in_dim(labels, freq * 2 * rows, 2 * rows)
    row_side = jnp.zeros((rows, 2 * rows), jnp.float32)
    column_side = jnp.zeros((rows, 2 * rows), jnp.float32)
    for d in range(classes):
        row_side = jnp.where(column_labels[None, :] == d, energy[d][:, None], row_side)
        column_side = jnp.where(own_labels[:, None] == d, column_energy[d][None, :], column_side)
    root = jnp.sqrt(row_side * column_side + 1e-06)
    late, third_back, third_ahead, fourth, root = together(late, third_back, third_ahead, fourth, root)
    late = jnp.sum(late, 0)

    from_previous = send(late, dz=1)
    from_partner = send(late[1], dyh=1)
    from_diagonal = send(late[2], dyh=1, dz=-1)
    from_previous, from_partner, from_diagonal = together(from_previous, from_partner, from_diagonal)
    pieces = gathered(
        info, early, late, from_previous, third_back, third_ahead, from_partner, fourth, from_diagonal
    )
    found = lax.all_to_all(pieces, "freq", 0, 0, tiled=True).reshape(2 * rows, rows)
    swapped = send(lax.dynamic_slice_in_dim(found, (1 - core) * rows, rows, 0), dc=1)

    same_y = step_y == 0
    inner_z = jnp.logical_or(z == 1, z == 2)
    by_row = jnp.where(
        step_z == 0,
        jnp.logical_or(same_y, yh == 1),
        jnp.where(step_z == 1, False, jnp.where(step_z == 2, jnp.where(same_y, inner_z, lower), True)),
    )
    return finished(jnp.stack([core, by_row.astype(jnp.int32)]), found, swapped, root)


def solution(mesh):
    placed = (P("blk", "freq"), P(), P(None, "freq"), P("freq"), P())
    return jax.shard_map(
        per_device, mesh=mesh, in_specs=placed, out_specs=P("blk", "freq"), check_vma=False
    )
```

```python
import jax
import jax.numpy as jnp
from jax import lax
from jax.experimental import pallas as pl
from jax.experimental.pallas import tpu as pltpu
from jax.sharding import PartitionSpec as P

BOTH = ("blk", "freq")
VMEM_BYTES = 60 * 1024 * 1024
LANES = 128
PARAMS = pltpu.CompilerParams(vmem_limit_bytes=VMEM_BYTES)
COST = pl.CostEstimate(flops=1024, bytes_accessed=1024, transcendentals=0)
VMEM = pl.BlockSpec(memory_space=pltpu.VMEM)
SMEM = pl.BlockSpec(memory_space=pltpu.SMEM)
ANY = pl.BlockSpec(memory_space=pl.ANY)


def places():
    return [
        (yh, z, c, f) for yh in range(2) for z in range(4) for c in range(2) for f in range(8)
    ]


def place_index(yh, z, c, f):
    return (((yh % 2) * 4 + z % 4) * 2 + c % 2) * 8 + f % 8


def route(dyh, dz, dc, dyl):
    return [
        (place_index(yh, z, c, f), place_index(yh + dyh, z + dz, c + dc, f + 4 * dyl))
        for yh, z, c, f in places()
    ]


def send(block, dyh=0, dz=0, dc=0, dyl=0):
    return lax.ppermute(block, BOTH, route(dyh, dz, dc, dyl))


def summed_along_x(tiles):
    groups = [list(range(4)), list(range(4, 8))]
    return summed(lax.all_to_all(tiles, "freq", 0, 0, axis_index_groups=groups, tiled=True))


def sum_kernel(tiles, out):
    total = tiles[0]
    for i in range(1, tiles.shape[0]):
        total = total + tiles[i]
    out[...] = total


def summed(tiles):
    return pl.pallas_call(
        sum_kernel,
        in_specs=[VMEM],
        out_specs=VMEM,
        out_shape=jax.ShapeDtypeStruct(tiles.shape[1:], tiles.dtype),
        compiler_params=PARAMS,
        cost_estimate=COST,
    )(tiles)


def together(*arrays):
    return lax.optimization_barrier(arrays)


def scaled(block, weight):
    return (block.astype(jnp.float32) * weight).astype(jnp.bfloat16)


def gram(a, b):
    return lax.dot_general(a, b, (((1,), (1,)), ((), ())), preferred_element_type=jnp.float32)


CORE, YH, Z, HIGH, NEXT_HIGH, PREV_HIGH, ON_B2, ON_B3, ON_B5, ON_B6 = range(10)


def span(which, half):
    return pl.ds(pl.multiple_of(which * half, LANES), half)


def spread_pairs():
    place = lax.broadcasted_iota(jnp.int32, (LANES, 2 * LANES), 0)
    return (lax.broadcasted_iota(jnp.int32, (LANES, 2 * LANES), 1) // 2 == place).astype(jnp.bfloat16)


def mask_kernel(info, hot, spectra, wedges, own, to_partner, to_next, to_previous, to_partner_b, to_previous_b, pairs):
    half = spectra.shape[1] // 2

    @pl.when(pl.program_id(0) == 0)
    def _():
        spread = spread_pairs()
        for j in range(half // LANES):
            some = wedges[:, pl.ds(j * LANES, LANES)].astype(jnp.float32).astype(jnp.bfloat16)
            wide = jnp.dot(some, spread, preferred_element_type=jnp.float32)
            pairs[:, pl.ds(j * 2 * LANES, 2 * LANES)] = wide.astype(jnp.bfloat16)

    keep = jnp.dot(hot[...], pairs[...], preferred_element_type=jnp.float32).astype(jnp.bfloat16)
    own[...] = spectra[...] * keep
    to_partner[...] = own[:, span(1 - info[YH], half)]
    to_next[...] = own[:, span(info[NEXT_HIGH], half)]
    to_previous[...] = own[:, span(info[PREV_HIGH], half)]
    to_partner_b[...] = own[:, span(info[YH], half)]
    to_previous_b[...] = own[:, span(1 - info[PREV_HIGH], half)]


def masked_blocks(info, hot, spectra, wedges):
    rows, width = spectra.shape
    classes = wedges.shape[0]
    part = rows // 4
    whole = lambda *shape: pl.BlockSpec(shape, lambda i, info: (0, 0))
    slab = lambda n: pl.BlockSpec((part, n), lambda i, info: (i, 0))
    half_block = jax.ShapeDtypeStruct((rows, width // 2), jnp.bfloat16)
    return pl.pallas_call(
        mask_kernel,
        grid_spec=pltpu.PrefetchScalarGridSpec(
            num_scalar_prefetch=1,
            grid=(4,),
            in_specs=[slab(classes), slab(width), whole(classes, width // 2)],
            out_specs=[slab(width)] + [slab(width // 2)] * 5 + [whole(classes, width)],
        ),
        out_shape=[
            jax.ShapeDtypeStruct((rows, width), jnp.bfloat16),
            *[half_block] * 5,
            jax.ShapeDtypeStruct((classes, width), jnp.bfloat16),
        ],
        compiler_params=PARAMS,
        cost_estimate=COST,
    )(info, hot, spectra, wedges)


def weight_kernel(shell_weight, shells, weight):
    spread = spread_pairs()

    def widen(x):
        return jnp.dot(x, spread, preferred_element_type=jnp.float32)

    for j in range(shells.shape[1] // LANES):
        shell = shells[:, pl.ds(j * LANES, LANES)]
        value = jnp.zeros(shell.shape, jnp.float32)
        for k in range(shell_weight.shape[0]):
            value = jnp.where(shell == k, shell_weight[k], value)
        top = value.astype(jnp.bfloat16)
        rest = value - top.astype(jnp.float32)
        middle = rest.astype(jnp.bfloat16)
        low = (rest - middle.astype(jnp.float32)).astype(jnp.bfloat16)
        weight[:, pl.ds(j * 2 * LANES, 2 * LANES)] = (widen(top) + widen(middle)) + widen(low)


def pair_weights(shell_weight, shells):
    return pl.pallas_call(
        weight_kernel,
        in_specs=[SMEM, VMEM],
        out_specs=VMEM,
        out_shape=jax.ShapeDtypeStruct((1, 2 * shells.shape[1]), jnp.float32),
        compiler_params=PARAMS,
        cost_estimate=COST,
    )(shell_weight, shells)


def first_kernel(info, own, sibling, energy, weight, out, own_w):
    slices = own.shape[0] // 4
    for x in range(4):
        out[x, 2 * slices :] = energy[...]
    own_w[...] = scaled(own[...], weight[...])

    def put(core, tile):
        at = pl.ds(pl.multiple_of(core * slices, 8), slices)
        out[:, at] = tile.reshape(4, slices, tile.shape[1])

    put(info[CORE], gram(own_w[...], own[...]))

    @pl.when(info[CORE] == 0)
    def _():
        put(1, gram(sibling[...], own_w[...]))

    @pl.when(info[CORE] == 1)
    def _():
        put(0, gram(scaled(sibling[...], weight[...]), own[...]))


def first_tiles(info, own, sibling, energy, weight):
    rows, width = own.shape
    return pl.pallas_call(
        first_kernel,
        in_specs=[SMEM, VMEM, VMEM, VMEM, VMEM],
        out_specs=[VMEM, VMEM],
        out_shape=[
            jax.ShapeDtypeStruct((4, rows // 2 + energy.shape[0], rows), jnp.float32),
            jax.ShapeDtypeStruct((rows, width), jnp.bfloat16),
        ],
        compiler_params=PARAMS,
        cost_estimate=COST,
    )(info, own, sibling, energy, weight)


def middle_kernel(
    info, own, own_w, sibling, partner, partner_s, following, previous, third_a_s, weight_yh, weight_high, out, scaled_b
):
    slices = partner.shape[0] // 4
    lower, on_b3, core = info[YH] == 0, info[ON_B3] == 1, info[CORE]
    w_yh, w_high = weight_yh[...], weight_high[...]

    def put(k, owner, tile):
        at = pl.ds(pl.multiple_of((2 * owner + k) * slices, 8), slices)
        out[:, at] = tile.reshape(4, slices, tile.shape[1])

    for is_low, third_a, third_b in ((True, following, previous), (False, previous, following)):
        is_plane = (info[Z] < 2) == is_low

        @pl.when(jnp.logical_and(is_plane, on_b3))
        def _(third_a=third_a, third_b=third_b):
            scaled_b[...] = scaled(third_b[...], w_high)
            put(0, core, gram(third_a[...], scaled_b[...]))
            put(0, 1 - core, gram(third_a_s[...], scaled_b[...]))

        @pl.when(jnp.logical_and(is_plane, jnp.logical_not(on_b3)))
        def _(third_a=third_a, third_b=third_b):
            put(0, core, gram(scaled(third_a[...], w_high), third_b[...]))
            put(0, 1 - core, gram(scaled(third_a_s[...], w_high), third_b[...]))

    @pl.when(lower)
    def _():
        put(1, core, gram(partner[...], own_w[...]))

        @pl.when(core == 1)
        def _():
            put(1, 0, gram(partner_s[...], own_w[...]))

        @pl.when(core == 0)
        def _():
            put(1, 1, gram(scaled(partner_s[...], w_yh), own[...]))

    @pl.when(jnp.logical_not(lower))
    def _():
        scaled_b[...] = scaled(partner[...], w_yh)
        put(1, core, gram(own[...], scaled_b[...]))

        @pl.when(core == 1)
        def _():
            put(1, 0, gram(sibling[...], scaled_b[...]))

        @pl.when(core == 0)
        def _():
            put(1, 1, gram(scaled(sibling[...], w_yh), partner[...]))


def middle_tiles(info, own, own_w, sibling, partner, partner_s, following, previous, third_a_s, weight):
    rows, width = own.shape
    half = width // 2
    at_yh = lambda n: pl.BlockSpec((n, half), lambda i, info: (0, info[YH]))
    whole = pl.BlockSpec((rows, half), lambda i, info: (0, 0))
    return pl.pallas_call(
        middle_kernel,
        grid_spec=pltpu.PrefetchScalarGridSpec(
            num_scalar_prefetch=1,
            grid=(1,),
            in_specs=[at_yh(rows)] * 3
            + [whole] * 5
            + [at_yh(1), pl.BlockSpec((1, half), lambda i, info: (0, info[HIGH]))],
            out_specs=pl.BlockSpec((4, rows, rows), lambda i, info: (0, 0, 0)),
            scratch_shapes=[pltpu.VMEM((rows, half), jnp.bfloat16)],
        ),
        out_shape=jax.ShapeDtypeStruct((4, rows, rows), jnp.float32),
        compiler_params=PARAMS,
        cost_estimate=COST,
    )(info, own, own_w, sibling, partner, partner_s, following, previous, third_a_s, weight, weight)


def late_kernel(
    is_mine, info, own, own_w, partner_a, partner_b, a_high, a_low, mine_high, mine_low, diagonal, a_diagonal,
    weight, *rest,
):
    out, a, a_w, own_b, partner, sixth_a, sixth_b, tiles, sems, out_sems = rest[-10:]
    half = partner_a.shape[1]
    slices = out.shape[2]
    lower = info[YH] == 0
    high_is_yh = info[HIGH] == info[YH]
    high, yh = info[HIGH], info[YH]

    def pick(n, dst, *choices):
        for chosen, src in choices:

            @pl.when(chosen)
            def _(src=src):
                pltpu.make_async_copy(src, dst, sems.at[n]).start()

        return pltpu.make_async_copy(choices[0][1], dst, sems.at[n])

    always = info[CORE] >= 0
    no = jnp.logical_not
    got_high = pick(0, a.at[:, span(high, half)], (always, a_high))
    got_low = pick(1, a.at[:, span(1 - high, half)], (always, a_low))
    got_own = pick(2, own_b, (info[ON_B2] == 1, own_w), (info[ON_B2] == 0, own))
    got_near = pick(3, partner.at[:, span(yh, half)], (always, partner_a))
    got_far = pick(4, partner.at[:, span(1 - yh, half)], (always, partner_b))
    got_a = pick(
        5,
        sixth_a,
        (no(lower), a_diagonal),
        (jnp.logical_and(lower, high_is_yh), a_high),
        (jnp.logical_and(lower, no(high_is_yh)), a_low),
    )
    got_b = pick(
        6,
        sixth_b,
        (lower, diagonal),
        (jnp.logical_and(no(lower), high_is_yh), mine_high),
        (jnp.logical_and(no(lower), no(high_is_yh)), mine_low),
    )
    owner = info[CORE] if is_mine else 1 - info[CORE]
    sent = []

    def put(k, tile):
        tiles[k] = tile.reshape(4, slices, tile.shape[1])

    def leave(k):
        copy = pltpu.make_async_copy(tiles.at[k], out.at[pl.ds(owner * 4, 4), k], out_sems.at[k])
        copy.start()
        sent.append(copy)

    got_high.wait()
    got_low.wait()
    a_w[...] = scaled(a[...], weight[...])
    got_own.wait()

    @pl.when(info[ON_B2] == 1)
    def _():
        put(0, gram(a[...], own_b[...]))

    @pl.when(info[ON_B2] == 0)
    def _():
        put(0, gram(a_w[...], own_b[...]))

    leave(0)
    got_near.wait()
    got_far.wait()

    @pl.when(info[ON_B5] == 1)
    def _():
        partner[...] = scaled(partner[...], weight[...])
        put(1, gram(a[...], partner[...]))

    @pl.when(info[ON_B5] == 0)
    def _():
        put(1, gram(a_w[...], partner[...]))

    leave(1)
    got_a.wait()
    got_b.wait()
    w_yh = weight[:, span(yh, half)]

    @pl.when(info[ON_B6] == 1)
    def _():
        sixth_b[...] = scaled(sixth_b[...], w_yh)

    @pl.when(info[ON_B6] == 0)
    def _():
        sixth_a[...] = scaled(sixth_a[...], w_yh)

    put(2, gram(sixth_a[...], sixth_b[...]))
    leave(2)
    for copy in sent:
        copy.wait()


def late_tiles(is_mine, info, own, own_w, partner_a, partner_b, a_high, a_low, mine_high, mine_low, diagonal,
               a_diagonal, weight, other=None):
    rows, width = own.shape
    half = width // 2
    arrays = [own, own_w, partner_a, partner_b, a_high, a_low, mine_high, mine_low, diagonal, a_diagonal, weight]
    specs = [SMEM] + [ANY] * 10 + [VMEM]
    aliases = {}
    if other is not None:
        arrays.append(other)
        specs.append(ANY)
        aliases = {len(specs) - 1: 0}
    block = lambda n: pltpu.VMEM((rows, n), jnp.bfloat16)

    def kernel(*refs):
        late_kernel(is_mine, *refs)

    return pl.pallas_call(
        kernel,
        in_specs=specs,
        out_specs=ANY,
        out_shape=jax.ShapeDtypeStruct((8, 3, rows // 4, rows), jnp.float32),
        scratch_shapes=[
            block(width),
            block(width),
            block(width),
            block(width),
            block(half),
            block(half),
            pltpu.VMEM((3, 4, rows // 4, rows), jnp.float32),
            pltpu.SemaphoreType.DMA((7,)),
            pltpu.SemaphoreType.DMA((3,)),
        ],
        input_output_aliases=aliases,
        compiler_params=PARAMS,
        cost_estimate=COST,
    )(info, *arrays)


def gather_kernel(info, early, late, from_previous, third_back, third_ahead, from_partner, fourth, from_diagonal, out):
    yh, z = info[YH], info[Z]

    def put(dyh, dz, value):
        out[(yh + dyh) % 2 * 4 + (z + dz) % 4] = value

    slices = out.shape[1]
    put(0, 0, early[:slices])
    put(0, 1, late[0])
    put(0, 2, third_back[...] + third_ahead[...])
    put(0, 3, from_previous[0])
    put(1, 0, early[2 * slices : 3 * slices] + fourth[...])
    put(1, 1, from_partner[...])
    put(1, 2, from_previous[2] + from_diagonal[...])
    put(1, 3, from_previous[1])


def gathered(info, *parts):
    slices, rows = parts[1].shape[1:]
    return pl.pallas_call(
        gather_kernel,
        in_specs=[SMEM] + [VMEM] * len(parts),
        out_specs=VMEM,
        out_shape=jax.ShapeDtypeStruct((8, slices, rows), jnp.float32),
    )(info, *parts)


def final_kernel(info, found, swapped, root, out):
    rows = swapped.shape[0]
    core, by_row = info[0], info[1]

    for is_first in (True, False):

        @pl.when(jnp.logical_and(by_row == 1, (core == 0) == is_first))
        def _(is_first=is_first):
            kept = found[:rows] if is_first else found[rows:]
            pair = (kept, swapped[...]) if is_first else (swapped[...], kept)
            out[...] = jnp.concatenate(pair, 1) / root[...]

    @pl.when(by_row == 0)
    def _():
        out[...] = found[...].T / root[...]


def finished(info, found, swapped, root):
    return pl.pallas_call(
        final_kernel,
        in_specs=[SMEM, VMEM, VMEM, VMEM],
        out_specs=VMEM,
        out_shape=jax.ShapeDtypeStruct(root.shape, jnp.float32),
    )(info, found, swapped, root)


def per_device(spectra, labels, wedges, shells, shell_weight):
    rows, width = spectra.shape
    half, slices = width // 2, rows // 4
    classes = wedges.shape[0]
    blk = lax.axis_index("blk")
    core, z, yh = blk % 2, (blk // 2) % 4, blk // 8
    freq = lax.axis_index("freq")

    def place(dyh, dz):
        return ((yh + dyh) % 2) * 4 + (z + dz) % 4

    def ahead(a, b):
        return ((a - b) % 8 < 4).astype(jnp.int32)

    def columns(block, which):
        return lax.dynamic_slice_in_dim(block, which * half, half, 1)

    low, lower = z < 2, yh == 0
    high = z // 2
    previous_high = ((z + 3) % 4) // 2
    info = jnp.stack(
        [
            core,
            yh,
            z,
            high,
            ((z + 1) % 4) // 2,
            previous_high,
            ahead(place(0, 1), place(0, 0)),
            jnp.where(low, ahead(place(0, 1), place(0, -1)), ahead(place(0, -1), place(0, 1))),
            ahead(place(0, 1), place(1, 0)),
            jnp.where(lower, ahead(place(0, 1), place(1, -1)), ahead(place(1, -1), place(0, 1))),
        ]
    ).astype(jnp.int32)

    class_range = jnp.arange(classes, dtype=jnp.int32)
    own_labels = lax.dynamic_slice_in_dim(labels, blk * rows, rows)
    hot = (own_labels[:, None] == class_range[None, :]).astype(jnp.bfloat16)
    own, to_partner, to_next, to_previous, to_partner_b, to_previous_b, pairs = masked_blocks(info, hot, spectra, wedges)

    following_a = send(to_previous, dz=-1)
    partner_a = send(to_partner, dyh=1)
    previous = send(to_next, dz=1)
    following_b = send(to_previous_b, dz=-1)
    sibling = send(own, dc=1)
    own, shells = together(own, shells)
    weight = pair_weights(shell_weight, shells[None, :])
    squares = own.astype(jnp.float32) ** 2 * weight
    partial_energy = lax.dot_general(
        pairs.astype(jnp.float32), squares, (((1,), (1,)), ((), ())), precision=lax.Precision.HIGHEST
    )
    q1, own_w = first_tiles(info, own, sibling, partial_energy, weight)
    p1 = summed_along_x(q1)
    partner_b = send(to_partner_b, dyh=1)
    partner_a, p1 = together(partner_a, p1)
    diagonal = send(partner_a, dz=1)
    partner_s = send(partner_a, dc=1)
    third_a_s = send(jnp.where(low, following_a, previous), dc=1)
    middle = middle_tiles(
        info, own, own_w, sibling, partner_a, partner_s, following_a, previous, third_a_s, weight
    )
    middle = summed_along_x(middle)
    following_b, partner_b, diagonal, middle = together(following_b, partner_b, diagonal, middle)

    following_as = send(following_a, dc=1)
    following_bs = send(following_b, dc=1)
    diagonal_s = send(diagonal, dc=1)
    late = late_tiles(
        True, info, own, own_w, partner_a, partner_b, following_a, following_b, following_a, following_b,
        diagonal, diagonal, weight,
    )
    late, following_as, following_bs, diagonal_s = together(late, following_as, following_bs, diagonal_s)
    late = late_tiles(
        False, info, own, own_w, partner_a, partner_b, following_as, following_bs, following_a, following_b,
        diagonal, diagonal_s, weight, late,
    )
    late = lax.all_to_all(late, "freq", 0, 0, tiled=True)

    own_yl = freq // 4

    def halves(which):
        return [
            lax.dynamic_slice_in_dim(p1, which * slices, slices, 0),
            lax.dynamic_slice_in_dim(middle, which * 2 * slices, 2 * slices, 0),
            p1[2 * slices :],
        ]

    early = jnp.concatenate(halves(own_yl)) + send(jnp.concatenate(halves(1 - own_yl)), dyl=1)
    third, energy = early[slices : 2 * slices], early[3 * slices :]
    third_energy = jnp.concatenate([third, energy])
    back, forth, opposite = send(third_energy, dz=1), send(third_energy, dz=-1), send(energy, dz=2)
    third_back, third_ahead = back[:slices], forth[:slices]
    plane = jnp.concatenate([energy, forth[slices:], opposite, back[slices:]])
    from_other = send(jnp.concatenate([early[2 * slices : 3 * slices], plane]), dyh=1)
    fourth = from_other[:slices]
    energies = jnp.concatenate([plane, from_other[slices:]])
    energies_s = send(energies, dc=1)
    step_y, step_z = (freq // 4 + yh) % 2, (freq % 4 - z) % 4
    column_energy = [
        lax.dynamic_slice_in_dim(e, (step_y * 4 + step_z) * classes, classes, 0) for e in (energies, energies_s)
    ]
    column_energy = jnp.where(
        core == 0, jnp.concatenate(column_energy, 1), jnp.concatenate(column_energy[::-1], 1)
    )
    column_labels = lax.dynamic_slice_in_dim(labels, freq * 2 * rows, 2 * rows)
    row_side = jnp.zeros((rows, 2 * rows), jnp.float32)
    column_side = jnp.zeros((rows, 2 * rows), jnp.float32)
    for d in range(classes):
        row_side = jnp.where(column_labels[None, :] == d, energy[d][:, None], row_side)
        column_side = jnp.where(own_labels[:, None] == d, column_energy[d][None, :], column_side)
    root = jnp.sqrt(row_side * column_side + 1e-06)
    late, third_back, third_ahead, fourth, root = together(late, third_back, third_ahead, fourth, root)
    late = jnp.sum(late, 0)

    from_previous = send(late, dz=1)
    from_partner = send(late[1], dyh=1)
    from_diagonal = send(late[2], dyh=1, dz=-1)
    from_previous, from_partner, from_diagonal = together(from_previous, from_partner, from_diagonal)
    pieces = gathered(
        info, early, late, from_previous, third_back, third_ahead, from_partner, fourth, from_diagonal
    )
    found = lax.all_to_all(pieces, "freq", 0, 0, tiled=True).reshape(2 * rows, rows)
    swapped = send(lax.dynamic_slice_in_dim(found, (1 - core) * rows, rows, 0), dc=1)

    same_y = step_y == 0
    inner_z = jnp.logical_or(z == 1, z == 2)
    by_row = jnp.where(
        step_z == 0,
        jnp.logical_or(same_y, yh == 1),
        jnp.where(step_z == 1, False, jnp.where(step_z == 2, jnp.where(same_y, inner_z, lower), True)),
    )
    return finished(jnp.stack([core, by_row.astype(jnp.int32)]), found, swapped, root)


def solution(mesh):
    placed = (P("blk", "freq"), P(), P(None, "freq"), P("freq"), P())
    return jax.shard_map(
        per_device, mesh=mesh, in_specs=placed, out_specs=P("blk", "freq"), check_vma=False
    )
```

```python
import jax
import jax.numpy as jnp
from jax import lax
from jax.experimental import pallas as pl
from jax.experimental.pallas import tpu as pltpu
from jax.sharding import PartitionSpec as P

BOTH = ("blk", "freq")
VMEM_BYTES = 60 * 1024 * 1024
LANES = 128
PARAMS = pltpu.CompilerParams(vmem_limit_bytes=VMEM_BYTES)
COST = pl.CostEstimate(flops=1024, bytes_accessed=1024, transcendentals=0)
VMEM = pl.BlockSpec(memory_space=pltpu.VMEM)
SMEM = pl.BlockSpec(memory_space=pltpu.SMEM)
ANY = pl.BlockSpec(memory_space=pl.ANY)


def places():
    return [
        (yh, z, c, f) for yh in range(2) for z in range(4) for c in range(2) for f in range(8)
    ]


def place_index(yh, z, c, f):
    return (((yh % 2) * 4 + z % 4) * 2 + c % 2) * 8 + f % 8


def route(dyh, dz, dc, dyl):
    return [
        (place_index(yh, z, c, f), place_index(yh + dyh, z + dz, c + dc, f + 4 * dyl))
        for yh, z, c, f in places()
    ]


def send(block, dyh=0, dz=0, dc=0, dyl=0):
    return lax.ppermute(block, BOTH, route(dyh, dz, dc, dyl))


def summed_along_x(tiles):
    groups = [list(range(4)), list(range(4, 8))]
    return summed(lax.all_to_all(tiles, "freq", 0, 0, axis_index_groups=groups, tiled=True))


def sum_kernel(tiles, out):
    total = tiles[0]
    for i in range(1, tiles.shape[0]):
        total = total + tiles[i]
    out[...] = total


def summed(tiles):
    return pl.pallas_call(
        sum_kernel,
        in_specs=[VMEM],
        out_specs=VMEM,
        out_shape=jax.ShapeDtypeStruct(tiles.shape[1:], tiles.dtype),
        compiler_params=PARAMS,
        cost_estimate=COST,
    )(tiles)


def together(*arrays):
    return lax.optimization_barrier(arrays)


def scaled(block, weight):
    return (block.astype(jnp.float32) * weight).astype(jnp.bfloat16)


def gram(a, b):
    return lax.dot_general(a, b, (((1,), (1,)), ((), ())), preferred_element_type=jnp.float32)


CORE, YH, Z, HIGH, NEXT_HIGH, PREV_HIGH, ON_B2, ON_B3, ON_B5, ON_B6 = range(10)


def span(which, half):
    return pl.ds(pl.multiple_of(which * half, LANES), half)


def spread_pairs():
    place = lax.broadcasted_iota(jnp.int32, (LANES, 2 * LANES), 0)
    return (lax.broadcasted_iota(jnp.int32, (LANES, 2 * LANES), 1) // 2 == place).astype(jnp.bfloat16)


def mask_kernel(info, hot, spectra, wedges, own, to_partner, to_next, to_previous, to_partner_b, to_previous_b, pairs):
    half = spectra.shape[1] // 2

    @pl.when(pl.program_id(0) == 0)
    def _():
        spread = spread_pairs()
        for j in range(half // LANES):
            some = wedges[:, pl.ds(j * LANES, LANES)].astype(jnp.float32).astype(jnp.bfloat16)
            wide = jnp.dot(some, spread, preferred_element_type=jnp.float32)
            pairs[:, pl.ds(j * 2 * LANES, 2 * LANES)] = wide.astype(jnp.bfloat16)

    keep = jnp.dot(hot[...], pairs[...], preferred_element_type=jnp.float32).astype(jnp.bfloat16)
    own[...] = spectra[...] * keep
    to_partner[...] = own[:, span(1 - info[YH], half)]
    to_next[...] = own[:, span(info[NEXT_HIGH], half)]
    to_previous[...] = own[:, span(info[PREV_HIGH], half)]
    to_partner_b[...] = own[:, span(info[YH], half)]
    to_previous_b[...] = own[:, span(1 - info[PREV_HIGH], half)]


def masked_blocks(info, hot, spectra, wedges):
    rows, width = spectra.shape
    classes = wedges.shape[0]
    part = rows // 4
    whole = lambda *shape: pl.BlockSpec(shape, lambda i, info: (0, 0))
    slab = lambda n: pl.BlockSpec((part, n), lambda i, info: (i, 0))
    half_block = jax.ShapeDtypeStruct((rows, width // 2), jnp.bfloat16)
    return pl.pallas_call(
        mask_kernel,
        grid_spec=pltpu.PrefetchScalarGridSpec(
            num_scalar_prefetch=1,
            grid=(4,),
            in_specs=[slab(classes), slab(width), whole(classes, width // 2)],
            out_specs=[slab(width)] + [slab(width // 2)] * 5 + [whole(classes, width)],
        ),
        out_shape=[
            jax.ShapeDtypeStruct((rows, width), jnp.bfloat16),
            *[half_block] * 5,
            jax.ShapeDtypeStruct((classes, width), jnp.bfloat16),
        ],
        compiler_params=PARAMS,
        cost_estimate=COST,
    )(info, hot, spectra, wedges)


def weight_kernel(shell_weight, shells, weight):
    spread = spread_pairs()

    def widen(x):
        return jnp.dot(x, spread, preferred_element_type=jnp.float32)

    for j in range(shells.shape[1] // LANES):
        shell = shells[:, pl.ds(j * LANES, LANES)]
        value = jnp.zeros(shell.shape, jnp.float32)
        for k in range(shell_weight.shape[0]):
            value = jnp.where(shell == k, shell_weight[k], value)
        top = value.astype(jnp.bfloat16)
        rest = value - top.astype(jnp.float32)
        middle = rest.astype(jnp.bfloat16)
        low = (rest - middle.astype(jnp.float32)).astype(jnp.bfloat16)
        weight[:, pl.ds(j * 2 * LANES, 2 * LANES)] = (widen(top) + widen(middle)) + widen(low)


def pair_weights(shell_weight, shells):
    return pl.pallas_call(
        weight_kernel,
        in_specs=[SMEM, VMEM],
        out_specs=VMEM,
        out_shape=jax.ShapeDtypeStruct((1, 2 * shells.shape[1]), jnp.float32),
        compiler_params=PARAMS,
        cost_estimate=COST,
    )(shell_weight, shells)


def first_kernel(info, own, sibling, weight, out, own_w, a, a_w, other, tiles, sems, out_sems):
    core = info[CORE]
    got_own = pltpu.make_async_copy(own, a, sems.at[0])
    got_sibling = pltpu.make_async_copy(sibling, other, sems.at[1])
    got_own.start()
    got_sibling.start()

    def leave(k, owner):
        copy = pltpu.make_async_copy(tiles.at[k], out.at[:, owner], out_sems.at[k])
        copy.start()
        return copy

    def put(k, tile):
        tiles[k] = tile.reshape(tiles.shape[1:])

    got_own.wait()
    a_w[...] = scaled(a[...], weight[...])
    left_w = pltpu.make_async_copy(a_w, own_w, out_sems.at[2])
    left_w.start()
    put(0, gram(a_w[...], a[...]))
    left_mine = leave(0, core)
    got_sibling.wait()

    @pl.when(core == 0)
    def _():
        put(1, gram(other[...], a_w[...]))

    @pl.when(core == 1)
    def _():
        put(1, gram(scaled(other[...], weight[...]), a[...]))

    left_other = leave(1, 1 - core)
    left_w.wait()
    left_mine.wait()
    left_other.wait()


def first_tiles(info, own, sibling, weight):
    rows, width = own.shape
    block = pltpu.VMEM((rows, width), jnp.bfloat16)
    return pl.pallas_call(
        first_kernel,
        in_specs=[SMEM, ANY, ANY, VMEM],
        out_specs=[ANY, ANY],
        out_shape=[
            jax.ShapeDtypeStruct((4, 2, rows // 4, rows), jnp.float32),
            jax.ShapeDtypeStruct((rows, width), jnp.bfloat16),
        ],
        scratch_shapes=[
            block,
            block,
            block,
            pltpu.VMEM((2, 4, rows // 4, rows), jnp.float32),
            pltpu.SemaphoreType.DMA((2,)),
            pltpu.SemaphoreType.DMA((3,)),
        ],
        compiler_params=PARAMS,
        cost_estimate=COST,
    )(info, own, sibling, weight)


def half_kernel(
    info, a_yes, a_no, other_yes, other_no, b_yes, b_no, weight, energy, out, a, other, b, b_w, tiles, sems, out_sems
):
    rows, half = a.shape
    core, first, on_b, on_b_other, at = info[0], info[1] == 1, info[2] == 1, info[3] == 1, span(info[4], half)
    w = weight[:, at]

    def pick(n, dst, yes, no):
        for chosen, src in ((first, yes), (jnp.logical_not(first), no)):
            src = src if src.shape[1] == half else src.at[:, at]

            @pl.when(chosen)
            def _(src=src):
                pltpu.make_async_copy(src, dst, sems.at[n]).start()

        return pltpu.make_async_copy(src, dst, sems.at[n])

    got_b = pick(0, b, b_yes, b_no)
    got_a = pick(1, a, a_yes, a_no)
    got_other = pick(2, other, other_yes, other_no)
    slices = tiles.shape[2]
    sent = []
    for x in range(4):
        copy = pltpu.make_async_copy(energy, out.at[x, pl.ds(2 * slices, energy.shape[0])], out_sems.at[2 + x])
        copy.start()
        sent.append(copy)
    got_b.wait()
    b_w[...] = scaled(b[...], w)

    def put(k, block, weighted, owner):
        @pl.when(weighted)
        def _():
            tiles[k] = gram(block[...], b_w[...]).reshape(tiles.shape[1:])

        @pl.when(jnp.logical_not(weighted))
        def _():
            tiles[k] = gram(scaled(block[...], w), b[...]).reshape(tiles.shape[1:])

        at = pl.ds(pl.multiple_of(owner * slices, 8), slices)
        copy = pltpu.make_async_copy(tiles.at[k], out.at[:, at], out_sems.at[k])
        copy.start()
        sent.append(copy)

    got_a.wait()
    put(0, a, on_b, core)
    got_other.wait()
    put(1, other, on_b_other, 1 - core)
    for copy in sent:
        copy.wait()


def half_tiles(info, *operands):
    rows, classes = operands[0].shape[0], operands[-1].shape[0]
    half = operands[-2].shape[1] // 2
    block = pltpu.VMEM((rows, half), jnp.bfloat16)
    return pl.pallas_call(
        half_kernel,
        in_specs=[SMEM] + [ANY] * 6 + [VMEM] * 2,
        out_specs=ANY,
        out_shape=jax.ShapeDtypeStruct((4, rows // 2 + classes, rows), jnp.float32),
        scratch_shapes=[
            block,
            block,
            block,
            block,
            pltpu.VMEM((2, 4, rows // 4, rows), jnp.float32),
            pltpu.SemaphoreType.DMA((3,)),
            pltpu.SemaphoreType.DMA((6,)),
        ],
        compiler_params=PARAMS,
        cost_estimate=COST,
    )(info, *operands)


def late_kernel(
    is_mine, info, own, own_w, partner_a, partner_b, a_high, a_low, mine_high, mine_low, diagonal, a_diagonal,
    weight, *rest,
):
    out, a, a_w, own_b, partner, sixth_a, sixth_b, tiles, sems, out_sems = rest[-10:]
    half = partner_a.shape[1]
    slices = out.shape[2]
    lower = info[YH] == 0
    high_is_yh = info[HIGH] == info[YH]
    high, yh = info[HIGH], info[YH]

    def pick(n, dst, *choices):
        for chosen, src in choices:

            @pl.when(chosen)
            def _(src=src):
                pltpu.make_async_copy(src, dst, sems.at[n]).start()

        return pltpu.make_async_copy(choices[0][1], dst, sems.at[n])

    always = info[CORE] >= 0
    no = jnp.logical_not
    got_high = pick(0, a.at[:, span(high, half)], (always, a_high))
    got_low = pick(1, a.at[:, span(1 - high, half)], (always, a_low))
    got_own = pick(2, own_b, (info[ON_B2] == 1, own_w), (info[ON_B2] == 0, own))
    got_near = pick(3, partner.at[:, span(yh, half)], (always, partner_a))
    got_far = pick(4, partner.at[:, span(1 - yh, half)], (always, partner_b))
    got_a = pick(
        5,
        sixth_a,
        (no(lower), a_diagonal),
        (jnp.logical_and(lower, high_is_yh), a_high),
        (jnp.logical_and(lower, no(high_is_yh)), a_low),
    )
    got_b = pick(
        6,
        sixth_b,
        (lower, diagonal),
        (jnp.logical_and(no(lower), high_is_yh), mine_high),
        (jnp.logical_and(no(lower), no(high_is_yh)), mine_low),
    )
    owner = info[CORE] if is_mine else 1 - info[CORE]
    sent = []

    def put(k, tile):
        tiles[k] = tile.reshape(4, slices, tile.shape[1])

    def leave(k):
        copy = pltpu.make_async_copy(tiles.at[k], out.at[pl.ds(owner * 4, 4), k], out_sems.at[k])
        copy.start()
        sent.append(copy)

    got_high.wait()
    got_low.wait()
    a_w[...] = scaled(a[...], weight[...])
    got_own.wait()

    @pl.when(info[ON_B2] == 1)
    def _():
        put(0, gram(a[...], own_b[...]))

    @pl.when(info[ON_B2] == 0)
    def _():
        put(0, gram(a_w[...], own_b[...]))

    leave(0)
    got_near.wait()
    got_far.wait()

    @pl.when(info[ON_B5] == 1)
    def _():
        partner[...] = scaled(partner[...], weight[...])
        put(1, gram(a[...], partner[...]))

    @pl.when(info[ON_B5] == 0)
    def _():
        put(1, gram(a_w[...], partner[...]))

    leave(1)
    got_a.wait()
    got_b.wait()
    w_yh = weight[:, span(yh, half)]

    @pl.when(info[ON_B6] == 1)
    def _():
        sixth_b[...] = scaled(sixth_b[...], w_yh)

    @pl.when(info[ON_B6] == 0)
    def _():
        sixth_a[...] = scaled(sixth_a[...], w_yh)

    put(2, gram(sixth_a[...], sixth_b[...]))
    leave(2)
    for copy in sent:
        copy.wait()


def late_tiles(is_mine, info, own, own_w, partner_a, partner_b, a_high, a_low, mine_high, mine_low, diagonal,
               a_diagonal, weight, other=None):
    rows, width = own.shape
    half = width // 2
    arrays = [own, own_w, partner_a, partner_b, a_high, a_low, mine_high, mine_low, diagonal, a_diagonal, weight]
    specs = [SMEM] + [ANY] * 10 + [VMEM]
    aliases = {}
    if other is not None:
        arrays.append(other)
        specs.append(ANY)
        aliases = {len(specs) - 1: 0}
    block = lambda n: pltpu.VMEM((rows, n), jnp.bfloat16)

    def kernel(*refs):
        late_kernel(is_mine, *refs)

    return pl.pallas_call(
        kernel,
        in_specs=specs,
        out_specs=ANY,
        out_shape=jax.ShapeDtypeStruct((8, 3, rows // 4, rows), jnp.float32),
        scratch_shapes=[
            block(width),
            block(width),
            block(width),
            block(width),
            block(half),
            block(half),
            pltpu.VMEM((3, 4, rows // 4, rows), jnp.float32),
            pltpu.SemaphoreType.DMA((7,)),
            pltpu.SemaphoreType.DMA((3,)),
        ],
        input_output_aliases=aliases,
        compiler_params=PARAMS,
        cost_estimate=COST,
    )(info, *arrays)


def gather_kernel(info, early, late, from_previous, third_back, third_ahead, from_partner, fourth, from_diagonal, out):
    yh, z = info[YH], info[Z]

    def put(dyh, dz, value):
        out[(yh + dyh) % 2 * 4 + (z + dz) % 4] = value

    slices = out.shape[1]
    put(0, 0, early[:slices])
    put(0, 1, late[0])
    put(0, 2, third_back[...] + third_ahead[...])
    put(0, 3, from_previous[0])
    put(1, 0, early[2 * slices : 3 * slices] + fourth[...])
    put(1, 1, from_partner[...])
    put(1, 2, from_previous[2] + from_diagonal[...])
    put(1, 3, from_previous[1])


def gathered(info, *parts):
    slices, rows = parts[1].shape[1:]
    return pl.pallas_call(
        gather_kernel,
        in_specs=[SMEM] + [VMEM] * len(parts),
        out_specs=VMEM,
        out_shape=jax.ShapeDtypeStruct((8, slices, rows), jnp.float32),
    )(info, *parts)


def final_kernel(info, found, swapped, root, out):
    rows = swapped.shape[0]
    core, by_row = info[0], info[1]

    for is_first in (True, False):

        @pl.when(jnp.logical_and(by_row == 1, (core == 0) == is_first))
        def _(is_first=is_first):
            kept = found[:rows] if is_first else found[rows:]
            pair = (kept, swapped[...]) if is_first else (swapped[...], kept)
            out[...] = jnp.concatenate(pair, 1) / root[...]

    @pl.when(by_row == 0)
    def _():
        out[...] = found[...].T / root[...]


def finished(info, found, swapped, root):
    return pl.pallas_call(
        final_kernel,
        in_specs=[SMEM, VMEM, VMEM, VMEM],
        out_specs=VMEM,
        out_shape=jax.ShapeDtypeStruct(root.shape, jnp.float32),
    )(info, found, swapped, root)


def per_device(spectra, labels, wedges, shells, shell_weight):
    rows, width = spectra.shape
    half, slices = width // 2, rows // 4
    classes = wedges.shape[0]
    blk = lax.axis_index("blk")
    core, z, yh = blk % 2, (blk // 2) % 4, blk // 8
    freq = lax.axis_index("freq")

    def place(dyh, dz):
        return ((yh + dyh) % 2) * 4 + (z + dz) % 4

    def ahead(a, b):
        return ((a - b) % 8 < 4).astype(jnp.int32)

    def columns(block, which):
        return lax.dynamic_slice_in_dim(block, which * half, half, 1)

    low, lower = z < 2, yh == 0
    high = z // 2
    previous_high = ((z + 3) % 4) // 2
    info = jnp.stack(
        [
            core,
            yh,
            z,
            high,
            ((z + 1) % 4) // 2,
            previous_high,
            ahead(place(0, 1), place(0, 0)),
            jnp.where(low, ahead(place(0, 1), place(0, -1)), ahead(place(0, -1), place(0, 1))),
            ahead(place(0, 1), place(1, 0)),
            jnp.where(lower, ahead(place(0, 1), place(1, -1)), ahead(place(1, -1), place(0, 1))),
        ]
    ).astype(jnp.int32)

    class_range = jnp.arange(classes, dtype=jnp.int32)
    own_labels = lax.dynamic_slice_in_dim(labels, blk * rows, rows)
    hot = (own_labels[:, None] == class_range[None, :]).astype(jnp.bfloat16)
    own, to_partner, to_next, to_previous, to_partner_b, to_previous_b, pairs = masked_blocks(info, hot, spectra, wedges)

    following_a = send(to_previous, dz=-1)
    partner_a = send(to_partner, dyh=1)
    previous = send(to_next, dz=1)
    following_b = send(to_previous_b, dz=-1)
    sibling = send(own, dc=1)
    own, shells = together(own, shells)
    weight = pair_weights(shell_weight, shells[None, :])
    q1, own_w = first_tiles(info, own, sibling, weight)
    p1 = summed_along_x(q1)
    own_e, q1 = together(own, q1)
    squares = own_e.astype(jnp.float32) ** 2 * weight
    partial_energy = lax.dot_general(
        pairs.astype(jnp.float32), squares, (((1,), (1,)), ((), ())), precision=lax.Precision.HIGHEST
    )
    partner_b = send(to_partner_b, dyh=1)
    partner_a, p1, partial_energy = together(partner_a, p1, partial_energy)
    diagonal = send(partner_a, dz=1)
    partner_s = send(partner_a, dc=1)
    third_a_s = send(jnp.where(low, following_a, previous), dc=1)
    fourth_info = jnp.stack([core, 1 - yh, 1, core, yh]).astype(jnp.int32)
    third_info = jnp.stack([core, low.astype(jnp.int32), info[ON_B3], info[ON_B3], high]).astype(jnp.int32)
    q4 = half_tiles(fourth_info, partner_a, own, partner_s, sibling, own, partner_a, weight, partial_energy)
    p4 = summed_along_x(q4)
    third_a_s, q4 = together(third_a_s, q4)
    q3 = half_tiles(third_info, following_a, previous, third_a_s, third_a_s, previous, following_a, weight, partial_energy)
    following_b, partner_b, diagonal, p4, q3 = together(following_b, partner_b, diagonal, p4, q3)
    p3 = summed_along_x(q3)

    following_as = send(following_a, dc=1)
    following_bs = send(following_b, dc=1)
    diagonal_s = send(diagonal, dc=1)
    late = late_tiles(
        True, info, own, own_w, partner_a, partner_b, following_a, following_b, following_a, following_b,
        diagonal, diagonal, weight,
    )
    late, following_as, following_bs, diagonal_s = together(late, following_as, following_bs, diagonal_s)
    late = late_tiles(
        False, info, own, own_w, partner_a, partner_b, following_as, following_bs, following_a, following_b,
        diagonal, diagonal_s, weight, late,
    )
    late, p3 = together(late, p3)
    late = lax.all_to_all(late, "freq", 0, 0, tiled=True)

    own_yl = freq // 4

    def halves(which):
        return [
            lax.dynamic_index_in_dim(p1, which, 0, keepdims=False),
            lax.dynamic_slice_in_dim(p3, which * slices, slices, 0),
            lax.dynamic_slice_in_dim(p4, which * slices, slices, 0),
            p4[2 * slices :],
        ]

    early = jnp.concatenate(halves(own_yl)) + send(jnp.concatenate(halves(1 - own_yl)), dyl=1)
    third, energy = early[slices : 2 * slices], early[3 * slices :]
    third_energy = jnp.concatenate([third, energy])
    back, forth, opposite = send(third_energy, dz=1), send(third_energy, dz=-1), send(energy, dz=2)
    third_back, third_ahead = back[:slices], forth[:slices]
    plane = jnp.concatenate([energy, forth[slices:], opposite, back[slices:]])
    from_other = send(jnp.concatenate([early[2 * slices : 3 * slices], plane]), dyh=1)
    fourth = from_other[:slices]
    energies = jnp.concatenate([plane, from_other[slices:]])
    energies_s = send(energies, dc=1)
    late, third_back, third_ahead, fourth, energies_s = together(
        late, third_back, third_ahead, fourth, energies_s
    )
    late = jnp.sum(late, 0)

    from_previous = send(late, dz=1)
    from_partner = send(late[1], dyh=1)
    from_diagonal = send(late[2], dyh=1, dz=-1)
    step_y, step_z = (freq // 4 + yh) % 2, (freq % 4 - z) % 4
    column_energy = [
        lax.dynamic_slice_in_dim(e, (step_y * 4 + step_z) * classes, classes, 0) for e in (energies, energies_s)
    ]
    column_energy = jnp.where(
        core == 0, jnp.concatenate(column_energy, 1), jnp.concatenate(column_energy[::-1], 1)
    )
    column_labels = lax.dynamic_slice_in_dim(labels, freq * 2 * rows, 2 * rows)
    row_side = jnp.zeros((rows, 2 * rows), jnp.float32)
    column_side = jnp.zeros((rows, 2 * rows), jnp.float32)
    for d in range(classes):
        row_side = jnp.where(column_labels[None, :] == d, energy[d][:, None], row_side)
        column_side = jnp.where(own_labels[:, None] == d, column_energy[d][None, :], column_side)
    root = jnp.sqrt(row_side * column_side + 1e-06)
    from_previous, from_partner, from_diagonal, root = together(from_previous, from_partner, from_diagonal, root)
    pieces = gathered(
        info, early, late, from_previous, third_back, third_ahead, from_partner, fourth, from_diagonal
    )
    found = lax.all_to_all(pieces, "freq", 0, 0, tiled=True).reshape(2 * rows, rows)
    swapped = send(lax.dynamic_slice_in_dim(found, (1 - core) * rows, rows, 0), dc=1)

    same_y = step_y == 0
    inner_z = jnp.logical_or(z == 1, z == 2)
    by_row = jnp.where(
        step_z == 0,
        jnp.logical_or(same_y, yh == 1),
        jnp.where(step_z == 1, False, jnp.where(step_z == 2, jnp.where(same_y, inner_z, lower), True)),
    )
    return finished(jnp.stack([core, by_row.astype(jnp.int32)]), found, swapped, root)


def solution(mesh):
    placed = (P("blk", "freq"), P(), P(None, "freq"), P("freq"), P())
    return jax.shard_map(
        per_device, mesh=mesh, in_specs=placed, out_specs=P("blk", "freq"), check_vma=False
    )
```

```python
import jax
import jax.numpy as jnp
from jax import lax
from jax.experimental import pallas as pl
from jax.experimental.pallas import tpu as pltpu
from jax.sharding import PartitionSpec as P

BOTH = ("blk", "freq")
VMEM_BYTES = 60 * 1024 * 1024
LANES = 128
PARAMS = pltpu.CompilerParams(vmem_limit_bytes=VMEM_BYTES)
COST = pl.CostEstimate(flops=1024, bytes_accessed=1024, transcendentals=0)
VMEM = pl.BlockSpec(memory_space=pltpu.VMEM)
SMEM = pl.BlockSpec(memory_space=pltpu.SMEM)
ANY = pl.BlockSpec(memory_space=pl.ANY)


def places():
    return [
        (yh, z, c, f) for yh in range(2) for z in range(4) for c in range(2) for f in range(8)
    ]


def place_index(yh, z, c, f):
    return (((yh % 2) * 4 + z % 4) * 2 + c % 2) * 8 + f % 8


def route(dyh, dz, dc, dyl):
    return [
        (place_index(yh, z, c, f), place_index(yh + dyh, z + dz, c + dc, f + 4 * dyl))
        for yh, z, c, f in places()
    ]


def send(block, dyh=0, dz=0, dc=0, dyl=0):
    return lax.ppermute(block, BOTH, route(dyh, dz, dc, dyl))


def summed_along_x(tiles):
    groups = [list(range(4)), list(range(4, 8))]
    return summed(lax.all_to_all(tiles, "freq", 0, 0, axis_index_groups=groups, tiled=True))


def sum_kernel(tiles, out):
    total = tiles[0]
    for i in range(1, tiles.shape[0]):
        total = total + tiles[i]
    out[...] = total


def summed(tiles):
    return pl.pallas_call(
        sum_kernel,
        in_specs=[VMEM],
        out_specs=VMEM,
        out_shape=jax.ShapeDtypeStruct(tiles.shape[1:], tiles.dtype),
        compiler_params=PARAMS,
        cost_estimate=COST,
    )(tiles)


def together(*arrays):
    return lax.optimization_barrier(arrays)


def scaled(block, weight):
    return (block.astype(jnp.float32) * weight).astype(jnp.bfloat16)


def gram(a, b):
    return lax.dot_general(a, b, (((1,), (1,)), ((), ())), preferred_element_type=jnp.float32)


CORE, YH, Z, HIGH, NEXT_HIGH, PREV_HIGH, ON_B2, ON_B3, ON_B5, ON_B6 = range(10)


def span(which, half):
    return pl.ds(pl.multiple_of(which * half, LANES), half)


def spread_pairs():
    place = lax.broadcasted_iota(jnp.int32, (LANES, 2 * LANES), 0)
    return (lax.broadcasted_iota(jnp.int32, (LANES, 2 * LANES), 1) // 2 == place).astype(jnp.bfloat16)


def mask_kernel(info, hot, spectra, wedges, own, to_partner, to_next, to_previous, to_partner_b, to_previous_b, pairs):
    half = spectra.shape[1] // 2

    @pl.when(pl.program_id(0) == 0)
    def _():
        spread = spread_pairs()
        for j in range(half // LANES):
            some = wedges[:, pl.ds(j * LANES, LANES)].astype(jnp.float32).astype(jnp.bfloat16)
            wide = jnp.dot(some, spread, preferred_element_type=jnp.float32)
            pairs[:, pl.ds(j * 2 * LANES, 2 * LANES)] = wide.astype(jnp.bfloat16)

    keep = jnp.dot(hot[...], pairs[...], preferred_element_type=jnp.float32).astype(jnp.bfloat16)
    own[...] = spectra[...] * keep
    to_partner[...] = own[:, span(1 - info[YH], half)]
    to_next[...] = own[:, span(info[NEXT_HIGH], half)]
    to_previous[...] = own[:, span(info[PREV_HIGH], half)]
    to_partner_b[...] = own[:, span(info[YH], half)]
    to_previous_b[...] = own[:, span(1 - info[PREV_HIGH], half)]


def masked_blocks(info, hot, spectra, wedges):
    rows, width = spectra.shape
    classes = wedges.shape[0]
    part = rows // 4
    whole = lambda *shape: pl.BlockSpec(shape, lambda i, info: (0, 0))
    slab = lambda n: pl.BlockSpec((part, n), lambda i, info: (i, 0))
    half_block = jax.ShapeDtypeStruct((rows, width // 2), jnp.bfloat16)
    return pl.pallas_call(
        mask_kernel,
        grid_spec=pltpu.PrefetchScalarGridSpec(
            num_scalar_prefetch=1,
            grid=(4,),
            in_specs=[slab(classes), slab(width), whole(classes, width // 2)],
            out_specs=[slab(width)] + [slab(width // 2)] * 5 + [whole(classes, width)],
        ),
        out_shape=[
            jax.ShapeDtypeStruct((rows, width), jnp.bfloat16),
            *[half_block] * 5,
            jax.ShapeDtypeStruct((classes, width), jnp.bfloat16),
        ],
        compiler_params=PARAMS,
        cost_estimate=COST,
    )(info, hot, spectra, wedges)


def weight_kernel(shell_weight, shells, weight):
    spread = spread_pairs()

    def widen(x):
        return jnp.dot(x, spread, preferred_element_type=jnp.float32)

    for j in range(shells.shape[1] // LANES):
        shell = shells[:, pl.ds(j * LANES, LANES)]
        value = jnp.zeros(shell.shape, jnp.float32)
        for k in range(shell_weight.shape[0]):
            value = jnp.where(shell == k, shell_weight[k], value)
        top = value.astype(jnp.bfloat16)
        rest = value - top.astype(jnp.float32)
        middle = rest.astype(jnp.bfloat16)
        low = (rest - middle.astype(jnp.float32)).astype(jnp.bfloat16)
        weight[:, pl.ds(j * 2 * LANES, 2 * LANES)] = (widen(top) + widen(middle)) + widen(low)


def pair_weights(shell_weight, shells):
    return pl.pallas_call(
        weight_kernel,
        in_specs=[SMEM, VMEM],
        out_specs=VMEM,
        out_shape=jax.ShapeDtypeStruct((1, 2 * shells.shape[1]), jnp.float32),
        compiler_params=PARAMS,
        cost_estimate=COST,
    )(shell_weight, shells)


def first_kernel(info, own, sibling, weight, out, own_w, a, a_w, other, tiles, sems, out_sems):
    core = info[CORE]
    got_own = pltpu.make_async_copy(own, a, sems.at[0])
    got_sibling = pltpu.make_async_copy(sibling, other, sems.at[1])
    got_own.start()
    got_sibling.start()

    def leave(k, owner):
        copy = pltpu.make_async_copy(tiles.at[k], out.at[:, owner], out_sems.at[k])
        copy.start()
        return copy

    def put(k, tile):
        tiles[k] = tile.reshape(tiles.shape[1:])

    got_own.wait()
    a_w[...] = scaled(a[...], weight[...])
    left_w = pltpu.make_async_copy(a_w, own_w, out_sems.at[2])
    left_w.start()
    put(0, gram(a_w[...], a[...]))
    left_mine = leave(0, core)
    got_sibling.wait()

    @pl.when(core == 0)
    def _():
        put(1, gram(other[...], a_w[...]))

    @pl.when(core == 1)
    def _():
        put(1, gram(scaled(other[...], weight[...]), a[...]))

    left_other = leave(1, 1 - core)
    left_w.wait()
    left_mine.wait()
    left_other.wait()


def first_tiles(info, own, sibling, weight):
    rows, width = own.shape
    block = pltpu.VMEM((rows, width), jnp.bfloat16)
    return pl.pallas_call(
        first_kernel,
        in_specs=[SMEM, ANY, ANY, VMEM],
        out_specs=[ANY, ANY],
        out_shape=[
            jax.ShapeDtypeStruct((4, 2, rows // 4, rows), jnp.float32),
            jax.ShapeDtypeStruct((rows, width), jnp.bfloat16),
        ],
        scratch_shapes=[
            block,
            block,
            block,
            pltpu.VMEM((2, 4, rows // 4, rows), jnp.float32),
            pltpu.SemaphoreType.DMA((2,)),
            pltpu.SemaphoreType.DMA((3,)),
        ],
        compiler_params=PARAMS,
        cost_estimate=COST,
    )(info, own, sibling, weight)


def half_kernel(k_tile, info, a_yes, a_no, other_yes, other_no, b_yes, b_no, weight, energy, *rest):
    out, a, other, b, b_w, tiles, sems, out_sems = rest[-8:]
    rows, half = a.shape
    core, first, on_b, on_b_other, at = info[0], info[1] == 1, info[2] == 1, info[3] == 1, span(info[4], half)
    w = weight[:, at]

    def pick(n, dst, yes, no):
        for chosen, src in ((first, yes), (jnp.logical_not(first), no)):
            src = src if src.shape[1] == half else src.at[:, at]

            @pl.when(chosen)
            def _(src=src):
                pltpu.make_async_copy(src, dst, sems.at[n]).start()

        return pltpu.make_async_copy(src, dst, sems.at[n])

    got_b = pick(0, b, b_yes, b_no)
    got_a = pick(1, a, a_yes, a_no)
    got_other = pick(2, other, other_yes, other_no)
    slices = tiles.shape[2]
    sent = []
    for x in range(4):
        copy = pltpu.make_async_copy(energy, out.at[x, k_tile, pl.ds(2 * slices, energy.shape[0])], out_sems.at[2 + x])
        copy.start()
        sent.append(copy)
    got_b.wait()
    b_w[...] = scaled(b[...], w)

    def put(k, block, weighted, owner):
        @pl.when(weighted)
        def _():
            tiles[k] = gram(block[...], b_w[...]).reshape(tiles.shape[1:])

        @pl.when(jnp.logical_not(weighted))
        def _():
            tiles[k] = gram(scaled(block[...], w), b[...]).reshape(tiles.shape[1:])

        at = pl.ds(pl.multiple_of(owner * slices, 8), slices)
        copy = pltpu.make_async_copy(tiles.at[k], out.at[:, k_tile, at], out_sems.at[k])
        copy.start()
        sent.append(copy)

    got_a.wait()
    put(0, a, on_b, core)
    got_other.wait()
    put(1, other, on_b_other, 1 - core)
    for copy in sent:
        copy.wait()


def half_tiles(k_tile, info, *operands, into=None):
    rows, classes = operands[0].shape[0], operands[-1].shape[0]
    half = operands[-2].shape[1] // 2
    block = pltpu.VMEM((rows, half), jnp.bfloat16)
    specs, aliases = [SMEM] + [ANY] * 6 + [VMEM] * 2, {}
    if into is not None:
        aliases = {len(specs): 0}
        specs, operands = specs + [ANY], operands + (into,)

    def kernel(*refs):
        half_kernel(k_tile, *refs)

    return pl.pallas_call(
        kernel,
        in_specs=specs,
        out_specs=ANY,
        out_shape=jax.ShapeDtypeStruct((4, 2, rows // 2 + classes, rows), jnp.float32),
        scratch_shapes=[
            block,
            block,
            block,
            block,
            pltpu.VMEM((2, 4, rows // 4, rows), jnp.float32),
            pltpu.SemaphoreType.DMA((3,)),
            pltpu.SemaphoreType.DMA((6,)),
        ],
        input_output_aliases=aliases,
        compiler_params=PARAMS,
        cost_estimate=COST,
    )(info, *operands)


def late_kernel(
    is_mine, info, own, own_w, partner_a, partner_b, a_high, a_low, mine_high, mine_low, diagonal, a_diagonal,
    weight, *rest,
):
    out, a, a_w, own_b, partner, sixth_a, sixth_b, tiles, sems, out_sems = rest[-10:]
    half = partner_a.shape[1]
    slices = out.shape[2]
    lower = info[YH] == 0
    high_is_yh = info[HIGH] == info[YH]
    high, yh = info[HIGH], info[YH]

    def pick(n, dst, *choices):
        for chosen, src in choices:

            @pl.when(chosen)
            def _(src=src):
                pltpu.make_async_copy(src, dst, sems.at[n]).start()

        return pltpu.make_async_copy(choices[0][1], dst, sems.at[n])

    always = info[CORE] >= 0
    no = jnp.logical_not
    got_high = pick(0, a.at[:, span(high, half)], (always, a_high))
    got_low = pick(1, a.at[:, span(1 - high, half)], (always, a_low))
    got_own = pick(2, own_b, (info[ON_B2] == 1, own_w), (info[ON_B2] == 0, own))
    got_near = pick(3, partner.at[:, span(yh, half)], (always, partner_a))
    got_far = pick(4, partner.at[:, span(1 - yh, half)], (always, partner_b))
    got_a = pick(
        5,
        sixth_a,
        (no(lower), a_diagonal),
        (jnp.logical_and(lower, high_is_yh), a_high),
        (jnp.logical_and(lower, no(high_is_yh)), a_low),
    )
    got_b = pick(
        6,
        sixth_b,
        (lower, diagonal),
        (jnp.logical_and(no(lower), high_is_yh), mine_high),
        (jnp.logical_and(no(lower), no(high_is_yh)), mine_low),
    )
    owner = info[CORE] if is_mine else 1 - info[CORE]
    sent = []

    def put(k, tile):
        tiles[k] = tile.reshape(4, slices, tile.shape[1])

    def leave(k):
        copy = pltpu.make_async_copy(tiles.at[k], out.at[pl.ds(owner * 4, 4), k], out_sems.at[k])
        copy.start()
        sent.append(copy)

    got_high.wait()
    got_low.wait()
    a_w[...] = scaled(a[...], weight[...])
    got_own.wait()

    @pl.when(info[ON_B2] == 1)
    def _():
        put(0, gram(a[...], own_b[...]))

    @pl.when(info[ON_B2] == 0)
    def _():
        put(0, gram(a_w[...], own_b[...]))

    leave(0)
    got_near.wait()
    got_far.wait()

    @pl.when(info[ON_B5] == 1)
    def _():
        partner[...] = scaled(partner[...], weight[...])
        put(1, gram(a[...], partner[...]))

    @pl.when(info[ON_B5] == 0)
    def _():
        put(1, gram(a_w[...], partner[...]))

    leave(1)
    got_a.wait()
    got_b.wait()
    w_yh = weight[:, span(yh, half)]

    @pl.when(info[ON_B6] == 1)
    def _():
        sixth_b[...] = scaled(sixth_b[...], w_yh)

    @pl.when(info[ON_B6] == 0)
    def _():
        sixth_a[...] = scaled(sixth_a[...], w_yh)

    put(2, gram(sixth_a[...], sixth_b[...]))
    leave(2)
    for copy in sent:
        copy.wait()


def late_tiles(is_mine, info, own, own_w, partner_a, partner_b, a_high, a_low, mine_high, mine_low, diagonal,
               a_diagonal, weight, other=None):
    rows, width = own.shape
    half = width // 2
    arrays = [own, own_w, partner_a, partner_b, a_high, a_low, mine_high, mine_low, diagonal, a_diagonal, weight]
    specs = [SMEM] + [ANY] * 10 + [VMEM]
    aliases = {}
    if other is not None:
        arrays.append(other)
        specs.append(ANY)
        aliases = {len(specs) - 1: 0}
    block = lambda n: pltpu.VMEM((rows, n), jnp.bfloat16)

    def kernel(*refs):
        late_kernel(is_mine, *refs)

    return pl.pallas_call(
        kernel,
        in_specs=specs,
        out_specs=ANY,
        out_shape=jax.ShapeDtypeStruct((8, 3, rows // 4, rows), jnp.float32),
        scratch_shapes=[
            block(width),
            block(width),
            block(width),
            block(width),
            block(half),
            block(half),
            pltpu.VMEM((3, 4, rows // 4, rows), jnp.float32),
            pltpu.SemaphoreType.DMA((7,)),
            pltpu.SemaphoreType.DMA((3,)),
        ],
        input_output_aliases=aliases,
        compiler_params=PARAMS,
        cost_estimate=COST,
    )(info, *arrays)


def gather_kernel(info, early, late, from_previous, third_back, third_ahead, from_partner, fourth, from_diagonal, out):
    yh, z = info[YH], info[Z]

    def put(dyh, dz, value):
        out[(yh + dyh) % 2 * 4 + (z + dz) % 4] = value

    slices = out.shape[1]
    put(0, 0, early[:slices])
    put(0, 1, late[0])
    put(0, 2, third_back[...] + third_ahead[...])
    put(0, 3, from_previous[0])
    put(1, 0, early[2 * slices : 3 * slices] + fourth[...])
    put(1, 1, from_partner[...])
    put(1, 2, from_previous[2] + from_diagonal[...])
    put(1, 3, from_previous[1])


def gathered(info, *parts):
    slices, rows = parts[1].shape[1:]
    return pl.pallas_call(
        gather_kernel,
        in_specs=[SMEM] + [VMEM] * len(parts),
        out_specs=VMEM,
        out_shape=jax.ShapeDtypeStruct((8, slices, rows), jnp.float32),
    )(info, *parts)


def final_kernel(info, found, swapped, root, out):
    rows = swapped.shape[0]
    core, by_row = info[0], info[1]

    for is_first in (True, False):

        @pl.when(jnp.logical_and(by_row == 1, (core == 0) == is_first))
        def _(is_first=is_first):
            kept = found[:rows] if is_first else found[rows:]
            pair = (kept, swapped[...]) if is_first else (swapped[...], kept)
            out[...] = jnp.concatenate(pair, 1) / root[...]

    @pl.when(by_row == 0)
    def _():
        out[...] = found[...].T / root[...]


def finished(info, found, swapped, root):
    return pl.pallas_call(
        final_kernel,
        in_specs=[SMEM, VMEM, VMEM, VMEM],
        out_specs=VMEM,
        out_shape=jax.ShapeDtypeStruct(root.shape, jnp.float32),
    )(info, found, swapped, root)


def per_device(spectra, labels, wedges, shells, shell_weight):
    rows, width = spectra.shape
    half, slices = width // 2, rows // 4
    classes = wedges.shape[0]
    blk = lax.axis_index("blk")
    core, z, yh = blk % 2, (blk // 2) % 4, blk // 8
    freq = lax.axis_index("freq")

    def place(dyh, dz):
        return ((yh + dyh) % 2) * 4 + (z + dz) % 4

    def ahead(a, b):
        return ((a - b) % 8 < 4).astype(jnp.int32)

    def columns(block, which):
        return lax.dynamic_slice_in_dim(block, which * half, half, 1)

    low, lower = z < 2, yh == 0
    high = z // 2
    previous_high = ((z + 3) % 4) // 2
    info = jnp.stack(
        [
            core,
            yh,
            z,
            high,
            ((z + 1) % 4) // 2,
            previous_high,
            ahead(place(0, 1), place(0, 0)),
            jnp.where(low, ahead(place(0, 1), place(0, -1)), ahead(place(0, -1), place(0, 1))),
            ahead(place(0, 1), place(1, 0)),
            jnp.where(lower, ahead(place(0, 1), place(1, -1)), ahead(place(1, -1), place(0, 1))),
        ]
    ).astype(jnp.int32)

    class_range = jnp.arange(classes, dtype=jnp.int32)
    own_labels = lax.dynamic_slice_in_dim(labels, blk * rows, rows)
    hot = (own_labels[:, None] == class_range[None, :]).astype(jnp.bfloat16)
    own, to_partner, to_next, to_previous, to_partner_b, to_previous_b, pairs = masked_blocks(info, hot, spectra, wedges)

    following_a = send(to_previous, dz=-1)
    partner_a = send(to_partner, dyh=1)
    previous = send(to_next, dz=1)
    following_b = send(to_previous_b, dz=-1)
    sibling = send(own, dc=1)
    own, shells = together(own, shells)
    weight = pair_weights(shell_weight, shells[None, :])
    q1, own_w = first_tiles(info, own, sibling, weight)
    p1 = summed_along_x(q1)
    own_e, q1 = together(own, q1)
    squares = own_e.astype(jnp.float32) ** 2 * weight
    partial_energy = lax.dot_general(
        pairs.astype(jnp.float32), squares, (((1,), (1,)), ((), ())), precision=lax.Precision.HIGHEST
    )
    partner_b = send(to_partner_b, dyh=1)
    partner_a, p1, partial_energy = together(partner_a, p1, partial_energy)
    diagonal = send(partner_a, dz=1)
    partner_s = send(partner_a, dc=1)
    third_a_s = send(jnp.where(low, following_a, previous), dc=1)
    fourth_info = jnp.stack([core, 1 - yh, 1, core, yh]).astype(jnp.int32)
    third_info = jnp.stack([core, low.astype(jnp.int32), info[ON_B3], info[ON_B3], high]).astype(jnp.int32)
    half_pair = half_tiles(
        1, fourth_info, partner_a, own, partner_s, sibling, own, partner_a, weight, partial_energy
    )
    half_pair = half_tiles(
        0, third_info, following_a, previous, third_a_s, third_a_s, previous, following_a, weight, partial_energy,
        into=half_pair,
    )
    half_pair = summed_along_x(half_pair)
    following_b, partner_b, diagonal, half_pair = together(following_b, partner_b, diagonal, half_pair)

    own_yl = freq // 4

    def halves(which):
        return [
            lax.dynamic_index_in_dim(p1, which, 0, keepdims=False),
            lax.dynamic_slice_in_dim(half_pair[0], which * slices, slices, 0),
            lax.dynamic_slice_in_dim(half_pair[1], which * slices, slices, 0),
            half_pair[1, 2 * slices :],
        ]

    early = send(jnp.concatenate(halves(1 - own_yl)), dyl=1)

    following_as = send(following_a, dc=1)
    following_bs = send(following_b, dc=1)
    diagonal_s = send(diagonal, dc=1)
    late = late_tiles(
        True, info, own, own_w, partner_a, partner_b, following_a, following_b, following_a, following_b,
        diagonal, diagonal, weight,
    )
    late, following_as, following_bs, diagonal_s, early = together(
        late, following_as, following_bs, diagonal_s, early
    )
    early = jnp.concatenate(halves(own_yl)) + early
    third, energy = early[slices : 2 * slices], early[3 * slices :]
    third_back, third_ahead = send(third, dz=1), send(third, dz=-1)
    from_other = send(early[2 * slices :], dyh=1)
    late = late_tiles(
        False, info, own, own_w, partner_a, partner_b, following_as, following_bs, following_a, following_b,
        diagonal, diagonal_s, weight, late,
    )
    late, third_back, third_ahead, from_other = together(late, third_back, third_ahead, from_other)
    late = lax.all_to_all(late, "freq", 0, 0, tiled=True)
    fourth, pair = from_other[:slices], jnp.concatenate([energy, from_other[slices:]])
    energies = jnp.concatenate([pair, send(pair, dz=-1), send(pair, dz=2), send(pair, dz=1)])
    energies_s = send(energies, dc=1)
    late = summed(late)

    from_previous = send(late, dz=1)
    from_partner = send(late[1], dyh=1)
    from_diagonal = send(late[2], dyh=1, dz=-1)
    step_y, step_z = (freq // 4 + yh) % 2, (freq % 4 - z) % 4
    column_energy = [
        lax.dynamic_slice_in_dim(e, (step_z * 2 + step_y) * classes, classes, 0) for e in (energies, energies_s)
    ]
    column_energy = jnp.where(
        core == 0, jnp.concatenate(column_energy, 1), jnp.concatenate(column_energy[::-1], 1)
    )
    column_labels = lax.dynamic_slice_in_dim(labels, freq * 2 * rows, 2 * rows)
    row_side = jnp.zeros((rows, 2 * rows), jnp.float32)
    column_side = jnp.zeros((rows, 2 * rows), jnp.float32)
    for d in range(classes):
        row_side = jnp.where(column_labels[None, :] == d, energy[d][:, None], row_side)
        column_side = jnp.where(own_labels[:, None] == d, column_energy[d][None, :], column_side)
    root = jnp.sqrt(row_side * column_side + 1e-06)
    from_previous, from_partner, from_diagonal, root = together(from_previous, from_partner, from_diagonal, root)
    pieces = gathered(
        info, early, late, from_previous, third_back, third_ahead, from_partner, fourth, from_diagonal
    )
    found = lax.all_to_all(pieces, "freq", 0, 0, tiled=True).reshape(2 * rows, rows)
    swapped = send(lax.dynamic_slice_in_dim(found, (1 - core) * rows, rows, 0), dc=1)

    same_y = step_y == 0
    inner_z = jnp.logical_or(z == 1, z == 2)
    by_row = jnp.where(
        step_z == 0,
        jnp.logical_or(same_y, yh == 1),
        jnp.where(step_z == 1, False, jnp.where(step_z == 2, jnp.where(same_y, inner_z, lower), True)),
    )
    return finished(jnp.stack([core, by_row.astype(jnp.int32)]), found, swapped, root)


def solution(mesh):
    placed = (P("blk", "freq"), P(), P(None, "freq"), P("freq"), P())
    return jax.shard_map(
        per_device, mesh=mesh, in_specs=placed, out_specs=P("blk", "freq"), check_vma=False
    )
```

```python
import jax
import jax.numpy as jnp
from jax import lax
from jax.experimental import pallas as pl
from jax.experimental.pallas import tpu as pltpu
from jax.sharding import PartitionSpec as P

BOTH = ("blk", "freq")
VMEM_BYTES = 60 * 1024 * 1024
LANES = 128
PARAMS = pltpu.CompilerParams(vmem_limit_bytes=VMEM_BYTES)
COST = pl.CostEstimate(flops=1024, bytes_accessed=1024, transcendentals=0)
VMEM = pl.BlockSpec(memory_space=pltpu.VMEM)
SMEM = pl.BlockSpec(memory_space=pltpu.SMEM)
ANY = pl.BlockSpec(memory_space=pl.ANY)


def places():
    return [
        (yh, z, c, f) for yh in range(2) for z in range(4) for c in range(2) for f in range(8)
    ]


def place_index(yh, z, c, f):
    return (((yh % 2) * 4 + z % 4) * 2 + c % 2) * 8 + f % 8


def route(dyh, dz, dc, dyl):
    return [
        (place_index(yh, z, c, f), place_index(yh + dyh, z + dz, c + dc, f + 4 * dyl))
        for yh, z, c, f in places()
    ]


def send(block, dyh=0, dz=0, dc=0, dyl=0):
    return lax.ppermute(block, BOTH, route(dyh, dz, dc, dyl))


def summed_along_x(tiles):
    groups = [list(range(4)), list(range(4, 8))]
    return jnp.sum(lax.all_to_all(tiles, "freq", 0, 0, axis_index_groups=groups, tiled=True), 0)


def together(*arrays):
    return lax.optimization_barrier(arrays)


def scaled(block, weight):
    return (block.astype(jnp.float32) * weight).astype(jnp.bfloat16)


def gram(a, b):
    return lax.dot_general(a, b, (((1,), (1,)), ((), ())), preferred_element_type=jnp.float32)


CORE, YH, Z, HIGH, NEXT_HIGH, PREV_HIGH, ON_B2, ON_B3, ON_B5, ON_B6, LOWER, LOW, ONE, BY_ROW = range(14)


def span(which, half):
    return pl.ds(pl.multiple_of(which * half, LANES), half)


def spread_pairs():
    place = lax.broadcasted_iota(jnp.int32, (LANES, 2 * LANES), 0)
    return (lax.broadcasted_iota(jnp.int32, (LANES, 2 * LANES), 1) // 2 == place).astype(jnp.bfloat16)


def mask_kernel(info, hot, spectra, wedges, own, to_partner, to_next, to_previous, to_partner_b, to_previous_b, pairs):
    half = spectra.shape[1] // 2

    @pl.when(pl.program_id(0) == 0)
    def _():
        spread = spread_pairs()
        for j in range(half // LANES):
            some = wedges[:, pl.ds(j * LANES, LANES)].astype(jnp.float32).astype(jnp.bfloat16)
            wide = jnp.dot(some, spread, preferred_element_type=jnp.float32)
            pairs[:, pl.ds(j * 2 * LANES, 2 * LANES)] = wide.astype(jnp.bfloat16)

    keep = jnp.dot(hot[...], pairs[...], preferred_element_type=jnp.float32).astype(jnp.bfloat16)
    own[...] = spectra[...] * keep
    to_partner[...] = own[:, span(1 - info[YH], half)]
    to_next[...] = own[:, span(info[NEXT_HIGH], half)]
    to_previous[...] = own[:, span(info[PREV_HIGH], half)]
    to_partner_b[...] = own[:, span(info[YH], half)]
    to_previous_b[...] = own[:, span(1 - info[PREV_HIGH], half)]


def masked_blocks(info, hot, spectra, wedges):
    rows, width = spectra.shape
    classes = wedges.shape[0]
    part = rows // 4
    whole = lambda *shape: pl.BlockSpec(shape, lambda i, info: (0, 0))
    slab = lambda n: pl.BlockSpec((part, n), lambda i, info: (i, 0))
    half_block = jax.ShapeDtypeStruct((rows, width // 2), jnp.bfloat16)
    return pl.pallas_call(
        mask_kernel,
        grid_spec=pltpu.PrefetchScalarGridSpec(
            num_scalar_prefetch=1,
            grid=(4,),
            in_specs=[slab(classes), slab(width), whole(classes, width // 2)],
            out_specs=[slab(width)] + [slab(width // 2)] * 5 + [whole(classes, width)],
        ),
        out_shape=[
            jax.ShapeDtypeStruct((rows, width), jnp.bfloat16),
            *[half_block] * 5,
            jax.ShapeDtypeStruct((classes, width), jnp.bfloat16),
        ],
        compiler_params=PARAMS,
        cost_estimate=COST,
    )(info, hot, spectra, wedges)


def weight_kernel(shell_weight, shells, weight):
    spread = spread_pairs()

    def widen(x):
        return jnp.dot(x, spread, preferred_element_type=jnp.float32)

    for j in range(shells.shape[1] // LANES):
        shell = shells[:, pl.ds(j * LANES, LANES)]
        value = jnp.zeros(shell.shape, jnp.float32)
        for k in range(shell_weight.shape[0]):
            value = jnp.where(shell == k, shell_weight[k], value)
        top = value.astype(jnp.bfloat16)
        rest = value - top.astype(jnp.float32)
        middle = rest.astype(jnp.bfloat16)
        low = (rest - middle.astype(jnp.float32)).astype(jnp.bfloat16)
        weight[:, pl.ds(j * 2 * LANES, 2 * LANES)] = (widen(top) + widen(middle)) + widen(low)


def pair_weights(shell_weight, shells):
    return pl.pallas_call(
        weight_kernel,
        in_specs=[SMEM, VMEM],
        out_specs=VMEM,
        out_shape=jax.ShapeDtypeStruct((1, 2 * shells.shape[1]), jnp.float32),
        compiler_params=PARAMS,
        cost_estimate=COST,
    )(shell_weight, shells)


def first_kernel(info, own, sibling, weight, out, own_w, a, other, tiles, sems, out_sems):
    core = info[CORE]
    got_own = pltpu.make_async_copy(own, a.at[0], sems.at[0])
    got_sibling = pltpu.make_async_copy(sibling, other.at[0], sems.at[1])
    got_own.start()
    got_sibling.start()

    def leave(k, owner):
        copy = pltpu.make_async_copy(tiles.at[k], out.at[:, owner], out_sems.at[k])
        copy.start()
        return copy

    def put(k, tile):
        tiles[k] = tile.reshape(tiles.shape[1:])

    got_own.wait()
    a[1] = scaled(a[0], weight[...])
    left_w = pltpu.make_async_copy(a.at[1], own_w, out_sems.at[2])
    left_w.start()
    put(0, gram(a[1], a[0]))
    left_mine = leave(0, core)
    got_sibling.wait()

    @pl.when(core == 1)
    def _():
        other[1] = scaled(other[0], weight[...])

    put(1, gram(other[core], a[1 - core]))
    left_other = leave(1, 1 - core)
    left_w.wait()
    left_mine.wait()
    left_other.wait()


def first_tiles(info, own, sibling, weight):
    rows, width = own.shape
    block = pltpu.VMEM((2, rows, width), jnp.bfloat16)
    return pl.pallas_call(
        first_kernel,
        in_specs=[SMEM, ANY, ANY, VMEM],
        out_specs=[ANY, ANY],
        out_shape=[
            jax.ShapeDtypeStruct((4, 2, rows // 4, rows), jnp.float32),
            jax.ShapeDtypeStruct((rows, width), jnp.bfloat16),
        ],
        scratch_shapes=[
            block,
            block,
            pltpu.VMEM((2, 4, rows // 4, rows), jnp.float32),
            pltpu.SemaphoreType.DMA((2,)),
            pltpu.SemaphoreType.DMA((3,)),
        ],
        compiler_params=PARAMS,
        cost_estimate=COST,
    )(info, own, sibling, weight)


def half_kernel(
    k_tile, first_at, on_b_at, on_b_other_at, half_at, info, a_yes, a_no, other_yes, other_no, b_yes, b_no,
    weight, energy, *rest,
):
    out, a, b, tiles, sems, out_sems = rest[-6:]
    rows, half = b.shape[1:]
    slices = tiles.shape[2]
    core, first, at = info[CORE], info[first_at] == 1, span(info[half_at], half)
    w = weight[:, at]

    def pick(n, dst, yes, no):
        for chosen, src in ((first, yes), (jnp.logical_not(first), no)):
            src = src if src.shape[1] == half else src.at[:, at]

            @pl.when(chosen)
            def _(src=src):
                pltpu.make_async_copy(src, dst, sems.at[n]).start()

        return pltpu.make_async_copy(src, dst, sems.at[n])

    got_b = pick(0, b.at[0], b_yes, b_no)
    got_a = [pick(1, a.at[0], a_yes, a_no), pick(2, a.at[2], other_yes, other_no)]
    sent = []

    def go(src, dst, n):
        copy = pltpu.make_async_copy(src, dst, out_sems.at[n])
        copy.start()
        sent.append(copy)

    for x in range(4):
        go(energy, out.at[x, k_tile, pl.ds(2 * slices, energy.shape[0])], 2 + x)
    got_b.wait()
    b[1] = scaled(b[0], w)
    for k, (on_b, owner) in enumerate(((info[on_b_at], core), (info[on_b_other_at], 1 - core))):
        got_a[k].wait()

        @pl.when(on_b == 0)
        def _(k=k):
            a[2 * k + 1] = scaled(a[2 * k], w)

        tiles[k] = gram(a[2 * k + 1 - on_b], b[on_b]).reshape(tiles.shape[1:])
        go(tiles.at[k], out.at[:, k_tile, pl.ds(pl.multiple_of(owner * slices, 8), slices)], k)
    for copy in sent:
        copy.wait()


def half_tiles(places_of, info, *operands, into=None):
    rows, classes = operands[0].shape[0], operands[-1].shape[0]
    half = operands[-2].shape[1] // 2
    specs, aliases = [SMEM] + [ANY] * 6 + [VMEM] * 2, {}
    if into is not None:
        aliases = {len(specs): 0}
        specs, operands = specs + [ANY], operands + (into,)

    def kernel(*refs):
        half_kernel(*places_of, *refs)

    return pl.pallas_call(
        kernel,
        in_specs=specs,
        out_specs=ANY,
        out_shape=jax.ShapeDtypeStruct((4, 2, rows // 2 + classes, rows), jnp.float32),
        scratch_shapes=[
            pltpu.VMEM((4, rows, half), jnp.bfloat16),
            pltpu.VMEM((2, rows, half), jnp.bfloat16),
            pltpu.VMEM((2, 4, rows // 4, rows), jnp.float32),
            pltpu.SemaphoreType.DMA((3,)),
            pltpu.SemaphoreType.DMA((6,)),
        ],
        input_output_aliases=aliases,
        compiler_params=PARAMS,
        cost_estimate=COST,
    )(info, *operands)


def late_kernel(
    is_mine, info, own, own_w, partner_a, partner_b, a_high, a_low, mine_high, mine_low, diagonal, a_diagonal,
    weight, *rest,
):
    out, a, own_b, partner, sixth_a, sixth_b, tiles, sems, out_sems = rest[-9:]
    half = partner_a.shape[1]
    slices = out.shape[2]
    lower = info[YH] == 0
    high_is_yh = info[HIGH] == info[YH]
    high, yh = info[HIGH], info[YH]

    def pick(n, dst, *choices):
        for chosen, src in choices:

            @pl.when(chosen)
            def _(src=src):
                pltpu.make_async_copy(src, dst, sems.at[n]).start()

        return pltpu.make_async_copy(choices[0][1], dst, sems.at[n])

    always = info[CORE] >= 0
    no = jnp.logical_not
    got_high = pick(0, a.at[0, :, span(high, half)], (always, a_high))
    got_low = pick(1, a.at[0, :, span(1 - high, half)], (always, a_low))
    got_own = pick(2, own_b, (info[ON_B2] == 1, own_w), (info[ON_B2] == 0, own))
    got_near = pick(3, partner.at[:, span(yh, half)], (always, partner_a))
    got_far = pick(4, partner.at[:, span(1 - yh, half)], (always, partner_b))
    got_a = pick(
        5,
        sixth_a,
        (no(lower), a_diagonal),
        (jnp.logical_and(lower, high_is_yh), a_high),
        (jnp.logical_and(lower, no(high_is_yh)), a_low),
    )
    got_b = pick(
        6,
        sixth_b,
        (lower, diagonal),
        (jnp.logical_and(no(lower), high_is_yh), mine_high),
        (jnp.logical_and(no(lower), no(high_is_yh)), mine_low),
    )
    owner = info[CORE] if is_mine else 1 - info[CORE]
    sent = []

    def put(k, tile):
        tiles[k] = tile.reshape(4, slices, tile.shape[1])

    def leave(k):
        copy = pltpu.make_async_copy(tiles.at[k], out.at[pl.ds(owner * 4, 4), k], out_sems.at[k])
        copy.start()
        sent.append(copy)

    got_high.wait()
    got_low.wait()
    a[1] = scaled(a[0], weight[...])
    got_own.wait()
    put(0, gram(a[1 - info[ON_B2]], own_b[...]))
    leave(0)
    got_near.wait()
    got_far.wait()

    @pl.when(info[ON_B5] == 1)
    def _():
        partner[...] = scaled(partner[...], weight[...])

    put(1, gram(a[1 - info[ON_B5]], partner[...]))
    leave(1)
    got_a.wait()
    got_b.wait()
    w_yh = weight[:, span(yh, half)]

    @pl.when(info[ON_B6] == 1)
    def _():
        sixth_b[...] = scaled(sixth_b[...], w_yh)

    @pl.when(info[ON_B6] == 0)
    def _():
        sixth_a[...] = scaled(sixth_a[...], w_yh)

    put(2, gram(sixth_a[...], sixth_b[...]))
    leave(2)
    for copy in sent:
        copy.wait()


def late_tiles(is_mine, info, own, own_w, partner_a, partner_b, a_high, a_low, mine_high, mine_low, diagonal,
               a_diagonal, weight, other=None):
    rows, width = own.shape
    half = width // 2
    arrays = [own, own_w, partner_a, partner_b, a_high, a_low, mine_high, mine_low, diagonal, a_diagonal, weight]
    specs = [SMEM] + [ANY] * 10 + [VMEM]
    aliases = {}
    if other is not None:
        arrays.append(other)
        specs.append(ANY)
        aliases = {len(specs) - 1: 0}
    block = lambda n: pltpu.VMEM((rows, n), jnp.bfloat16)

    def kernel(*refs):
        late_kernel(is_mine, *refs)

    return pl.pallas_call(
        kernel,
        in_specs=specs,
        out_specs=ANY,
        out_shape=jax.ShapeDtypeStruct((8, 3, rows // 4, rows), jnp.float32),
        scratch_shapes=[
            pltpu.VMEM((2, rows, width), jnp.bfloat16),
            block(width),
            block(width),
            block(half),
            block(half),
            pltpu.VMEM((3, 4, rows // 4, rows), jnp.float32),
            pltpu.SemaphoreType.DMA((7,)),
            pltpu.SemaphoreType.DMA((3,)),
        ],
        input_output_aliases=aliases,
        compiler_params=PARAMS,
        cost_estimate=COST,
    )(info, *arrays)


def gather_kernel(info, early, late, from_previous, third_back, third_ahead, from_other, from_diagonal, out):
    yh, z = info[YH], info[Z]

    def put(dyh, dz, value):
        out[(yh + dyh) % 2 * 4 + (z + dz) % 4] = value

    slices = out.shape[1]
    put(0, 0, early[:slices])
    put(0, 1, late[0])
    put(0, 2, third_back[...] + third_ahead[...])
    put(0, 3, from_previous[0])
    put(1, 0, early[2 * slices : 3 * slices] + from_other[slices : 2 * slices])
    put(1, 1, from_other[:slices])
    put(1, 2, from_previous[2] + from_diagonal[...])
    put(1, 3, from_previous[1])


def gathered(info, *parts):
    slices, rows = parts[1].shape[1:]
    return pl.pallas_call(
        gather_kernel,
        in_specs=[SMEM] + [VMEM] * len(parts),
        out_specs=VMEM,
        out_shape=jax.ShapeDtypeStruct((8, slices, rows), jnp.float32),
    )(info, *parts)


def final_kernel(info, found, swapped, root, out):
    rows = swapped.shape[0]
    core, by_row = info[CORE], info[BY_ROW]

    for is_first in (True, False):

        @pl.when(jnp.logical_and(by_row == 1, (core == 0) == is_first))
        def _(is_first=is_first):
            kept = found[:rows] if is_first else found[rows:]
            pair = (kept, swapped[...]) if is_first else (swapped[...], kept)
            out[...] = jnp.concatenate(pair, 1) / root[...]

    @pl.when(by_row == 0)
    def _():
        out[...] = found[...].T / root[...]


def finished(info, found, swapped, root):
    return pl.pallas_call(
        final_kernel,
        in_specs=[SMEM, VMEM, VMEM, VMEM],
        out_specs=VMEM,
        out_shape=jax.ShapeDtypeStruct(root.shape, jnp.float32),
    )(info, found, swapped, root)


def per_device(spectra, labels, wedges, shells, shell_weight):
    rows, width = spectra.shape
    half, slices = width // 2, rows // 4
    classes = wedges.shape[0]
    blk = lax.axis_index("blk")
    core, z, yh = blk % 2, (blk // 2) % 4, blk // 8
    freq = lax.axis_index("freq")

    def place(dyh, dz):
        return ((yh + dyh) % 2) * 4 + (z + dz) % 4

    def ahead(a, b):
        return ((a - b) % 8 < 4).astype(jnp.int32)

    def columns(block, which):
        return lax.dynamic_slice_in_dim(block, which * half, half, 1)

    low, lower = z < 2, yh == 0
    high = z // 2
    previous_high = ((z + 3) % 4) // 2
    step_y, step_z = (freq // 4 + yh) % 2, (freq % 4 - z) % 4
    same_y = step_y == 0
    inner_z = jnp.logical_or(z == 1, z == 2)
    by_row = jnp.where(
        step_z == 0,
        jnp.logical_or(same_y, yh == 1),
        jnp.where(step_z == 1, False, jnp.where(step_z == 2, jnp.where(same_y, inner_z, lower), True)),
    )
    info = jnp.stack(
        [
            core,
            yh,
            z,
            high,
            ((z + 1) % 4) // 2,
            previous_high,
            ahead(place(0, 1), place(0, 0)),
            jnp.where(low, ahead(place(0, 1), place(0, -1)), ahead(place(0, -1), place(0, 1))),
            ahead(place(0, 1), place(1, 0)),
            jnp.where(lower, ahead(place(0, 1), place(1, -1)), ahead(place(1, -1), place(0, 1))),
            lower.astype(jnp.int32),
            low.astype(jnp.int32),
            jnp.int32(1),
            by_row.astype(jnp.int32),
        ]
    ).astype(jnp.int32)

    class_range = jnp.arange(classes, dtype=jnp.int32)
    own_labels = lax.dynamic_slice_in_dim(labels, blk * rows, rows)
    hot = (own_labels[:, None] == class_range[None, :]).astype(jnp.bfloat16)
    own, to_partner, to_next, to_previous, to_partner_b, to_previous_b, pairs = masked_blocks(info, hot, spectra, wedges)

    following_a = send(to_previous, dz=-1)
    partner_a = send(to_partner, dyh=1)
    previous = send(to_next, dz=1)
    following_b = send(to_previous_b, dz=-1)
    sibling = send(own, dc=1)
    own, shells = together(own, shells)
    weight = pair_weights(shell_weight, shells[None, :])
    q1, own_w = first_tiles(info, own, sibling, weight)
    p1 = summed_along_x(q1)
    own_e, q1 = together(own, q1)
    squares = own_e.astype(jnp.float32) ** 2 * weight
    partial_energy = lax.dot_general(
        pairs.astype(jnp.float32), squares, (((1,), (1,)), ((), ())), precision=lax.Precision.HIGHEST
    )
    partner_b = send(to_partner_b, dyh=1)
    partner_a, p1, partial_energy = together(partner_a, p1, partial_energy)
    diagonal = send(partner_a, dz=1)
    partner_s = send(partner_a, dc=1)
    third_a_s = send(jnp.where(low, following_a, previous), dc=1)
    half_pair = half_tiles(
        (1, LOWER, ONE, CORE, YH), info, partner_a, own, partner_s, sibling, own, partner_a, weight, partial_energy
    )
    half_pair = half_tiles(
        (0, LOW, ON_B3, ON_B3, HIGH), info, following_a, previous, third_a_s, third_a_s, previous, following_a, weight,
        partial_energy, into=half_pair,
    )
    half_pair = summed_along_x(half_pair)
    following_b, partner_b, diagonal, half_pair = together(following_b, partner_b, diagonal, half_pair)

    following_as = send(following_a, dc=1)
    following_bs = send(following_b, dc=1)
    diagonal_s = send(diagonal, dc=1)
    late = late_tiles(
        True, info, own, own_w, partner_a, partner_b, following_a, following_b, following_a, following_b,
        diagonal, diagonal, weight,
    )
    late, following_as, following_bs, diagonal_s = together(late, following_as, following_bs, diagonal_s)
    late = late_tiles(
        False, info, own, own_w, partner_a, partner_b, following_as, following_bs, following_a, following_b,
        diagonal, diagonal_s, weight, late,
    )
    late, p1, half_pair = together(late, p1, half_pair)
    late = lax.all_to_all(late, "freq", 0, 0, tiled=True)

    own_yl = freq // 4

    def halves(which):
        return [
            lax.dynamic_index_in_dim(p1, which, 0, keepdims=False),
            lax.dynamic_slice_in_dim(half_pair[0], which * slices, slices, 0),
            lax.dynamic_slice_in_dim(half_pair[1], which * slices, slices, 0),
            half_pair[1, 2 * slices :],
        ]

    early = jnp.concatenate(halves(own_yl)) + send(jnp.concatenate(halves(1 - own_yl)), dyl=1)
    third, energy = early[slices : 2 * slices], early[3 * slices :]
    third_energy = jnp.concatenate([third, energy])
    back, forth, opposite = send(third_energy, dz=1), send(third_energy, dz=-1), send(energy, dz=2)
    late, back, forth, opposite = together(late, back, forth, opposite)
    third_back, third_ahead = back[:slices], forth[:slices]
    plane = jnp.concatenate([energy, forth[slices:], opposite, back[slices:]])
    late = jnp.sum(late, 0)

    from_previous = send(late, dz=1)
    from_other = send(jnp.concatenate([late[1], early[2 * slices : 3 * slices], plane]), dyh=1)
    from_diagonal = send(late[2], dyh=1, dz=-1)
    from_previous, from_other, from_diagonal = together(from_previous, from_other, from_diagonal)
    pieces = gathered(info, early, late, from_previous, third_back, third_ahead, from_other, from_diagonal)
    found = lax.all_to_all(pieces, "freq", 0, 0, tiled=True).reshape(2 * rows, rows)
    swapped = send(lax.dynamic_slice_in_dim(found, (1 - core) * rows, rows, 0), dc=1)

    energies = jnp.concatenate([plane, from_other[2 * slices :]])
    energies_s = send(energies, dc=1)
    column_energy = [
        lax.dynamic_slice_in_dim(e, (step_y * 4 + step_z) * classes, classes, 0) for e in (energies, energies_s)
    ]
    column_energy = jnp.where(
        core == 0, jnp.concatenate(column_energy, 1), jnp.concatenate(column_energy[::-1], 1)
    )
    column_labels = lax.dynamic_slice_in_dim(labels, freq * 2 * rows, 2 * rows)
    row_side = jnp.zeros((rows, 2 * rows), jnp.float32)
    column_side = jnp.zeros((rows, 2 * rows), jnp.float32)
    for d in range(classes):
        row_side = jnp.where(column_labels[None, :] == d, energy[d][:, None], row_side)
        column_side = jnp.where(own_labels[:, None] == d, column_energy[d][None, :], column_side)
    root = jnp.sqrt(row_side * column_side + 1e-06)
    found, root = together(found, root)
    return finished(info, found, swapped, root)


def solution(mesh):
    placed = (P("blk", "freq"), P(), P(None, "freq"), P("freq"), P())
    return jax.shard_map(
        per_device, mesh=mesh, in_specs=placed, out_specs=P("blk", "freq"), check_vma=False
    )
```

```python
import jax
import jax.numpy as jnp
from jax import lax
from jax.experimental import pallas as pl
from jax.experimental.pallas import tpu as pltpu
from jax.sharding import PartitionSpec as P

BOTH = ("blk", "freq")
VMEM_BYTES = 60 * 1024 * 1024
LANES = 128
PARAMS = pltpu.CompilerParams(vmem_limit_bytes=VMEM_BYTES)
COST = pl.CostEstimate(flops=1024, bytes_accessed=1024, transcendentals=0)
VMEM = pl.BlockSpec(memory_space=pltpu.VMEM)
SMEM = pl.BlockSpec(memory_space=pltpu.SMEM)
ANY = pl.BlockSpec(memory_space=pl.ANY)


def places():
    return [
        (yh, z, c, f) for yh in range(2) for z in range(4) for c in range(2) for f in range(8)
    ]


def place_index(yh, z, c, f):
    return (((yh % 2) * 4 + z % 4) * 2 + c % 2) * 8 + f % 8


def route(dyh, dz, dc, dyl):
    return [
        (place_index(yh, z, c, f), place_index(yh + dyh, z + dz, c + dc, f + 4 * dyl))
        for yh, z, c, f in places()
    ]


def send(block, dyh=0, dz=0, dc=0, dyl=0):
    return lax.ppermute(block, BOTH, route(dyh, dz, dc, dyl))


def summed_along_x(tiles):
    groups = [list(range(4)), list(range(4, 8))]
    return jnp.sum(lax.all_to_all(tiles, "freq", 0, 0, axis_index_groups=groups, tiled=True), 0)


def together(*arrays):
    return lax.optimization_barrier(arrays)


def scaled(block, weight):
    return (block.astype(jnp.float32) * weight).astype(jnp.bfloat16)


def gram(a, b):
    return lax.dot_general(a, b, (((1,), (1,)), ((), ())), preferred_element_type=jnp.float32)


CORE, YH, Z, HIGH, NEXT_HIGH, PREV_HIGH, ON_B2, ON_B3, ON_B5, ON_B6, LOWER, LOW, ONE, BY_ROW = range(14)


def span(which, half):
    return pl.ds(pl.multiple_of(which * half, LANES), half)


def spread_pairs():
    place = lax.broadcasted_iota(jnp.int32, (LANES, 2 * LANES), 0)
    return (lax.broadcasted_iota(jnp.int32, (LANES, 2 * LANES), 1) // 2 == place).astype(jnp.bfloat16)


def mask_kernel(info, hot, spectra, wedges, own, to_partner, to_next, to_previous, to_partner_b, to_previous_b, pairs):
    half = spectra.shape[1] // 2

    @pl.when(pl.program_id(0) == 0)
    def _():
        spread = spread_pairs()
        for j in range(half // LANES):
            some = wedges[:, pl.ds(j * LANES, LANES)].astype(jnp.float32).astype(jnp.bfloat16)
            wide = jnp.dot(some, spread, preferred_element_type=jnp.float32)
            pairs[:, pl.ds(j * 2 * LANES, 2 * LANES)] = wide.astype(jnp.bfloat16)

    keep = jnp.dot(hot[...], pairs[...], preferred_element_type=jnp.float32).astype(jnp.bfloat16)
    own[...] = spectra[...] * keep
    to_partner[...] = own[:, span(1 - info[YH], half)]
    to_next[...] = own[:, span(info[NEXT_HIGH], half)]
    to_previous[...] = own[:, span(info[PREV_HIGH], half)]
    to_partner_b[...] = own[:, span(info[YH], half)]
    to_previous_b[...] = own[:, span(1 - info[PREV_HIGH], half)]


def masked_blocks(info, hot, spectra, wedges):
    rows, width = spectra.shape
    classes = wedges.shape[0]
    part = rows // 4
    whole = lambda *shape: pl.BlockSpec(shape, lambda i, info: (0, 0))
    slab = lambda n: pl.BlockSpec((part, n), lambda i, info: (i, 0))
    half_block = jax.ShapeDtypeStruct((rows, width // 2), jnp.bfloat16)
    return pl.pallas_call(
        mask_kernel,
        grid_spec=pltpu.PrefetchScalarGridSpec(
            num_scalar_prefetch=1,
            grid=(4,),
            in_specs=[slab(classes), slab(width), whole(classes, width // 2)],
            out_specs=[slab(width)] + [slab(width // 2)] * 5 + [whole(classes, width)],
        ),
        out_shape=[
            jax.ShapeDtypeStruct((rows, width), jnp.bfloat16),
            *[half_block] * 5,
            jax.ShapeDtypeStruct((classes, width), jnp.bfloat16),
        ],
        compiler_params=PARAMS,
        cost_estimate=COST,
    )(info, hot, spectra, wedges)


def weight_kernel(shell_weight, shells, weight):
    spread = spread_pairs()

    def widen(x):
        return jnp.dot(x, spread, preferred_element_type=jnp.float32)

    for j in range(shells.shape[1] // LANES):
        shell = shells[:, pl.ds(j * LANES, LANES)]
        value = jnp.zeros(shell.shape, jnp.float32)
        for k in range(shell_weight.shape[0]):
            value = jnp.where(shell == k, shell_weight[k], value)
        top = value.astype(jnp.bfloat16)
        rest = value - top.astype(jnp.float32)
        middle = rest.astype(jnp.bfloat16)
        low = (rest - middle.astype(jnp.float32)).astype(jnp.bfloat16)
        weight[:, pl.ds(j * 2 * LANES, 2 * LANES)] = (widen(top) + widen(middle)) + widen(low)


def pair_weights(shell_weight, shells):
    return pl.pallas_call(
        weight_kernel,
        in_specs=[SMEM, VMEM],
        out_specs=VMEM,
        out_shape=jax.ShapeDtypeStruct((1, 2 * shells.shape[1]), jnp.float32),
        compiler_params=PARAMS,
        cost_estimate=COST,
    )(shell_weight, shells)


def first_kernel(info, own, sibling, weight, out, own_w, a, other, tiles, sems, out_sems):
    core = info[CORE]
    got_own = pltpu.make_async_copy(own, a.at[0], sems.at[0])
    got_sibling = pltpu.make_async_copy(sibling, other.at[0], sems.at[1])
    got_own.start()
    got_sibling.start()

    def leave(k, owner):
        copy = pltpu.make_async_copy(tiles.at[k], out.at[:, owner], out_sems.at[k])
        copy.start()
        return copy

    def put(k, tile):
        tiles[k] = tile.reshape(tiles.shape[1:])

    got_own.wait()
    a[1] = scaled(a[0], weight[...])
    left_w = pltpu.make_async_copy(a.at[1], own_w, out_sems.at[2])
    left_w.start()
    put(0, gram(a[1], a[0]))
    left_mine = leave(0, core)
    got_sibling.wait()

    @pl.when(core == 1)
    def _():
        other[1] = scaled(other[0], weight[...])

    put(1, gram(other[core], a[1 - core]))
    left_other = leave(1, 1 - core)
    left_w.wait()
    left_mine.wait()
    left_other.wait()


def first_tiles(info, own, sibling, weight):
    rows, width = own.shape
    block = pltpu.VMEM((2, rows, width), jnp.bfloat16)
    return pl.pallas_call(
        first_kernel,
        in_specs=[SMEM, ANY, ANY, VMEM],
        out_specs=[ANY, ANY],
        out_shape=[
            jax.ShapeDtypeStruct((4, 2, rows // 4, rows), jnp.float32),
            jax.ShapeDtypeStruct((rows, width), jnp.bfloat16),
        ],
        scratch_shapes=[
            block,
            block,
            pltpu.VMEM((2, 4, rows // 4, rows), jnp.float32),
            pltpu.SemaphoreType.DMA((2,)),
            pltpu.SemaphoreType.DMA((3,)),
        ],
        compiler_params=PARAMS,
        cost_estimate=COST,
    )(info, own, sibling, weight)


def half_kernel(
    k_tile, first_at, on_b_at, on_b_other_at, half_at, info, a_yes, a_no, other_yes, other_no, b_yes, b_no,
    weight, energy, *rest,
):
    out, a, b, tiles, sems, out_sems = rest[-6:]
    rows, half = b.shape[1:]
    slices = tiles.shape[2]
    core, first, at = info[CORE], info[first_at] == 1, span(info[half_at], half)
    w = weight[:, at]

    def pick(n, dst, yes, no):
        for chosen, src in ((first, yes), (jnp.logical_not(first), no)):
            src = src if src.shape[1] == half else src.at[:, at]

            @pl.when(chosen)
            def _(src=src):
                pltpu.make_async_copy(src, dst, sems.at[n]).start()

        return pltpu.make_async_copy(src, dst, sems.at[n])

    got_b = pick(0, b.at[0], b_yes, b_no)
    got_a = [pick(1, a.at[0], a_yes, a_no), pick(2, a.at[2], other_yes, other_no)]
    sent = []

    def go(src, dst, n):
        copy = pltpu.make_async_copy(src, dst, out_sems.at[n])
        copy.start()
        sent.append(copy)

    for x in range(4):
        go(energy, out.at[x, k_tile, pl.ds(2 * slices, energy.shape[0])], 2 + x)
    got_b.wait()
    b[1] = scaled(b[0], w)
    for k, (on_b, owner) in enumerate(((info[on_b_at], core), (info[on_b_other_at], 1 - core))):
        got_a[k].wait()

        @pl.when(on_b == 0)
        def _(k=k):
            a[2 * k + 1] = scaled(a[2 * k], w)

        tiles[k] = gram(a[2 * k + 1 - on_b], b[on_b]).reshape(tiles.shape[1:])
        go(tiles.at[k], out.at[:, k_tile, pl.ds(pl.multiple_of(owner * slices, 8), slices)], k)
    for copy in sent:
        copy.wait()


def half_tiles(places_of, info, *operands, into=None):
    rows, classes = operands[0].shape[0], operands[-1].shape[0]
    half = operands[-2].shape[1] // 2
    specs, aliases = [SMEM] + [ANY] * 6 + [VMEM] * 2, {}
    if into is not None:
        aliases = {len(specs): 0}
        specs, operands = specs + [ANY], operands + (into,)

    def kernel(*refs):
        half_kernel(*places_of, *refs)

    return pl.pallas_call(
        kernel,
        in_specs=specs,
        out_specs=ANY,
        out_shape=jax.ShapeDtypeStruct((4, 2, rows // 2 + classes, rows), jnp.float32),
        scratch_shapes=[
            pltpu.VMEM((4, rows, half), jnp.bfloat16),
            pltpu.VMEM((2, rows, half), jnp.bfloat16),
            pltpu.VMEM((2, 4, rows // 4, rows), jnp.float32),
            pltpu.SemaphoreType.DMA((3,)),
            pltpu.SemaphoreType.DMA((6,)),
        ],
        input_output_aliases=aliases,
        compiler_params=PARAMS,
        cost_estimate=COST,
    )(info, *operands)


def late_kernel(
    is_mine, info, own, own_w, partner_a, partner_b, a_high, a_low, mine_high, mine_low, diagonal, a_diagonal,
    weight, *rest,
):
    out, a, own_b, partner, sixth_a, sixth_b, tiles, sems, out_sems = rest[-9:]
    half = partner_a.shape[1]
    slices = out.shape[2]
    lower = info[YH] == 0
    high_is_yh = info[HIGH] == info[YH]
    high, yh = info[HIGH], info[YH]

    def pick(n, dst, *choices):
        for chosen, src in choices:

            @pl.when(chosen)
            def _(src=src):
                pltpu.make_async_copy(src, dst, sems.at[n]).start()

        return pltpu.make_async_copy(choices[0][1], dst, sems.at[n])

    always = info[CORE] >= 0
    no = jnp.logical_not
    got_b = pick(
        6,
        sixth_b,
        (lower, diagonal),
        (jnp.logical_and(no(lower), high_is_yh), mine_high),
        (jnp.logical_and(no(lower), no(high_is_yh)), mine_low),
    )
    got_a = pick(
        5,
        sixth_a,
        (no(lower), a_diagonal),
        (jnp.logical_and(lower, high_is_yh), a_high),
        (jnp.logical_and(lower, no(high_is_yh)), a_low),
    )
    got_high = pick(0, a.at[0, :, span(high, half)], (always, a_high))
    got_low = pick(1, a.at[0, :, span(1 - high, half)], (always, a_low))
    got_own = pick(2, own_b, (info[ON_B2] == 1, own_w), (info[ON_B2] == 0, own))
    got_near = pick(3, partner.at[:, span(yh, half)], (always, partner_a))
    got_far = pick(4, partner.at[:, span(1 - yh, half)], (always, partner_b))
    owner = info[CORE] if is_mine else 1 - info[CORE]
    sent = []

    def put(k, tile):
        tiles[k] = tile.reshape(4, slices, tile.shape[1])

    def leave(k):
        copy = pltpu.make_async_copy(tiles.at[k], out.at[pl.ds(owner * 4, 4), k], out_sems.at[k])
        copy.start()
        sent.append(copy)

    got_a.wait()
    got_b.wait()
    w_yh = weight[:, span(yh, half)]

    @pl.when(info[ON_B6] == 1)
    def _():
        sixth_b[...] = scaled(sixth_b[...], w_yh)

    @pl.when(info[ON_B6] == 0)
    def _():
        sixth_a[...] = scaled(sixth_a[...], w_yh)

    put(2, gram(sixth_a[...], sixth_b[...]))
    leave(2)
    got_high.wait()
    got_low.wait()
    a[1] = scaled(a[0], weight[...])
    got_own.wait()
    put(0, gram(a[1 - info[ON_B2]], own_b[...]))
    leave(0)
    got_near.wait()
    got_far.wait()

    @pl.when(info[ON_B5] == 1)
    def _():
        partner[...] = scaled(partner[...], weight[...])

    put(1, gram(a[1 - info[ON_B5]], partner[...]))
    leave(1)
    for copy in sent:
        copy.wait()


def late_tiles(is_mine, info, own, own_w, partner_a, partner_b, a_high, a_low, mine_high, mine_low, diagonal,
               a_diagonal, weight, other=None):
    rows, width = own.shape
    half = width // 2
    arrays = [own, own_w, partner_a, partner_b, a_high, a_low, mine_high, mine_low, diagonal, a_diagonal, weight]
    specs = [SMEM] + [ANY] * 10 + [VMEM]
    aliases = {}
    if other is not None:
        arrays.append(other)
        specs.append(ANY)
        aliases = {len(specs) - 1: 0}
    block = lambda n: pltpu.VMEM((rows, n), jnp.bfloat16)

    def kernel(*refs):
        late_kernel(is_mine, *refs)

    return pl.pallas_call(
        kernel,
        in_specs=specs,
        out_specs=ANY,
        out_shape=jax.ShapeDtypeStruct((8, 3, rows // 4, rows), jnp.float32),
        scratch_shapes=[
            pltpu.VMEM((2, rows, width), jnp.bfloat16),
            block(width),
            block(width),
            block(half),
            block(half),
            pltpu.VMEM((3, 4, rows // 4, rows), jnp.float32),
            pltpu.SemaphoreType.DMA((7,)),
            pltpu.SemaphoreType.DMA((3,)),
        ],
        input_output_aliases=aliases,
        compiler_params=PARAMS,
        cost_estimate=COST,
    )(info, *arrays)


def gather_kernel(info, early, late, from_previous, third_back, third_ahead, from_other, from_diagonal, out):
    yh, z = info[YH], info[Z]

    def put(dyh, dz, value):
        out[(yh + dyh) % 2 * 4 + (z + dz) % 4] = value

    slices = out.shape[1]
    put(0, 0, early[:slices])
    put(0, 1, late[0])
    put(0, 2, third_back[:slices] + third_ahead[:slices])
    put(0, 3, from_previous[0])
    put(1, 0, early[2 * slices : 3 * slices] + from_other[slices : 2 * slices])
    put(1, 1, from_other[:slices])
    put(1, 2, from_previous[2] + from_diagonal[...])
    put(1, 3, from_previous[1])


def gathered(info, *parts):
    slices, rows = parts[1].shape[1:]
    return pl.pallas_call(
        gather_kernel,
        in_specs=[SMEM] + [VMEM] * len(parts),
        out_specs=VMEM,
        out_shape=jax.ShapeDtypeStruct((8, slices, rows), jnp.float32),
    )(info, *parts)


def final_kernel(info, found, swapped, root, out):
    rows = swapped.shape[0]
    core, by_row = info[CORE], info[BY_ROW]

    for is_first in (True, False):

        @pl.when(jnp.logical_and(by_row == 1, (core == 0) == is_first))
        def _(is_first=is_first):
            kept = found[:rows] if is_first else found[rows:]
            pair = (kept, swapped[...]) if is_first else (swapped[...], kept)
            out[...] = jnp.concatenate(pair, 1) / root[...]

    @pl.when(by_row == 0)
    def _():
        out[...] = found[...].T / root[...]


def finished(info, found, swapped, root):
    return pl.pallas_call(
        final_kernel,
        in_specs=[SMEM, VMEM, VMEM, VMEM],
        out_specs=VMEM,
        out_shape=jax.ShapeDtypeStruct(root.shape, jnp.float32),
    )(info, found, swapped, root)


def per_device(spectra, labels, wedges, shells, shell_weight):
    rows, width = spectra.shape
    half, slices = width // 2, rows // 4
    classes = wedges.shape[0]
    blk = lax.axis_index("blk")
    core, z, yh = blk % 2, (blk // 2) % 4, blk // 8
    freq = lax.axis_index("freq")

    def place(dyh, dz):
        return ((yh + dyh) % 2) * 4 + (z + dz) % 4

    def ahead(a, b):
        return ((a - b) % 8 < 4).astype(jnp.int32)

    def columns(block, which):
        return lax.dynamic_slice_in_dim(block, which * half, half, 1)

    low, lower = z < 2, yh == 0
    high = z // 2
    previous_high = ((z + 3) % 4) // 2
    step_y, step_z = (freq // 4 + yh) % 2, (freq % 4 - z) % 4
    same_y = step_y == 0
    inner_z = jnp.logical_or(z == 1, z == 2)
    by_row = jnp.where(
        step_z == 0,
        jnp.logical_or(same_y, yh == 1),
        jnp.where(step_z == 1, False, jnp.where(step_z == 2, jnp.where(same_y, inner_z, lower), True)),
    )
    info = jnp.stack(
        [
            core,
            yh,
            z,
            high,
            ((z + 1) % 4) // 2,
            previous_high,
            ahead(place(0, 1), place(0, 0)),
            jnp.where(low, ahead(place(0, 1), place(0, -1)), ahead(place(0, -1), place(0, 1))),
            ahead(place(0, 1), place(1, 0)),
            jnp.where(lower, ahead(place(0, 1), place(1, -1)), ahead(place(1, -1), place(0, 1))),
            lower.astype(jnp.int32),
            low.astype(jnp.int32),
            jnp.int32(1),
            by_row.astype(jnp.int32),
        ]
    ).astype(jnp.int32)

    class_range = jnp.arange(classes, dtype=jnp.int32)
    own_labels = lax.dynamic_slice_in_dim(labels, blk * rows, rows)
    hot = (own_labels[:, None] == class_range[None, :]).astype(jnp.bfloat16)
    own, to_partner, to_next, to_previous, to_partner_b, to_previous_b, pairs = masked_blocks(info, hot, spectra, wedges)

    following_a = send(to_previous, dz=-1)
    partner_a = send(to_partner, dyh=1)
    previous = send(to_next, dz=1)
    following_b = send(to_previous_b, dz=-1)
    sibling = send(own, dc=1)
    own, shells = together(own, shells)
    weight = pair_weights(shell_weight, shells[None, :])
    q1, own_w = first_tiles(info, own, sibling, weight)
    p1 = summed_along_x(q1)
    own_e, q1 = together(own, q1)
    squares = own_e.astype(jnp.float32) ** 2 * weight
    partial_energy = lax.dot_general(
        pairs.astype(jnp.float32), squares, (((1,), (1,)), ((), ())), precision=lax.Precision.HIGHEST
    )
    partner_b = send(to_partner_b, dyh=1)
    partner_a, p1, partial_energy = together(partner_a, p1, partial_energy)
    diagonal = send(partner_a, dz=1)
    partner_s = send(partner_a, dc=1)
    third_a_s = send(jnp.where(low, following_a, previous), dc=1)
    half_pair = half_tiles(
        (1, LOWER, ONE, CORE, YH), info, partner_a, own, partner_s, sibling, own, partner_a, weight, partial_energy
    )
    half_pair = half_tiles(
        (0, LOW, ON_B3, ON_B3, HIGH), info, following_a, previous, third_a_s, third_a_s, previous, following_a, weight,
        partial_energy, into=half_pair,
    )
    half_pair = summed_along_x(half_pair)
    following_b, partner_b, diagonal, half_pair = together(following_b, partner_b, diagonal, half_pair)

    own_yl = freq // 4

    def halves(which):
        return [
            lax.dynamic_index_in_dim(p1, which, 0, keepdims=False),
            lax.dynamic_slice_in_dim(half_pair[0], which * slices, slices, 0),
            lax.dynamic_slice_in_dim(half_pair[1], which * slices, slices, 0),
            half_pair[1, 2 * slices :],
        ]

    following_as = send(following_a, dc=1)
    following_bs = send(following_b, dc=1)
    diagonal_s = send(diagonal, dc=1)
    early = send(jnp.concatenate(halves(1 - own_yl)), dyl=1)
    late = late_tiles(
        True, info, own, own_w, partner_a, partner_b, following_a, following_b, following_a, following_b,
        diagonal, diagonal, weight,
    )
    late, following_as, following_bs, diagonal_s = together(late, following_as, following_bs, diagonal_s)
    late = late_tiles(
        False, info, own, own_w, partner_a, partner_b, following_as, following_bs, following_a, following_b,
        diagonal, diagonal_s, weight, late,
    )
    late, early = together(late, early)
    late = lax.all_to_all(late, "freq", 0, 0, tiled=True)

    early = jnp.concatenate(halves(own_yl)) + early
    third, energy = early[slices : 2 * slices], early[3 * slices :]
    third_energy = jnp.concatenate([third, energy])
    back, forth, opposite = send(third_energy, dz=1), send(third_energy, dz=-1), send(energy, dz=2)
    fourth_plane = jnp.concatenate(
        [early[2 * slices : 3 * slices], energy, forth[slices:], opposite, back[slices:]]
    )
    late, fourth_plane = together(late, fourth_plane)
    sixth = jnp.sum(late[:, 2], 0)
    late = jnp.sum(late, 0)

    from_previous = send(late, dz=1)
    from_other = send(jnp.concatenate([late[1], fourth_plane]), dyh=1)
    from_diagonal = send(sixth, dyh=1, dz=-1)
    from_previous, from_other, from_diagonal = together(from_previous, from_other, from_diagonal)
    pieces = gathered(info, early, late, from_previous, back, forth, from_other, from_diagonal)
    found = lax.all_to_all(pieces, "freq", 0, 0, tiled=True).reshape(2 * rows, rows)
    swapped = send(lax.dynamic_slice_in_dim(found, (1 - core) * rows, rows, 0), dc=1)

    energies = jnp.concatenate([fourth_plane[slices:], from_other[2 * slices :]])
    energies_s = send(energies, dc=1)
    column_energy = [
        lax.dynamic_slice_in_dim(e, (step_y * 4 + step_z) * classes, classes, 0) for e in (energies, energies_s)
    ]
    column_energy = jnp.where(
        core == 0, jnp.concatenate(column_energy, 1), jnp.concatenate(column_energy[::-1], 1)
    )
    column_labels = lax.dynamic_slice_in_dim(labels, freq * 2 * rows, 2 * rows)
    row_side = jnp.zeros((rows, 2 * rows), jnp.float32)
    column_side = jnp.zeros((rows, 2 * rows), jnp.float32)
    for d in range(classes):
        row_side = jnp.where(column_labels[None, :] == d, energy[d][:, None], row_side)
        column_side = jnp.where(own_labels[:, None] == d, column_energy[d][None, :], column_side)
    root = jnp.sqrt(row_side * column_side + 1e-06)
    found, root = together(found, root)
    return finished(info, found, swapped, root)


def solution(mesh):
    placed = (P("blk", "freq"), P(), P(None, "freq"), P("freq"), P())
    return jax.shard_map(
        per_device, mesh=mesh, in_specs=placed, out_specs=P("blk", "freq"), check_vma=False
    )
```

```python
import jax
import jax.numpy as jnp
from jax import lax
from jax.experimental import pallas as pl
from jax.experimental.pallas import tpu as pltpu
from jax.sharding import PartitionSpec as P

BOTH = ("blk", "freq")
VMEM_BYTES = 60 * 1024 * 1024
LANES = 128
PARAMS = pltpu.CompilerParams(vmem_limit_bytes=VMEM_BYTES)
COST = pl.CostEstimate(flops=1024, bytes_accessed=1024, transcendentals=0)
VMEM = pl.BlockSpec(memory_space=pltpu.VMEM)
SMEM = pl.BlockSpec(memory_space=pltpu.SMEM)
ANY = pl.BlockSpec(memory_space=pl.ANY)


def places():
    return [
        (yh, z, c, f) for yh in range(2) for z in range(4) for c in range(2) for f in range(8)
    ]


def place_index(yh, z, c, f):
    return (((yh % 2) * 4 + z % 4) * 2 + c % 2) * 8 + f % 8


def route(dyh, dz, dc, dyl):
    return [
        (place_index(yh, z, c, f), place_index(yh + dyh, z + dz, c + dc, f + 4 * dyl))
        for yh, z, c, f in places()
    ]


def send(block, dyh=0, dz=0, dc=0, dyl=0):
    return lax.ppermute(block, BOTH, route(dyh, dz, dc, dyl))


def summed_along_x(tiles):
    groups = [list(range(4)), list(range(4, 8))]
    return jnp.sum(lax.all_to_all(tiles, "freq", 0, 0, axis_index_groups=groups, tiled=True), 0)


def together(*arrays):
    return lax.optimization_barrier(arrays)


def scaled(block, weight):
    return (block.astype(jnp.float32) * weight).astype(jnp.bfloat16)


def gram(a, b):
    return lax.dot_general(a, b, (((1,), (1,)), ((), ())), preferred_element_type=jnp.float32)


CORE, YH, Z, HIGH, NEXT_HIGH, PREV_HIGH, ON_B2, ON_B3, ON_B5, ON_B6, LOWER, LOW, ONE, BY_ROW = range(14)


def span(which, half):
    return pl.ds(pl.multiple_of(which * half, LANES), half)


def spread_pairs():
    place = lax.broadcasted_iota(jnp.int32, (LANES, 2 * LANES), 0)
    return (lax.broadcasted_iota(jnp.int32, (LANES, 2 * LANES), 1) // 2 == place).astype(jnp.bfloat16)


def mask_kernel(info, hots, spectra, sibling, wedges, own, own_sibling, to_partner_b, to_previous_b, pairs):
    half = spectra.shape[1] // 2

    @pl.when(pl.program_id(0) == 0)
    def _():
        spread = spread_pairs()
        for j in range(half // LANES):
            some = wedges[:, pl.ds(j * LANES, LANES)].astype(jnp.float32).astype(jnp.bfloat16)
            wide = jnp.dot(some, spread, preferred_element_type=jnp.float32)
            pairs[:, pl.ds(j * 2 * LANES, 2 * LANES)] = wide.astype(jnp.bfloat16)

    for k, (block, out) in enumerate(((spectra, own), (sibling, own_sibling))):
        keep = jnp.dot(hots[k], pairs[...], preferred_element_type=jnp.float32).astype(jnp.bfloat16)
        out[...] = block[...] * keep
    to_partner_b[...] = own[:, span(info[YH], half)]
    to_previous_b[...] = own[:, span(1 - info[PREV_HIGH], half)]


def masked_blocks(info, hots, spectra, sibling, wedges):
    rows, width = spectra.shape
    classes = wedges.shape[0]
    part = rows // 4
    whole = lambda *shape: pl.BlockSpec(shape, lambda i, info: (0, 0))
    slab = lambda n: pl.BlockSpec((part, n), lambda i, info: (i, 0))
    block = jax.ShapeDtypeStruct((rows, width), jnp.bfloat16)
    half_block = jax.ShapeDtypeStruct((rows, width // 2), jnp.bfloat16)
    return pl.pallas_call(
        mask_kernel,
        grid_spec=pltpu.PrefetchScalarGridSpec(
            num_scalar_prefetch=1,
            grid=(4,),
            in_specs=[
                pl.BlockSpec((2, part, classes), lambda i, info: (0, i, 0)),
                slab(width),
                slab(width),
                whole(classes, width // 2),
            ],
            out_specs=[slab(width)] * 2 + [slab(width // 2)] * 2 + [whole(classes, width)],
        ),
        out_shape=[block, block, half_block, half_block, jax.ShapeDtypeStruct((classes, width), jnp.bfloat16)],
        compiler_params=PARAMS,
        cost_estimate=COST,
    )(info, hots, spectra, sibling, wedges)


def received_kernel(info, hots, pairs, following, partner, previous, out_following, out_partner, out_previous, third):
    half = following.shape[1]

    def masked(k, block, at):
        keep = jnp.dot(hots[k], pairs[:, at], preferred_element_type=jnp.float32).astype(jnp.bfloat16)
        return block[...] * keep

    at_high = span(info[HIGH], half)
    out_following[...] = masked(0, following, at_high)
    out_partner[...] = masked(1, partner, span(info[YH], half))
    out_previous[...] = masked(2, previous, at_high)

    @pl.when(info[LOW] == 1)
    def _():
        third[...] = out_following[...]

    @pl.when(info[LOW] == 0)
    def _():
        third[...] = out_previous[...]


def masked_received(info, hots, pairs, *blocks):
    rows, half = blocks[0].shape
    classes, width = pairs.shape
    part = rows // 4
    slab = pl.BlockSpec((part, half), lambda i, info: (i, 0))
    return pl.pallas_call(
        received_kernel,
        grid_spec=pltpu.PrefetchScalarGridSpec(
            num_scalar_prefetch=1,
            grid=(4,),
            in_specs=[
                pl.BlockSpec((3, part, classes), lambda i, info: (0, i, 0)),
                pl.BlockSpec((classes, width), lambda i, info: (0, 0)),
                slab,
                slab,
                slab,
            ],
            out_specs=[slab] * 4,
        ),
        out_shape=[jax.ShapeDtypeStruct((rows, half), jnp.bfloat16)] * 4,
        compiler_params=PARAMS,
        cost_estimate=COST,
    )(info, hots, pairs, *blocks)


def weight_kernel(shell_weight, shells, weight):
    spread = spread_pairs()

    def widen(x):
        return jnp.dot(x, spread, preferred_element_type=jnp.float32)

    for j in range(shells.shape[1] // LANES):
        shell = shells[:, pl.ds(j * LANES, LANES)]
        value = jnp.zeros(shell.shape, jnp.float32)
        for k in range(shell_weight.shape[0]):
            value = jnp.where(shell == k, shell_weight[k], value)
        top = value.astype(jnp.bfloat16)
        rest = value - top.astype(jnp.float32)
        middle = rest.astype(jnp.bfloat16)
        low = (rest - middle.astype(jnp.float32)).astype(jnp.bfloat16)
        weight[:, pl.ds(j * 2 * LANES, 2 * LANES)] = (widen(top) + widen(middle)) + widen(low)


def pair_weights(shell_weight, shells):
    return pl.pallas_call(
        weight_kernel,
        in_specs=[SMEM, VMEM],
        out_specs=VMEM,
        out_shape=jax.ShapeDtypeStruct((1, 2 * shells.shape[1]), jnp.float32),
        compiler_params=PARAMS,
        cost_estimate=COST,
    )(shell_weight, shells)


def first_kernel(info, own, sibling, weight, out, own_w, a, other, tiles, sems, out_sems):
    core = info[CORE]
    got_own = pltpu.make_async_copy(own, a.at[0], sems.at[0])
    got_sibling = pltpu.make_async_copy(sibling, other.at[0], sems.at[1])
    got_own.start()
    got_sibling.start()

    def leave(k, owner):
        copy = pltpu.make_async_copy(tiles.at[k], out.at[:, owner], out_sems.at[k])
        copy.start()
        return copy

    def put(k, tile):
        tiles[k] = tile.reshape(tiles.shape[1:])

    got_own.wait()
    a[1] = scaled(a[0], weight[...])
    left_w = pltpu.make_async_copy(a.at[1], own_w, out_sems.at[2])
    left_w.start()
    put(0, gram(a[1], a[0]))
    left_mine = leave(0, core)
    got_sibling.wait()

    @pl.when(core == 1)
    def _():
        other[1] = scaled(other[0], weight[...])

    put(1, gram(other[core], a[1 - core]))
    left_other = leave(1, 1 - core)
    left_w.wait()
    left_mine.wait()
    left_other.wait()


def first_tiles(info, own, sibling, weight):
    rows, width = own.shape
    block = pltpu.VMEM((2, rows, width), jnp.bfloat16)
    return pl.pallas_call(
        first_kernel,
        in_specs=[SMEM, ANY, ANY, VMEM],
        out_specs=[ANY, ANY],
        out_shape=[
            jax.ShapeDtypeStruct((4, 2, rows // 4, rows), jnp.float32),
            jax.ShapeDtypeStruct((rows, width), jnp.bfloat16),
        ],
        scratch_shapes=[
            block,
            block,
            pltpu.VMEM((2, 4, rows // 4, rows), jnp.float32),
            pltpu.SemaphoreType.DMA((2,)),
            pltpu.SemaphoreType.DMA((3,)),
        ],
        compiler_params=PARAMS,
        cost_estimate=COST,
    )(info, own, sibling, weight)


def half_kernel(
    k_tile, first_at, on_b_at, on_b_other_at, half_at, info, a_yes, a_no, other_yes, other_no, b_yes, b_no,
    weight, energy, *rest,
):
    out, a, b, tiles, sems, out_sems = rest[-6:]
    rows, half = b.shape[1:]
    slices = tiles.shape[2]
    core, first, at = info[CORE], info[first_at] == 1, span(info[half_at], half)
    w = weight[:, at]

    def pick(n, dst, yes, no):
        for chosen, src in ((first, yes), (jnp.logical_not(first), no)):
            src = src if src.shape[1] == half else src.at[:, at]

            @pl.when(chosen)
            def _(src=src):
                pltpu.make_async_copy(src, dst, sems.at[n]).start()

        return pltpu.make_async_copy(src, dst, sems.at[n])

    got_b = pick(0, b.at[0], b_yes, b_no)
    got_a = [pick(1, a.at[0], a_yes, a_no), pick(2, a.at[2], other_yes, other_no)]
    sent = []

    def go(src, dst, n):
        copy = pltpu.make_async_copy(src, dst, out_sems.at[n])
        copy.start()
        sent.append(copy)

    for x in range(4):
        go(energy, out.at[x, k_tile, pl.ds(2 * slices, energy.shape[0])], 2 + x)
    got_b.wait()
    b[1] = scaled(b[0], w)
    for k, (on_b, owner) in enumerate(((info[on_b_at], core), (info[on_b_other_at], 1 - core))):
        got_a[k].wait()

        @pl.when(on_b == 0)
        def _(k=k):
            a[2 * k + 1] = scaled(a[2 * k], w)

        tiles[k] = gram(a[2 * k + 1 - on_b], b[on_b]).reshape(tiles.shape[1:])
        go(tiles.at[k], out.at[:, k_tile, pl.ds(pl.multiple_of(owner * slices, 8), slices)], k)
    for copy in sent:
        copy.wait()


def half_tiles(places_of, info, *operands, into=None):
    rows, classes = operands[0].shape[0], operands[-1].shape[0]
    half = operands[-2].shape[1] // 2
    specs, aliases = [SMEM] + [ANY] * 6 + [VMEM] * 2, {}
    if into is not None:
        aliases = {len(specs): 0}
        specs, operands = specs + [ANY], operands + (into,)

    def kernel(*refs):
        half_kernel(*places_of, *refs)

    return pl.pallas_call(
        kernel,
        in_specs=specs,
        out_specs=ANY,
        out_shape=jax.ShapeDtypeStruct((4, 2, rows // 2 + classes, rows), jnp.float32),
        scratch_shapes=[
            pltpu.VMEM((4, rows, half), jnp.bfloat16),
            pltpu.VMEM((2, rows, half), jnp.bfloat16),
            pltpu.VMEM((2, 4, rows // 4, rows), jnp.float32),
            pltpu.SemaphoreType.DMA((3,)),
            pltpu.SemaphoreType.DMA((6,)),
        ],
        input_output_aliases=aliases,
        compiler_params=PARAMS,
        cost_estimate=COST,
    )(info, *operands)


def late_kernel(
    is_mine, info, own, own_w, partner_a, partner_b, a_high, a_low, mine_high, mine_low, diagonal, a_diagonal,
    weight, *rest,
):
    out, a, own_b, partner, sixth_a, sixth_b, tiles, sems, out_sems = rest[-9:]
    half = partner_a.shape[1]
    slices = out.shape[2]
    lower = info[YH] == 0
    high_is_yh = info[HIGH] == info[YH]
    high, yh = info[HIGH], info[YH]

    def pick(n, dst, *choices):
        for chosen, src in choices:

            @pl.when(chosen)
            def _(src=src):
                pltpu.make_async_copy(src, dst, sems.at[n]).start()

        return pltpu.make_async_copy(choices[0][1], dst, sems.at[n])

    always = info[CORE] >= 0
    no = jnp.logical_not
    got_b = pick(
        6,
        sixth_b,
        (lower, diagonal),
        (jnp.logical_and(no(lower), high_is_yh), mine_high),
        (jnp.logical_and(no(lower), no(high_is_yh)), mine_low),
    )
    got_a = pick(
        5,
        sixth_a,
        (no(lower), a_diagonal),
        (jnp.logical_and(lower, high_is_yh), a_high),
        (jnp.logical_and(lower, no(high_is_yh)), a_low),
    )
    got_high = pick(0, a.at[0, :, span(high, half)], (always, a_high))
    got_low = pick(1, a.at[0, :, span(1 - high, half)], (always, a_low))
    got_own = pick(2, own_b, (info[ON_B2] == 1, own_w), (info[ON_B2] == 0, own))
    got_near = pick(3, partner.at[:, span(yh, half)], (always, partner_a))
    got_far = pick(4, partner.at[:, span(1 - yh, half)], (always, partner_b))
    owner = info[CORE] if is_mine else 1 - info[CORE]
    sent = []

    def put(k, tile):
        tiles[k] = tile.reshape(4, slices, tile.shape[1])

    def leave(k):
        copy = pltpu.make_async_copy(tiles.at[k], out.at[pl.ds(owner * 4, 4), k], out_sems.at[k])
        copy.start()
        sent.append(copy)

    got_a.wait()
    got_b.wait()
    w_yh = weight[:, span(yh, half)]

    @pl.when(info[ON_B6] == 1)
    def _():
        sixth_b[...] = scaled(sixth_b[...], w_yh)

    @pl.when(info[ON_B6] == 0)
    def _():
        sixth_a[...] = scaled(sixth_a[...], w_yh)

    put(2, gram(sixth_a[...], sixth_b[...]))
    leave(2)
    got_high.wait()
    got_low.wait()
    a[1] = scaled(a[0], weight[...])
    got_own.wait()
    put(0, gram(a[1 - info[ON_B2]], own_b[...]))
    leave(0)
    got_near.wait()
    got_far.wait()

    @pl.when(info[ON_B5] == 1)
    def _():
        partner[...] = scaled(partner[...], weight[...])

    put(1, gram(a[1 - info[ON_B5]], partner[...]))
    leave(1)
    for copy in sent:
        copy.wait()


def late_tiles(is_mine, info, own, own_w, partner_a, partner_b, a_high, a_low, mine_high, mine_low, diagonal,
               a_diagonal, weight, other=None):
    rows, width = own.shape
    half = width // 2
    arrays = [own, own_w, partner_a, partner_b, a_high, a_low, mine_high, mine_low, diagonal, a_diagonal, weight]
    specs = [SMEM] + [ANY] * 10 + [VMEM]
    aliases = {}
    if other is not None:
        arrays.append(other)
        specs.append(ANY)
        aliases = {len(specs) - 1: 0}
    block = lambda n: pltpu.VMEM((rows, n), jnp.bfloat16)

    def kernel(*refs):
        late_kernel(is_mine, *refs)

    return pl.pallas_call(
        kernel,
        in_specs=specs,
        out_specs=ANY,
        out_shape=jax.ShapeDtypeStruct((8, 3, rows // 4, rows), jnp.float32),
        scratch_shapes=[
            pltpu.VMEM((2, rows, width), jnp.bfloat16),
            block(width),
            block(width),
            block(half),
            block(half),
            pltpu.VMEM((3, 4, rows // 4, rows), jnp.float32),
            pltpu.SemaphoreType.DMA((7,)),
            pltpu.SemaphoreType.DMA((3,)),
        ],
        input_output_aliases=aliases,
        compiler_params=PARAMS,
        cost_estimate=COST,
    )(info, *arrays)


def gather_kernel(info, early, late, from_previous, third_back, third_ahead, from_other, from_diagonal, out):
    yh, z = info[YH], info[Z]

    def put(dyh, dz, value):
        out[(yh + dyh) % 2 * 4 + (z + dz) % 4] = value

    slices = out.shape[1]
    put(0, 0, early[:slices])
    put(0, 1, late[0])
    put(0, 2, third_back[:slices] + third_ahead[:slices])
    put(0, 3, from_previous[0])
    put(1, 0, early[2 * slices : 3 * slices] + from_other[slices : 2 * slices])
    put(1, 1, from_other[:slices])
    put(1, 2, from_previous[2] + from_diagonal[...])
    put(1, 3, from_previous[1])


def gathered(info, *parts):
    slices, rows = parts[1].shape[1:]
    return pl.pallas_call(
        gather_kernel,
        in_specs=[SMEM] + [VMEM] * len(parts),
        out_specs=VMEM,
        out_shape=jax.ShapeDtypeStruct((8, slices, rows), jnp.float32),
    )(info, *parts)


def final_kernel(info, found, swapped, root, out):
    rows = swapped.shape[0]
    core, by_row = info[CORE], info[BY_ROW]

    for is_first in (True, False):

        @pl.when(jnp.logical_and(by_row == 1, (core == 0) == is_first))
        def _(is_first=is_first):
            kept = found[:rows] if is_first else found[rows:]
            pair = (kept, swapped[...]) if is_first else (swapped[...], kept)
            out[...] = jnp.concatenate(pair, 1) / root[...]

    @pl.when(by_row == 0)
    def _():
        out[...] = found[...].T / root[...]


def finished(info, found, swapped, root):
    return pl.pallas_call(
        final_kernel,
        in_specs=[SMEM, VMEM, VMEM, VMEM],
        out_specs=VMEM,
        out_shape=jax.ShapeDtypeStruct(root.shape, jnp.float32),
    )(info, found, swapped, root)


def per_device(spectra, labels, wedges, shells, shell_weight):
    rows, width = spectra.shape
    half, slices = width // 2, rows // 4
    classes = wedges.shape[0]
    blk = lax.axis_index("blk")
    core, z, yh = blk % 2, (blk // 2) % 4, blk // 8
    freq = lax.axis_index("freq")

    def place(dyh, dz):
        return ((yh + dyh) % 2) * 4 + (z + dz) % 4

    def ahead(a, b):
        return ((a - b) % 8 < 4).astype(jnp.int32)

    def columns(block, which):
        return lax.dynamic_slice_in_dim(block, which * half, half, 1)

    low, lower = z < 2, yh == 0
    high = z // 2
    previous_high = ((z + 3) % 4) // 2
    step_y, step_z = (freq // 4 + yh) % 2, (freq % 4 - z) % 4
    same_y = step_y == 0
    inner_z = jnp.logical_or(z == 1, z == 2)
    by_row = jnp.where(
        step_z == 0,
        jnp.logical_or(same_y, yh == 1),
        jnp.where(step_z == 1, False, jnp.where(step_z == 2, jnp.where(same_y, inner_z, lower), True)),
    )
    info = jnp.stack(
        [
            core,
            yh,
            z,
            high,
            ((z + 1) % 4) // 2,
            previous_high,
            ahead(place(0, 1), place(0, 0)),
            jnp.where(low, ahead(place(0, 1), place(0, -1)), ahead(place(0, -1), place(0, 1))),
            ahead(place(0, 1), place(1, 0)),
            jnp.where(lower, ahead(place(0, 1), place(1, -1)), ahead(place(1, -1), place(0, 1))),
            lower.astype(jnp.int32),
            low.astype(jnp.int32),
            jnp.int32(1),
            by_row.astype(jnp.int32),
        ]
    ).astype(jnp.int32)

    class_range = jnp.arange(classes, dtype=jnp.int32)
    following_a = send(columns(spectra, previous_high), dz=-1)
    partner_a = send(columns(spectra, 1 - yh), dyh=1)
    previous = send(columns(spectra, (z + 1) % 4 // 2), dz=1)

    sibling = send(spectra, dc=1)

    def labels_of(block):
        return lax.dynamic_slice_in_dim(labels, block * rows, rows)

    own_labels = labels_of(blk)
    hots = jnp.stack(
        [own_labels, labels_of(blk + 1 - 2 * core)]
        + [labels_of(place(dyh, dz) * 2 + core) for dyh, dz in ((0, 1), (1, 0), (0, -1))]
    )
    hots = (hots[:, :, None] == class_range[None, None, :]).astype(jnp.bfloat16)
    own, sibling, to_partner_b, to_previous_b, pairs = masked_blocks(info, hots[:2], spectra, sibling, wedges)
    following_b = send(to_previous_b, dz=-1)
    own, shells = together(own, shells)
    weight = pair_weights(shell_weight, shells[None, :])
    q1, own_w = first_tiles(info, own, sibling, weight)
    p1 = summed_along_x(q1)
    own_e, q1 = together(own, q1)
    squares = own_e.astype(jnp.float32) ** 2 * weight
    partial_energy = lax.dot_general(
        pairs.astype(jnp.float32), squares, (((1,), (1,)), ((), ())), precision=lax.Precision.HIGHEST
    )
    partner_b = send(to_partner_b, dyh=1)
    partner_a, p1, partial_energy = together(partner_a, p1, partial_energy)
    following_a, partner_a, previous, third_a = masked_received(info, hots[2:], pairs, following_a, partner_a, previous)
    diagonal = send(partner_a, dz=1)
    partner_s = send(partner_a, dc=1)
    third_a_s = send(third_a, dc=1)
    half_pair = half_tiles(
        (1, LOWER, ONE, CORE, YH), info, partner_a, own, partner_s, sibling, own, partner_a, weight, partial_energy
    )
    half_pair = half_tiles(
        (0, LOW, ON_B3, ON_B3, HIGH), info, following_a, previous, third_a_s, third_a_s, previous, following_a, weight,
        partial_energy, into=half_pair,
    )
    half_pair = summed_along_x(half_pair)
    following_b, partner_b, diagonal, half_pair = together(following_b, partner_b, diagonal, half_pair)

    own_yl = freq // 4

    def halves(which):
        return [
            lax.dynamic_index_in_dim(p1, which, 0, keepdims=False),
            lax.dynamic_slice_in_dim(half_pair[0], which * slices, slices, 0),
            lax.dynamic_slice_in_dim(half_pair[1], which * slices, slices, 0),
            half_pair[1, 2 * slices :],
        ]

    following_as = send(following_a, dc=1)
    following_bs = send(following_b, dc=1)
    diagonal_s = send(diagonal, dc=1)
    early = send(jnp.concatenate(halves(1 - own_yl)), dyl=1)
    late = late_tiles(
        True, info, own, own_w, partner_a, partner_b, following_a, following_b, following_a, following_b,
        diagonal, diagonal, weight,
    )
    late, following_as, following_bs, diagonal_s = together(late, following_as, following_bs, diagonal_s)
    late = late_tiles(
        False, info, own, own_w, partner_a, partner_b, following_as, following_bs, following_a, following_b,
        diagonal, diagonal_s, weight, late,
    )
    late, early = together(late, early)
    late = lax.all_to_all(late, "freq", 0, 0, tiled=True)

    early = jnp.concatenate(halves(own_yl)) + early
    third, energy = early[slices : 2 * slices], early[3 * slices :]
    third_energy = jnp.concatenate([third, energy])
    back, forth, opposite = send(third_energy, dz=1), send(third_energy, dz=-1), send(energy, dz=2)
    fourth_plane = jnp.concatenate(
        [early[2 * slices : 3 * slices], energy, forth[slices:], opposite, back[slices:]]
    )
    late, fourth_plane = together(late, fourth_plane)
    sixth = jnp.sum(late[:, 2], 0)
    late = jnp.sum(late, 0)

    from_previous = send(late, dz=1)
    from_other = send(jnp.concatenate([late[1], fourth_plane]), dyh=1)
    from_diagonal = send(sixth, dyh=1, dz=-1)
    from_previous, from_other, from_diagonal = together(from_previous, from_other, from_diagonal)
    pieces = gathered(info, early, late, from_previous, back, forth, from_other, from_diagonal)
    found = lax.all_to_all(pieces, "freq", 0, 0, tiled=True).reshape(2 * rows, rows)
    swapped = send(lax.dynamic_slice_in_dim(found, (1 - core) * rows, rows, 0), dc=1)

    energies = jnp.concatenate([fourth_plane[slices:], from_other[2 * slices :]])
    energies_s = send(energies, dc=1)
    column_energy = [
        lax.dynamic_slice_in_dim(e, (step_y * 4 + step_z) * classes, classes, 0) for e in (energies, energies_s)
    ]
    column_energy = jnp.where(
        core == 0, jnp.concatenate(column_energy, 1), jnp.concatenate(column_energy[::-1], 1)
    )
    column_labels = lax.dynamic_slice_in_dim(labels, freq * 2 * rows, 2 * rows)
    row_side = jnp.zeros((rows, 2 * rows), jnp.float32)
    column_side = jnp.zeros((rows, 2 * rows), jnp.float32)
    for d in range(classes):
        row_side = jnp.where(column_labels[None, :] == d, energy[d][:, None], row_side)
        column_side = jnp.where(own_labels[:, None] == d, column_energy[d][None, :], column_side)
    root = jnp.sqrt(row_side * column_side + 1e-06)
    found, root = together(found, root)
    return finished(info, found, swapped, root)


def solution(mesh):
    placed = (P("blk", "freq"), P(), P(None, "freq"), P("freq"), P())
    return jax.shard_map(
        per_device, mesh=mesh, in_specs=placed, out_specs=P("blk", "freq"), check_vma=False
    )
```

```python
import jax
import jax.numpy as jnp
from jax import lax
from jax.experimental import pallas as pl
from jax.experimental.pallas import tpu as pltpu
from jax.sharding import PartitionSpec as P

BOTH = ("blk", "freq")
VMEM_BYTES = 60 * 1024 * 1024
LANES = 128
PARAMS = pltpu.CompilerParams(vmem_limit_bytes=VMEM_BYTES)
COST = pl.CostEstimate(flops=1024, bytes_accessed=1024, transcendentals=0)
VMEM = pl.BlockSpec(memory_space=pltpu.VMEM)
SMEM = pl.BlockSpec(memory_space=pltpu.SMEM)
ANY = pl.BlockSpec(memory_space=pl.ANY)


def places():
    return [
        (yh, z, c, f) for yh in range(2) for z in range(4) for c in range(2) for f in range(8)
    ]


def place_index(yh, z, c, f):
    return (((yh % 2) * 4 + z % 4) * 2 + c % 2) * 8 + f % 8


def route(dyh, dz, dc, dyl):
    return [
        (place_index(yh, z, c, f), place_index(yh + dyh, z + dz, c + dc, f + 4 * dyl))
        for yh, z, c, f in places()
    ]


def send(block, dyh=0, dz=0, dc=0, dyl=0):
    return lax.ppermute(block, BOTH, route(dyh, dz, dc, dyl))


def summed_along_x(tiles):
    groups = [list(range(4)), list(range(4, 8))]
    return jnp.sum(lax.all_to_all(tiles, "freq", 0, 0, axis_index_groups=groups, tiled=True), 0)


def together(*arrays):
    return lax.optimization_barrier(arrays)


def scaled(block, weight):
    return (block.astype(jnp.float32) * weight).astype(jnp.bfloat16)


def gram(a, b):
    return lax.dot_general(a, b, (((1,), (1,)), ((), ())), preferred_element_type=jnp.float32)


CORE, YH, Z, HIGH, NEXT_HIGH, PREV_HIGH, ON_B2, ON_B3, ON_B5, ON_B6, LOWER, LOW, ONE, BY_ROW = range(14)


def span(which, half):
    return pl.ds(pl.multiple_of(which * half, LANES), half)


def spread_pairs():
    place = lax.broadcasted_iota(jnp.int32, (LANES, 2 * LANES), 0)
    return (lax.broadcasted_iota(jnp.int32, (LANES, 2 * LANES), 1) // 2 == place).astype(jnp.bfloat16)


def mask_kernel(info, hot, spectra, wedges, own, to_partner, to_next, to_previous, pairs):
    half = spectra.shape[1] // 2

    @pl.when(pl.program_id(0) == 0)
    def _():
        spread = spread_pairs()
        for j in range(half // LANES):
            some = wedges[:, pl.ds(j * LANES, LANES)].astype(jnp.float32).astype(jnp.bfloat16)
            wide = jnp.dot(some, spread, preferred_element_type=jnp.float32)
            pairs[:, pl.ds(j * 2 * LANES, 2 * LANES)] = wide.astype(jnp.bfloat16)

    keep = jnp.dot(hot[...], pairs[...], preferred_element_type=jnp.float32).astype(jnp.bfloat16)
    own[...] = spectra[...] * keep
    to_partner[...] = own[:, span(1 - info[YH], half)]
    to_next[...] = own[:, span(info[NEXT_HIGH], half)]
    to_previous[...] = own[:, span(info[PREV_HIGH], half)]


def masked_blocks(info, hot, spectra, wedges):
    rows, width = spectra.shape
    classes = wedges.shape[0]
    part = rows // 4
    whole = lambda *shape: pl.BlockSpec(shape, lambda i, info: (0, 0))
    slab = lambda n: pl.BlockSpec((part, n), lambda i, info: (i, 0))
    half_block = jax.ShapeDtypeStruct((rows, width // 2), jnp.bfloat16)
    return pl.pallas_call(
        mask_kernel,
        grid_spec=pltpu.PrefetchScalarGridSpec(
            num_scalar_prefetch=1,
            grid=(4,),
            in_specs=[slab(classes), slab(width), whole(classes, width // 2)],
            out_specs=[slab(width)] + [slab(width // 2)] * 3 + [whole(classes, width)],
        ),
        out_shape=[
            jax.ShapeDtypeStruct((rows, width), jnp.bfloat16),
            *[half_block] * 3,
            jax.ShapeDtypeStruct((classes, width), jnp.bfloat16),
        ],
        compiler_params=PARAMS,
        cost_estimate=COST,
    )(info, hot, spectra, wedges)


def weight_kernel(shell_weight, shells, weight):
    spread = spread_pairs()

    def widen(x):
        return jnp.dot(x, spread, preferred_element_type=jnp.float32)

    for j in range(shells.shape[1] // LANES):
        shell = shells[:, pl.ds(j * LANES, LANES)]
        value = jnp.zeros(shell.shape, jnp.float32)
        for k in range(shell_weight.shape[0]):
            value = jnp.where(shell == k, shell_weight[k], value)
        top = value.astype(jnp.bfloat16)
        rest = value - top.astype(jnp.float32)
        middle = rest.astype(jnp.bfloat16)
        low = (rest - middle.astype(jnp.float32)).astype(jnp.bfloat16)
        weight[:, pl.ds(j * 2 * LANES, 2 * LANES)] = (widen(top) + widen(middle)) + widen(low)


def pair_weights(shell_weight, shells):
    return pl.pallas_call(
        weight_kernel,
        in_specs=[SMEM, VMEM],
        out_specs=VMEM,
        out_shape=jax.ShapeDtypeStruct((1, 2 * shells.shape[1]), jnp.float32),
        compiler_params=PARAMS,
        cost_estimate=COST,
    )(shell_weight, shells)


def first_kernel(info, own, sibling, weight, out, own_w, a, other, tiles, sems, out_sems):
    core = info[CORE]
    got_own = pltpu.make_async_copy(own, a.at[0], sems.at[0])
    got_sibling = pltpu.make_async_copy(sibling, other.at[0], sems.at[1])
    got_own.start()
    got_sibling.start()

    def leave(k, owner):
        copy = pltpu.make_async_copy(tiles.at[k], out.at[:, owner], out_sems.at[k])
        copy.start()
        return copy

    def put(k, tile):
        tiles[k] = tile.reshape(tiles.shape[1:])

    got_own.wait()
    a[1] = scaled(a[0], weight[...])
    left_w = pltpu.make_async_copy(a.at[1], own_w, out_sems.at[2])
    left_w.start()
    put(0, gram(a[1], a[0]))
    left_mine = leave(0, core)
    got_sibling.wait()

    @pl.when(core == 1)
    def _():
        other[1] = scaled(other[0], weight[...])

    put(1, gram(other[core], a[1 - core]))
    left_other = leave(1, 1 - core)
    left_w.wait()
    left_mine.wait()
    left_other.wait()


def first_tiles(info, own, sibling, weight):
    rows, width = own.shape
    block = pltpu.VMEM((2, rows, width), jnp.bfloat16)
    return pl.pallas_call(
        first_kernel,
        in_specs=[SMEM, ANY, ANY, VMEM],
        out_specs=[ANY, ANY],
        out_shape=[
            jax.ShapeDtypeStruct((4, 2, rows // 4, rows), jnp.float32),
            jax.ShapeDtypeStruct((rows, width), jnp.bfloat16),
        ],
        scratch_shapes=[
            block,
            block,
            pltpu.VMEM((2, 4, rows // 4, rows), jnp.float32),
            pltpu.SemaphoreType.DMA((2,)),
            pltpu.SemaphoreType.DMA((3,)),
        ],
        compiler_params=PARAMS,
        cost_estimate=COST,
    )(info, own, sibling, weight)


def half_kernel(jobs, info, *refs):
    operands, (weight, energy, out, a, b, tiles, sems, out_sems) = refs[:-8], refs[-8:]
    rows, half = b.shape[2:]
    slices = tiles.shape[3]
    core = info[CORE]
    sent = []

    def go(src, dst, n):
        copy = pltpu.make_async_copy(src, dst, out_sems.at[n])
        copy.start()
        sent.append(copy)

    def fetch(k, first_at, half_at):
        first, at = info[first_at] == 1, span(info[half_at], half)

        def pick(n, dst, yes, no):
            for chosen, src in ((first, yes), (jnp.logical_not(first), no)):
                src = src if src.shape[1] == half else src.at[:, at]

                @pl.when(chosen)
                def _(src=src):
                    pltpu.make_async_copy(src, dst, sems.at[k, n]).start()

            return pltpu.make_async_copy(src, dst, sems.at[k, n])

        a_yes, a_no, other_yes, other_no, b_yes, b_no = operands[6 * k : 6 * k + 6]
        got_b = pick(0, b.at[k, 0], b_yes, b_no)
        return got_b, [pick(1, a.at[k, 0], a_yes, a_no), pick(2, a.at[k, 2], other_yes, other_no)]

    got = [fetch(k, job[0], job[3]) for k, job in enumerate(jobs)]
    for k in range(len(jobs)):
        for x in range(4):
            go(energy, out.at[x, k, pl.ds(2 * slices, energy.shape[0])], 6 * k + 2 + x)
    for k, (_, on_b_at, on_b_other_at, half_at) in enumerate(jobs):
        got_b, got_a = got[k]
        w = weight[:, span(info[half_at], half)]
        got_b.wait()
        b[k, 1] = scaled(b[k, 0], w)
        for n, (on_b, owner) in enumerate(((info[on_b_at], core), (info[on_b_other_at], 1 - core))):
            got_a[n].wait()

            @pl.when(on_b == 0)
            def _(n=n, k=k, w=w):
                a[k, 2 * n + 1] = scaled(a[k, 2 * n], w)

            tiles[k, n] = gram(a[k, 2 * n + 1 - on_b], b[k, on_b]).reshape(tiles.shape[2:])
            go(tiles.at[k, n], out.at[:, k, pl.ds(pl.multiple_of(owner * slices, 8), slices)], 6 * k + n)
    for copy in sent:
        copy.wait()


def half_tiles(jobs, info, *operands):
    rows, classes = operands[0].shape[0], operands[-1].shape[0]
    half = operands[-2].shape[1] // 2

    def kernel(*refs):
        half_kernel(jobs, *refs)

    return pl.pallas_call(
        kernel,
        in_specs=[SMEM] + [ANY] * (len(operands) - 2) + [VMEM] * 2,
        out_specs=ANY,
        out_shape=jax.ShapeDtypeStruct((4, 2, rows // 2 + classes, rows), jnp.float32),
        scratch_shapes=[
            pltpu.VMEM((2, 4, rows, half), jnp.bfloat16),
            pltpu.VMEM((2, 2, rows, half), jnp.bfloat16),
            pltpu.VMEM((2, 2, 4, rows // 4, rows), jnp.float32),
            pltpu.SemaphoreType.DMA((2, 3)),
            pltpu.SemaphoreType.DMA((12,)),
        ],
        compiler_params=PARAMS,
        cost_estimate=COST,
    )(info, *operands)


def late_kernel(
    is_mine, info, own, own_w, partner_a, partner_b, a_high, a_low, mine_high, mine_low, diagonal, a_diagonal,
    weight, *rest,
):
    out, a, own_b, partner, sixth_a, sixth_b, tiles, sems, out_sems = rest[-9:]
    half = partner_a.shape[1]
    slices = out.shape[2]
    lower = info[YH] == 0
    high_is_yh = info[HIGH] == info[YH]
    high, yh = info[HIGH], info[YH]

    def pick(n, dst, *choices):
        for chosen, src in choices:

            @pl.when(chosen)
            def _(src=src):
                pltpu.make_async_copy(src, dst, sems.at[n]).start()

        return pltpu.make_async_copy(choices[0][1], dst, sems.at[n])

    always = info[CORE] >= 0
    no = jnp.logical_not
    got_b = pick(
        6,
        sixth_b,
        (lower, diagonal),
        (jnp.logical_and(no(lower), high_is_yh), mine_high),
        (jnp.logical_and(no(lower), no(high_is_yh)), mine_low),
    )
    got_a = pick(
        5,
        sixth_a,
        (no(lower), a_diagonal),
        (jnp.logical_and(lower, high_is_yh), a_high),
        (jnp.logical_and(lower, no(high_is_yh)), a_low),
    )
    got_high = pick(0, a.at[0, :, span(high, half)], (always, a_high))
    got_low = pick(1, a.at[0, :, span(1 - high, half)], (always, a_low))
    got_own = pick(2, own_b, (info[ON_B2] == 1, own_w), (info[ON_B2] == 0, own))
    got_near = pick(3, partner.at[:, span(yh, half)], (always, partner_a))
    got_far = pick(4, partner.at[:, span(1 - yh, half)], (always, partner_b))
    owner = info[CORE] if is_mine else 1 - info[CORE]
    sent = []

    def put(k, tile):
        tiles[k] = tile.reshape(4, slices, tile.shape[1])

    def leave(k):
        copy = pltpu.make_async_copy(tiles.at[k], out.at[pl.ds(owner * 4, 4), k], out_sems.at[k])
        copy.start()
        sent.append(copy)

    got_a.wait()
    got_b.wait()
    w_yh = weight[:, span(yh, half)]

    @pl.when(info[ON_B6] == 1)
    def _():
        sixth_b[...] = scaled(sixth_b[...], w_yh)

    @pl.when(info[ON_B6] == 0)
    def _():
        sixth_a[...] = scaled(sixth_a[...], w_yh)

    put(2, gram(sixth_a[...], sixth_b[...]))
    leave(2)
    got_high.wait()
    got_low.wait()
    a[1] = scaled(a[0], weight[...])
    got_own.wait()
    put(0, gram(a[1 - info[ON_B2]], own_b[...]))
    leave(0)
    got_near.wait()
    got_far.wait()

    @pl.when(info[ON_B5] == 1)
    def _():
        partner[...] = scaled(partner[...], weight[...])

    put(1, gram(a[1 - info[ON_B5]], partner[...]))
    leave(1)
    for copy in sent:
        copy.wait()


def late_tiles(is_mine, info, own, own_w, partner_a, partner_b, a_high, a_low, mine_high, mine_low, diagonal,
               a_diagonal, weight, other=None):
    rows, width = own.shape
    half = width // 2
    arrays = [own, own_w, partner_a, partner_b, a_high, a_low, mine_high, mine_low, diagonal, a_diagonal, weight]
    specs = [SMEM] + [ANY] * 10 + [VMEM]
    aliases = {}
    if other is not None:
        arrays.append(other)
        specs.append(ANY)
        aliases = {len(specs) - 1: 0}
    block = lambda n: pltpu.VMEM((rows, n), jnp.bfloat16)

    def kernel(*refs):
        late_kernel(is_mine, *refs)

    return pl.pallas_call(
        kernel,
        in_specs=specs,
        out_specs=ANY,
        out_shape=jax.ShapeDtypeStruct((8, 3, rows // 4, rows), jnp.float32),
        scratch_shapes=[
            pltpu.VMEM((2, rows, width), jnp.bfloat16),
            block(width),
            block(width),
            block(half),
            block(half),
            pltpu.VMEM((3, 4, rows // 4, rows), jnp.float32),
            pltpu.SemaphoreType.DMA((7,)),
            pltpu.SemaphoreType.DMA((3,)),
        ],
        input_output_aliases=aliases,
        compiler_params=PARAMS,
        cost_estimate=COST,
    )(info, *arrays)


def gather_kernel(info, early, late, from_previous, third_back, third_ahead, from_other, from_diagonal, out):
    yh, z = info[YH], info[Z]

    def put(dyh, dz, value):
        out[(yh + dyh) % 2 * 4 + (z + dz) % 4] = value

    slices = out.shape[1]
    put(0, 0, early[:slices])
    put(0, 1, late[0])
    put(0, 2, third_back[:slices] + third_ahead[:slices])
    put(0, 3, from_previous[0])
    put(1, 0, early[2 * slices : 3 * slices] + from_other[slices : 2 * slices])
    put(1, 1, from_other[:slices])
    put(1, 2, from_previous[2] + from_diagonal[...])
    put(1, 3, from_previous[1])


def gathered(info, *parts):
    slices, rows = parts[1].shape[1:]
    return pl.pallas_call(
        gather_kernel,
        in_specs=[SMEM] + [VMEM] * len(parts),
        out_specs=VMEM,
        out_shape=jax.ShapeDtypeStruct((8, slices, rows), jnp.float32),
    )(info, *parts)


def final_kernel(info, found, swapped, root, out):
    rows = swapped.shape[0]
    core, by_row = info[CORE], info[BY_ROW]

    for is_first in (True, False):

        @pl.when(jnp.logical_and(by_row == 1, (core == 0) == is_first))
        def _(is_first=is_first):
            kept = found[:rows] if is_first else found[rows:]
            pair = (kept, swapped[...]) if is_first else (swapped[...], kept)
            out[...] = jnp.concatenate(pair, 1) / root[...]

    @pl.when(by_row == 0)
    def _():
        out[...] = found[...].T / root[...]


def finished(info, found, swapped, root):
    return pl.pallas_call(
        final_kernel,
        in_specs=[SMEM, VMEM, VMEM, VMEM],
        out_specs=VMEM,
        out_shape=jax.ShapeDtypeStruct(root.shape, jnp.float32),
    )(info, found, swapped, root)


def per_device(spectra, labels, wedges, shells, shell_weight):
    rows, width = spectra.shape
    half, slices = width // 2, rows // 4
    classes = wedges.shape[0]
    blk = lax.axis_index("blk")
    core, z, yh = blk % 2, (blk // 2) % 4, blk // 8
    freq = lax.axis_index("freq")

    def place(dyh, dz):
        return ((yh + dyh) % 2) * 4 + (z + dz) % 4

    def ahead(a, b):
        return ((a - b) % 8 < 4).astype(jnp.int32)

    def columns(block, which):
        return lax.dynamic_slice_in_dim(block, which * half, half, 1)

    low, lower = z < 2, yh == 0
    high = z // 2
    previous_high = ((z + 3) % 4) // 2
    step_y, step_z = (freq // 4 + yh) % 2, (freq % 4 - z) % 4
    same_y = step_y == 0
    inner_z = jnp.logical_or(z == 1, z == 2)
    by_row = jnp.where(
        step_z == 0,
        jnp.logical_or(same_y, yh == 1),
        jnp.where(step_z == 1, False, jnp.where(step_z == 2, jnp.where(same_y, inner_z, lower), True)),
    )
    info = jnp.stack(
        [
            core,
            yh,
            z,
            high,
            ((z + 1) % 4) // 2,
            previous_high,
            ahead(place(0, 1), place(0, 0)),
            jnp.where(low, ahead(place(0, 1), place(0, -1)), ahead(place(0, -1), place(0, 1))),
            ahead(place(0, 1), place(1, 0)),
            jnp.where(lower, ahead(place(0, 1), place(1, -1)), ahead(place(1, -1), place(0, 1))),
            lower.astype(jnp.int32),
            low.astype(jnp.int32),
            jnp.int32(1),
            by_row.astype(jnp.int32),
        ]
    ).astype(jnp.int32)

    class_range = jnp.arange(classes, dtype=jnp.int32)
    own_labels = lax.dynamic_slice_in_dim(labels, blk * rows, rows)
    hot = (own_labels[:, None] == class_range[None, :]).astype(jnp.bfloat16)
    own, to_partner, to_next, to_previous, pairs = masked_blocks(info, hot, spectra, wedges)

    following_a = send(to_previous, dz=-1)
    partner_a = send(to_partner, dyh=1)
    previous = send(to_next, dz=1)
    sibling = send(own, dc=1)
    own, shells = together(own, shells)
    weight = pair_weights(shell_weight, shells[None, :])
    q1, own_w = first_tiles(info, own, sibling, weight)
    p1 = summed_along_x(q1)
    own_e, q1 = together(own, q1)
    squares = own_e.astype(jnp.float32) ** 2 * weight
    partial_energy = lax.dot_general(
        pairs.astype(jnp.float32), squares, (((1,), (1,)), ((), ())), precision=lax.Precision.HIGHEST
    )
    to_previous_b, to_partner_b = columns(own_e, 1 - previous_high), columns(own_e, yh)
    following_a, partner_a, previous, p1, partial_energy, to_previous_b, to_partner_b = together(
        following_a, partner_a, previous, p1, partial_energy, to_previous_b, to_partner_b
    )
    following_b = send(to_previous_b, dz=-1)
    partner_b = send(to_partner_b, dyh=1)
    diagonal = send(partner_a, dz=1)
    partner_s = send(partner_a, dc=1)
    third_a_s = send(jnp.where(low, following_a, previous), dc=1)
    half_pair = half_tiles(
        ((LOWER, ONE, CORE, YH), (LOW, ON_B3, ON_B3, HIGH)), info, partner_a, own, partner_s, sibling, own, partner_a,
        following_a, previous, third_a_s, third_a_s, previous, following_a, weight, partial_energy,
    )
    half_pair = summed_along_x(half_pair)
    following_b, partner_b, diagonal, half_pair = together(following_b, partner_b, diagonal, half_pair)

    own_yl = freq // 4

    def halves(which):
        return [
            lax.dynamic_index_in_dim(p1, which, 0, keepdims=False),
            lax.dynamic_slice_in_dim(half_pair[1], which * slices, slices, 0),
            lax.dynamic_slice_in_dim(half_pair[0], which * slices, slices, 0),
            half_pair[0, 2 * slices :],
        ]

    following_as = send(following_a, dc=1)
    following_bs = send(following_b, dc=1)
    diagonal_s = send(diagonal, dc=1)
    early = send(jnp.concatenate(halves(1 - own_yl)), dyl=1)
    late = late_tiles(
        True, info, own, own_w, partner_a, partner_b, following_a, following_b, following_a, following_b,
        diagonal, diagonal, weight,
    )
    late, following_as, following_bs, diagonal_s = together(late, following_as, following_bs, diagonal_s)
    late = late_tiles(
        False, info, own, own_w, partner_a, partner_b, following_as, following_bs, following_a, following_b,
        diagonal, diagonal_s, weight, late,
    )
    late, early = together(late, early)
    late = lax.all_to_all(late, "freq", 0, 0, tiled=True)

    early = jnp.concatenate(halves(own_yl)) + early
    third, energy = early[slices : 2 * slices], early[3 * slices :]
    third_energy = jnp.concatenate([third, energy])
    back, forth, opposite = send(third_energy, dz=1), send(third_energy, dz=-1), send(energy, dz=2)
    fourth_plane = jnp.concatenate(
        [early[2 * slices : 3 * slices], energy, forth[slices:], opposite, back[slices:]]
    )
    late, fourth_plane = together(late, fourth_plane)
    sixth = jnp.sum(late[:, 2], 0)
    late = jnp.sum(late, 0)

    from_previous = send(late, dz=1)
    from_other = send(jnp.concatenate([late[1], fourth_plane]), dyh=1)
    from_diagonal = send(sixth, dyh=1, dz=-1)
    from_previous, from_other, from_diagonal = together(from_previous, from_other, from_diagonal)
    pieces = gathered(info, early, late, from_previous, back, forth, from_other, from_diagonal)
    found = lax.all_to_all(pieces, "freq", 0, 0, tiled=True).reshape(2 * rows, rows)
    swapped = send(lax.dynamic_slice_in_dim(found, (1 - core) * rows, rows, 0), dc=1)

    energies = jnp.concatenate([fourth_plane[slices:], from_other[2 * slices :]])
    energies_s = send(energies, dc=1)
    column_energy = [
        lax.dynamic_slice_in_dim(e, (step_y * 4 + step_z) * classes, classes, 0) for e in (energies, energies_s)
    ]
    column_energy = jnp.where(
        core == 0, jnp.concatenate(column_energy, 1), jnp.concatenate(column_energy[::-1], 1)
    )
    column_labels = lax.dynamic_slice_in_dim(labels, freq * 2 * rows, 2 * rows)
    row_side = jnp.zeros((rows, 2 * rows), jnp.float32)
    column_side = jnp.zeros((rows, 2 * rows), jnp.float32)
    for d in range(classes):
        row_side = jnp.where(column_labels[None, :] == d, energy[d][:, None], row_side)
        column_side = jnp.where(own_labels[:, None] == d, column_energy[d][None, :], column_side)
    root = jnp.sqrt(row_side * column_side + 1e-06)
    found, root = together(found, root)
    return finished(info, found, swapped, root)


def solution(mesh):
    placed = (P("blk", "freq"), P(), P(None, "freq"), P("freq"), P())
    return jax.shard_map(
        per_device, mesh=mesh, in_specs=placed, out_specs=P("blk", "freq"), check_vma=False
    )
```

```python
import jax
import jax.numpy as jnp
from jax import lax
from jax.experimental import pallas as pl
from jax.experimental.pallas import tpu as pltpu
from jax.sharding import PartitionSpec as P

BOTH = ("blk", "freq")
VMEM_BYTES = 60 * 1024 * 1024
LANES = 128
PARAMS = pltpu.CompilerParams(vmem_limit_bytes=VMEM_BYTES)
COST = pl.CostEstimate(flops=1024, bytes_accessed=1024, transcendentals=0)
VMEM = pl.BlockSpec(memory_space=pltpu.VMEM)
SMEM = pl.BlockSpec(memory_space=pltpu.SMEM)
ANY = pl.BlockSpec(memory_space=pl.ANY)


def places():
    return [
        (yh, z, c, f) for yh in range(2) for z in range(4) for c in range(2) for f in range(8)
    ]


def place_index(yh, z, c, f):
    return (((yh % 2) * 4 + z % 4) * 2 + c % 2) * 8 + f % 8


def route(dyh, dz, dc, dyl, dx):
    return [
        (place_index(yh, z, c, f), place_index(yh + dyh, z + dz, c + dc, (f // 4 + dyl) * 4 + (f + dx) % 4))
        for yh, z, c, f in places()
    ]


def send(block, dyh=0, dz=0, dc=0, dyl=0, dx=0):
    return lax.ppermute(block, BOTH, route(dyh, dz, dc, dyl, dx))


def summed_along_x(tiles):
    groups = [list(range(4)), list(range(4, 8))]
    return jnp.sum(lax.all_to_all(tiles, "freq", 0, 0, axis_index_groups=groups, tiled=True), 0)


def together(*arrays):
    return lax.optimization_barrier(arrays)


def scaled(block, weight):
    return (block.astype(jnp.float32) * weight).astype(jnp.bfloat16)


def gram(a, b):
    return lax.dot_general(a, b, (((1,), (1,)), ((), ())), preferred_element_type=jnp.float32)


CORE, YH, Z, HIGH, NEXT_HIGH, PREV_HIGH, ON_B2, ON_B3, ON_B5, ON_B6, LOWER, LOW, ONE, BY_ROW, X = range(15)


def span(which, half):
    return pl.ds(pl.multiple_of(which * half, LANES), half)


def spread_pairs():
    place = lax.broadcasted_iota(jnp.int32, (LANES, 2 * LANES), 0)
    return (lax.broadcasted_iota(jnp.int32, (LANES, 2 * LANES), 1) // 2 == place).astype(jnp.bfloat16)


def mask_kernel(info, hot, spectra, wedges, own, to_partner, to_next, to_previous, pairs):
    half = spectra.shape[1] // 2

    @pl.when(pl.program_id(0) == 0)
    def _():
        spread = spread_pairs()
        for j in range(half // LANES):
            some = wedges[:, pl.ds(j * LANES, LANES)].astype(jnp.float32).astype(jnp.bfloat16)
            wide = jnp.dot(some, spread, preferred_element_type=jnp.float32)
            pairs[:, pl.ds(j * 2 * LANES, 2 * LANES)] = wide.astype(jnp.bfloat16)

    keep = jnp.dot(hot[...], pairs[...], preferred_element_type=jnp.float32).astype(jnp.bfloat16)
    own[...] = spectra[...] * keep
    to_partner[...] = own[:, span(1 - info[YH], half)]
    to_next[...] = own[:, span(info[NEXT_HIGH], half)]
    to_previous[...] = own[:, span(info[PREV_HIGH], half)]


def masked_blocks(info, hot, spectra, wedges):
    rows, width = spectra.shape
    classes = wedges.shape[0]
    part = rows // 4
    whole = lambda *shape: pl.BlockSpec(shape, lambda i, info: (0, 0))
    slab = lambda n: pl.BlockSpec((part, n), lambda i, info: (i, 0))
    half_block = jax.ShapeDtypeStruct((rows, width // 2), jnp.bfloat16)
    return pl.pallas_call(
        mask_kernel,
        grid_spec=pltpu.PrefetchScalarGridSpec(
            num_scalar_prefetch=1,
            grid=(4,),
            in_specs=[slab(classes), slab(width), whole(classes, width // 2)],
            out_specs=[slab(width)] + [slab(width // 2)] * 3 + [whole(classes, width)],
        ),
        out_shape=[
            jax.ShapeDtypeStruct((rows, width), jnp.bfloat16),
            *[half_block] * 3,
            jax.ShapeDtypeStruct((classes, width), jnp.bfloat16),
        ],
        compiler_params=PARAMS,
        cost_estimate=COST,
    )(info, hot, spectra, wedges)


def weight_kernel(shell_weight, shells, weight):
    spread = spread_pairs()

    def widen(x):
        return jnp.dot(x, spread, preferred_element_type=jnp.float32)

    for j in range(shells.shape[1] // LANES):
        shell = shells[:, pl.ds(j * LANES, LANES)]
        value = jnp.zeros(shell.shape, jnp.float32)
        for k in range(shell_weight.shape[0]):
            value = jnp.where(shell == k, shell_weight[k], value)
        top = value.astype(jnp.bfloat16)
        rest = value - top.astype(jnp.float32)
        middle = rest.astype(jnp.bfloat16)
        low = (rest - middle.astype(jnp.float32)).astype(jnp.bfloat16)
        weight[:, pl.ds(j * 2 * LANES, 2 * LANES)] = (widen(top) + widen(middle)) + widen(low)


def pair_weights(shell_weight, shells):
    return pl.pallas_call(
        weight_kernel,
        in_specs=[SMEM, VMEM],
        out_specs=VMEM,
        out_shape=jax.ShapeDtypeStruct((1, 2 * shells.shape[1]), jnp.float32),
        compiler_params=PARAMS,
        cost_estimate=COST,
    )(shell_weight, shells)


def first_kernel(info, own, sibling, weight, out, own_w, a, other, tiles, sems, out_sems):
    core = info[CORE]
    got_own = pltpu.make_async_copy(own, a.at[0], sems.at[0])
    got_sibling = pltpu.make_async_copy(sibling, other.at[0], sems.at[1])
    got_own.start()
    got_sibling.start()

    def leave(k, owner):
        copy = pltpu.make_async_copy(tiles.at[k], out.at[:, owner], out_sems.at[k])
        copy.start()
        return copy

    def put(k, tile):
        tiles[k] = tile.reshape(tiles.shape[1:])

    got_own.wait()
    a[1] = scaled(a[0], weight[...])
    left_w = pltpu.make_async_copy(a.at[1], own_w, out_sems.at[2])
    left_w.start()
    put(0, gram(a[1], a[0]))
    left_mine = leave(0, core)
    got_sibling.wait()

    @pl.when(core == 1)
    def _():
        other[1] = scaled(other[0], weight[...])

    put(1, gram(other[core], a[1 - core]))
    left_other = leave(1, 1 - core)
    left_w.wait()
    left_mine.wait()
    left_other.wait()


def first_tiles(info, own, sibling, weight):
    rows, width = own.shape
    block = pltpu.VMEM((2, rows, width), jnp.bfloat16)
    return pl.pallas_call(
        first_kernel,
        in_specs=[SMEM, ANY, ANY, VMEM],
        out_specs=[ANY, ANY],
        out_shape=[
            jax.ShapeDtypeStruct((4, 2, rows // 4, rows), jnp.float32),
            jax.ShapeDtypeStruct((rows, width), jnp.bfloat16),
        ],
        scratch_shapes=[
            block,
            block,
            pltpu.VMEM((2, 4, rows // 4, rows), jnp.float32),
            pltpu.SemaphoreType.DMA((2,)),
            pltpu.SemaphoreType.DMA((3,)),
        ],
        compiler_params=PARAMS,
        cost_estimate=COST,
    )(info, own, sibling, weight)


def half_kernel(jobs, info, *refs):
    operands, (weight, energy), outs, (a, b, tiles, sems, out_sems) = refs[:-11], refs[-11:-9], refs[-9:-5], refs[-5:]
    rows, half = b.shape[2:]
    slices = tiles.shape[3]
    core = info[CORE]
    sent = []

    def go(src, dst, n):
        copy = pltpu.make_async_copy(src, dst, out_sems.at[n])
        copy.start()
        sent.append(copy)

    def fetch(k, first_at, half_at):
        first, at = info[first_at] == 1, span(info[half_at], half)

        def pick(n, dst, yes, no):
            for chosen, src in ((first, yes), (jnp.logical_not(first), no)):
                src = src if src.shape[1] == half else src.at[:, at]

                @pl.when(chosen)
                def _(src=src):
                    pltpu.make_async_copy(src, dst, sems.at[k, n]).start()

            return pltpu.make_async_copy(src, dst, sems.at[k, n])

        a_yes, a_no, other_yes, other_no, b_yes, b_no = operands[6 * k : 6 * k + 6]
        got_b = pick(0, b.at[k, 0], b_yes, b_no)
        return got_b, [pick(1, a.at[k, 0], a_yes, a_no), pick(2, a.at[k, 2], other_yes, other_no)]

    got = [fetch(k, job[0], job[3]) for k, job in enumerate(jobs)]
    for k in range(len(jobs)):
        for x in range(4):
            go(energy, outs[x].at[k, pl.ds(2 * slices, energy.shape[0])], 12 * k + 8 + x)
    for k, (_, on_b_at, on_b_other_at, half_at) in enumerate(jobs):
        got_b, got_a = got[k]
        w = weight[:, span(info[half_at], half)]
        got_b.wait()
        b[k, 1] = scaled(b[k, 0], w)
        for n, (on_b, owner) in enumerate(((info[on_b_at], core), (info[on_b_other_at], 1 - core))):
            got_a[n].wait()

            @pl.when(on_b == 0)
            def _(n=n, k=k, w=w):
                a[k, 2 * n + 1] = scaled(a[k, 2 * n], w)

            tiles[k, n] = gram(a[k, 2 * n + 1 - on_b], b[k, on_b]).reshape(tiles.shape[2:])
            at = pl.ds(pl.multiple_of(owner * slices, 8), slices)
            for x in range(4):
                go(tiles.at[k, n, (info[X] + x) % 4], outs[x].at[k, at], 12 * k + 4 * n + x)
    for copy in sent:
        copy.wait()


def half_tiles(jobs, info, *operands):
    rows, classes = operands[0].shape[0], operands[-1].shape[0]
    half = operands[-2].shape[1] // 2

    def kernel(*refs):
        half_kernel(jobs, *refs)

    return pl.pallas_call(
        kernel,
        in_specs=[SMEM] + [ANY] * (len(operands) - 2) + [VMEM] * 2,
        out_specs=[ANY] * 4,
        out_shape=[jax.ShapeDtypeStruct((2, rows // 2 + classes, rows), jnp.float32)] * 4,
        scratch_shapes=[
            pltpu.VMEM((2, 4, rows, half), jnp.bfloat16),
            pltpu.VMEM((2, 2, rows, half), jnp.bfloat16),
            pltpu.VMEM((2, 2, 4, rows // 4, rows), jnp.float32),
            pltpu.SemaphoreType.DMA((2, 3)),
            pltpu.SemaphoreType.DMA((24,)),
        ],
        compiler_params=PARAMS,
        cost_estimate=COST,
    )(info, *operands)


def late_kernel(
    is_mine, info, own, own_w, partner_a, partner_b, a_high, a_low, mine_high, mine_low, diagonal, a_diagonal,
    weight, *rest,
):
    out, a, own_b, partner, sixth_a, sixth_b, tiles, sems, out_sems = rest[-9:]
    half = partner_a.shape[1]
    slices = out.shape[2]
    lower = info[YH] == 0
    high_is_yh = info[HIGH] == info[YH]
    high, yh = info[HIGH], info[YH]

    def pick(n, dst, *choices):
        for chosen, src in choices:

            @pl.when(chosen)
            def _(src=src):
                pltpu.make_async_copy(src, dst, sems.at[n]).start()

        return pltpu.make_async_copy(choices[0][1], dst, sems.at[n])

    always = info[CORE] >= 0
    no = jnp.logical_not
    got_b = pick(
        6,
        sixth_b,
        (lower, diagonal),
        (jnp.logical_and(no(lower), high_is_yh), mine_high),
        (jnp.logical_and(no(lower), no(high_is_yh)), mine_low),
    )
    got_a = pick(
        5,
        sixth_a,
        (no(lower), a_diagonal),
        (jnp.logical_and(lower, high_is_yh), a_high),
        (jnp.logical_and(lower, no(high_is_yh)), a_low),
    )
    got_high = pick(0, a.at[0, :, span(high, half)], (always, a_high))
    got_low = pick(1, a.at[0, :, span(1 - high, half)], (always, a_low))
    got_own = pick(2, own_b, (info[ON_B2] == 1, own_w), (info[ON_B2] == 0, own))
    got_near = pick(3, partner.at[:, span(yh, half)], (always, partner_a))
    got_far = pick(4, partner.at[:, span(1 - yh, half)], (always, partner_b))
    owner = info[CORE] if is_mine else 1 - info[CORE]
    sent = []

    def put(k, tile):
        tiles[k] = tile.reshape(4, slices, tile.shape[1])

    def leave(k):
        copy = pltpu.make_async_copy(tiles.at[k], out.at[pl.ds(owner * 4, 4), k], out_sems.at[k])
        copy.start()
        sent.append(copy)

    got_a.wait()
    got_b.wait()
    w_yh = weight[:, span(yh, half)]

    @pl.when(info[ON_B6] == 1)
    def _():
        sixth_b[...] = scaled(sixth_b[...], w_yh)

    @pl.when(info[ON_B6] == 0)
    def _():
        sixth_a[...] = scaled(sixth_a[...], w_yh)

    put(2, gram(sixth_a[...], sixth_b[...]))
    leave(2)
    got_high.wait()
    got_low.wait()
    a[1] = scaled(a[0], weight[...])
    got_own.wait()
    put(0, gram(a[1 - info[ON_B2]], own_b[...]))
    leave(0)
    got_near.wait()
    got_far.wait()

    @pl.when(info[ON_B5] == 1)
    def _():
        partner[...] = scaled(partner[...], weight[...])

    put(1, gram(a[1 - info[ON_B5]], partner[...]))
    leave(1)
    for copy in sent:
        copy.wait()


def late_tiles(is_mine, info, own, own_w, partner_a, partner_b, a_high, a_low, mine_high, mine_low, diagonal,
               a_diagonal, weight, other=None):
    rows, width = own.shape
    half = width // 2
    arrays = [own, own_w, partner_a, partner_b, a_high, a_low, mine_high, mine_low, diagonal, a_diagonal, weight]
    specs = [SMEM] + [ANY] * 10 + [VMEM]
    aliases = {}
    if other is not None:
        arrays.append(other)
        specs.append(ANY)
        aliases = {len(specs) - 1: 0}
    block = lambda n: pltpu.VMEM((rows, n), jnp.bfloat16)

    def kernel(*refs):
        late_kernel(is_mine, *refs)

    return pl.pallas_call(
        kernel,
        in_specs=specs,
        out_specs=ANY,
        out_shape=jax.ShapeDtypeStruct((8, 3, rows // 4, rows), jnp.float32),
        scratch_shapes=[
            pltpu.VMEM((2, rows, width), jnp.bfloat16),
            block(width),
            block(width),
            block(half),
            block(half),
            pltpu.VMEM((3, 4, rows // 4, rows), jnp.float32),
            pltpu.SemaphoreType.DMA((7,)),
            pltpu.SemaphoreType.DMA((3,)),
        ],
        input_output_aliases=aliases,
        compiler_params=PARAMS,
        cost_estimate=COST,
    )(info, *arrays)


def gather_kernel(info, early, late, from_previous, third_back, third_ahead, from_other, from_diagonal, out):
    yh, z = info[YH], info[Z]

    def put(dyh, dz, value):
        out[(yh + dyh) % 2 * 4 + (z + dz) % 4] = value

    slices = out.shape[1]
    put(0, 0, early[:slices])
    put(0, 1, late[0])
    put(0, 2, third_back[:slices] + third_ahead[:slices])
    put(0, 3, from_previous[0])
    put(1, 0, early[2 * slices : 3 * slices] + from_other[slices : 2 * slices])
    put(1, 1, from_other[:slices])
    put(1, 2, from_previous[2] + from_diagonal[...])
    put(1, 3, from_previous[1])


def gathered(info, *parts):
    slices, rows = parts[1].shape[1:]
    return pl.pallas_call(
        gather_kernel,
        in_specs=[SMEM] + [VMEM] * len(parts),
        out_specs=VMEM,
        out_shape=jax.ShapeDtypeStruct((8, slices, rows), jnp.float32),
    )(info, *parts)


def final_kernel(info, found, swapped, root, out):
    rows = swapped.shape[0]
    core, by_row = info[CORE], info[BY_ROW]

    for is_first in (True, False):

        @pl.when(jnp.logical_and(by_row == 1, (core == 0) == is_first))
        def _(is_first=is_first):
            kept = found[:rows] if is_first else found[rows:]
            pair = (kept, swapped[...]) if is_first else (swapped[...], kept)
            out[...] = jnp.concatenate(pair, 1) / root[...]

    @pl.when(by_row == 0)
    def _():
        out[...] = found[...].T / root[...]


def finished(info, found, swapped, root):
    return pl.pallas_call(
        final_kernel,
        in_specs=[SMEM, VMEM, VMEM, VMEM],
        out_specs=VMEM,
        out_shape=jax.ShapeDtypeStruct(root.shape, jnp.float32),
    )(info, found, swapped, root)


def per_device(spectra, labels, wedges, shells, shell_weight):
    rows, width = spectra.shape
    half, slices = width // 2, rows // 4
    classes = wedges.shape[0]
    blk = lax.axis_index("blk")
    core, z, yh = blk % 2, (blk // 2) % 4, blk // 8
    freq = lax.axis_index("freq")

    def place(dyh, dz):
        return ((yh + dyh) % 2) * 4 + (z + dz) % 4

    def ahead(a, b):
        return ((a - b) % 8 < 4).astype(jnp.int32)

    def columns(block, which):
        return lax.dynamic_slice_in_dim(block, which * half, half, 1)

    low, lower = z < 2, yh == 0
    high = z // 2
    previous_high = ((z + 3) % 4) // 2
    step_y, step_z = (freq // 4 + yh) % 2, (freq % 4 - z) % 4
    same_y = step_y == 0
    inner_z = jnp.logical_or(z == 1, z == 2)
    by_row = jnp.where(
        step_z == 0,
        jnp.logical_or(same_y, yh == 1),
        jnp.where(step_z == 1, False, jnp.where(step_z == 2, jnp.where(same_y, inner_z, lower), True)),
    )
    info = jnp.stack(
        [
            core,
            yh,
            z,
            high,
            ((z + 1) % 4) // 2,
            previous_high,
            ahead(place(0, 1), place(0, 0)),
            jnp.where(low, ahead(place(0, 1), place(0, -1)), ahead(place(0, -1), place(0, 1))),
            ahead(place(0, 1), place(1, 0)),
            jnp.where(lower, ahead(place(0, 1), place(1, -1)), ahead(place(1, -1), place(0, 1))),
            lower.astype(jnp.int32),
            low.astype(jnp.int32),
            jnp.int32(1),
            by_row.astype(jnp.int32),
            freq % 4,
        ]
    ).astype(jnp.int32)

    class_range = jnp.arange(classes, dtype=jnp.int32)
    own_labels = lax.dynamic_slice_in_dim(labels, blk * rows, rows)
    hot = (own_labels[:, None] == class_range[None, :]).astype(jnp.bfloat16)
    own, to_partner, to_next, to_previous, pairs = masked_blocks(info, hot, spectra, wedges)

    following_a = send(to_previous, dz=-1)
    partner_a = send(to_partner, dyh=1)
    previous = send(to_next, dz=1)
    sibling = send(own, dc=1)
    own, shells = together(own, shells)
    weight = pair_weights(shell_weight, shells[None, :])
    q1, own_w = first_tiles(info, own, sibling, weight)
    p1 = summed_along_x(q1)
    own_e, q1 = together(own, q1)
    squares = own_e.astype(jnp.float32) ** 2 * weight
    partial_energy = lax.dot_general(
        pairs.astype(jnp.float32), squares, (((1,), (1,)), ((), ())), precision=lax.Precision.HIGHEST
    )
    to_previous_b, to_partner_b = columns(own_e, 1 - previous_high), columns(own_e, yh)
    following_a, partner_a, previous, p1, partial_energy, to_previous_b, to_partner_b = together(
        following_a, partner_a, previous, p1, partial_energy, to_previous_b, to_partner_b
    )
    following_b = send(to_previous_b, dz=-1)
    partner_b = send(to_partner_b, dyh=1)
    diagonal = send(partner_a, dz=1)
    partner_s = send(partner_a, dc=1)
    third_a_s = send(jnp.where(low, following_a, previous), dc=1)
    half_pair = half_tiles(
        ((LOWER, ONE, CORE, YH), (LOW, ON_B3, ON_B3, HIGH)), info, partner_a, own, partner_s, sibling, own, partner_a,
        following_a, previous, third_a_s, third_a_s, previous, following_a, weight, partial_energy,
    )
    half_pair = half_pair[0] + send(half_pair[1], dx=1) + send(half_pair[2], dx=2) + send(half_pair[3], dx=-1)
    following_b, partner_b, diagonal, half_pair = together(following_b, partner_b, diagonal, half_pair)

    own_yl = freq // 4

    def halves(which):
        return [
            lax.dynamic_index_in_dim(p1, which, 0, keepdims=False),
            lax.dynamic_slice_in_dim(half_pair[1], which * slices, slices, 0),
            lax.dynamic_slice_in_dim(half_pair[0], which * slices, slices, 0),
            half_pair[0, 2 * slices :],
        ]

    following_as = send(following_a, dc=1)
    following_bs = send(following_b, dc=1)
    diagonal_s = send(diagonal, dc=1)
    early = send(jnp.concatenate(halves(1 - own_yl)), dyl=1)
    late = late_tiles(
        True, info, own, own_w, partner_a, partner_b, following_a, following_b, following_a, following_b,
        diagonal, diagonal, weight,
    )
    late, following_as, following_bs, diagonal_s = together(late, following_as, following_bs, diagonal_s)
    late = late_tiles(
        False, info, own, own_w, partner_a, partner_b, following_as, following_bs, following_a, following_b,
        diagonal, diagonal_s, weight, late,
    )
    late, early = together(late, early)
    late = lax.all_to_all(late, "freq", 0, 0, tiled=True)

    early = jnp.concatenate(halves(own_yl)) + early
    third, energy = early[slices : 2 * slices], early[3 * slices :]
    third_energy = jnp.concatenate([third, energy])
    back, forth, opposite = send(third_energy, dz=1), send(third_energy, dz=-1), send(energy, dz=2)
    fourth_plane = jnp.concatenate(
        [early[2 * slices : 3 * slices], energy, forth[slices:], opposite, back[slices:]]
    )
    late, fourth_plane = together(late, fourth_plane)
    sixth = jnp.sum(late[:, 2], 0)
    late = jnp.sum(late, 0)

    from_previous = send(late, dz=1)
    from_other = send(jnp.concatenate([late[1], fourth_plane]), dyh=1)
    from_diagonal = send(sixth, dyh=1, dz=-1)
    from_previous, from_other, from_diagonal = together(from_previous, from_other, from_diagonal)
    pieces = gathered(info, early, late, from_previous, back, forth, from_other, from_diagonal)
    found = lax.all_to_all(pieces, "freq", 0, 0, tiled=True).reshape(2 * rows, rows)
    swapped = send(lax.dynamic_slice_in_dim(found, (1 - core) * rows, rows, 0), dc=1)

    energies = jnp.concatenate([fourth_plane[slices:], from_other[2 * slices :]])
    energies_s = send(energies, dc=1)
    column_energy = [
        lax.dynamic_slice_in_dim(e, (step_y * 4 + step_z) * classes, classes, 0) for e in (energies, energies_s)
    ]
    column_energy = jnp.where(
        core == 0, jnp.concatenate(column_energy, 1), jnp.concatenate(column_energy[::-1], 1)
    )
    labels, pieces = together(labels, pieces)
    own_labels = lax.dynamic_slice_in_dim(labels, blk * rows, rows)
    column_labels = lax.dynamic_slice_in_dim(labels, freq * 2 * rows, 2 * rows)
    row_side = jnp.zeros((rows, 2 * rows), jnp.float32)
    column_side = jnp.zeros((rows, 2 * rows), jnp.float32)
    for d in range(classes):
        row_side = jnp.where(column_labels[None, :] == d, energy[d][:, None], row_side)
        column_side = jnp.where(own_labels[:, None] == d, column_energy[d][None, :], column_side)
    root = jnp.sqrt(row_side * column_side + 1e-06)
    found, root = together(found, root)
    return finished(info, found, swapped, root)


def solution(mesh):
    placed = (P("blk", "freq"), P(), P(None, "freq"), P("freq"), P())
    return jax.shard_map(
        per_device, mesh=mesh, in_specs=placed, out_specs=P("blk", "freq"), check_vma=False
    )
```

```python
import jax
import jax.numpy as jnp
from jax import lax
from jax.experimental import pallas as pl
from jax.experimental.pallas import tpu as pltpu
from jax.sharding import PartitionSpec as P

BOTH = ("blk", "freq")
VMEM_BYTES = 60 * 1024 * 1024
LANES = 128
PARAMS = pltpu.CompilerParams(vmem_limit_bytes=VMEM_BYTES)
COST = pl.CostEstimate(flops=1024, bytes_accessed=1024, transcendentals=0)
VMEM = pl.BlockSpec(memory_space=pltpu.VMEM)
SMEM = pl.BlockSpec(memory_space=pltpu.SMEM)
ANY = pl.BlockSpec(memory_space=pl.ANY)


def places():
    return [
        (yh, z, c, f) for yh in range(2) for z in range(4) for c in range(2) for f in range(8)
    ]


def place_index(yh, z, c, f):
    return (((yh % 2) * 4 + z % 4) * 2 + c % 2) * 8 + f % 8


def route(dyh, dz, dc, dyl, dx):
    return [
        (place_index(yh, z, c, f), place_index(yh + dyh, z + dz, c + dc, (f // 4 + dyl) * 4 + (f + dx) % 4))
        for yh, z, c, f in places()
    ]


def send(block, dyh=0, dz=0, dc=0, dyl=0, dx=0):
    return lax.ppermute(block, BOTH, route(dyh, dz, dc, dyl, dx))


def summed_along_x(tiles):
    groups = [list(range(4)), list(range(4, 8))]
    return jnp.sum(lax.all_to_all(tiles, "freq", 0, 0, axis_index_groups=groups, tiled=True), 0)


def together(*arrays):
    return lax.optimization_barrier(arrays)


def scaled(block, weight):
    return (block.astype(jnp.float32) * weight).astype(jnp.bfloat16)


def gram(a, b):
    return lax.dot_general(a, b, (((1,), (1,)), ((), ())), preferred_element_type=jnp.float32)


CORE, YH, Z, HIGH, NEXT_HIGH, PREV_HIGH, ON_B2, ON_B3, ON_B5, ON_B6, LOWER, LOW, ONE, BY_ROW, X = range(15)


def span(which, half):
    return pl.ds(pl.multiple_of(which * half, LANES), half)


def spread_pairs():
    place = lax.broadcasted_iota(jnp.int32, (LANES, 2 * LANES), 0)
    return (lax.broadcasted_iota(jnp.int32, (LANES, 2 * LANES), 1) // 2 == place).astype(jnp.bfloat16)


def mask_kernel(info, hot, spectra, wedges, own, to_partner, to_next, to_previous, pairs):
    half = spectra.shape[1] // 2

    @pl.when(pl.program_id(0) == 0)
    def _():
        spread = spread_pairs()
        for j in range(half // LANES):
            some = wedges[:, pl.ds(j * LANES, LANES)].astype(jnp.float32).astype(jnp.bfloat16)
            wide = jnp.dot(some, spread, preferred_element_type=jnp.float32)
            pairs[:, pl.ds(j * 2 * LANES, 2 * LANES)] = wide.astype(jnp.bfloat16)

    keep = jnp.dot(hot[...], pairs[...], preferred_element_type=jnp.float32).astype(jnp.bfloat16)
    own[...] = spectra[...] * keep
    to_partner[...] = own[:, span(1 - info[YH], half)]
    to_next[...] = own[:, span(info[NEXT_HIGH], half)]
    to_previous[...] = own[:, span(info[PREV_HIGH], half)]


def masked_blocks(info, hot, spectra, wedges):
    rows, width = spectra.shape
    classes = wedges.shape[0]
    part = rows // 4
    whole = lambda *shape: pl.BlockSpec(shape, lambda i, info: (0, 0))
    slab = lambda n: pl.BlockSpec((part, n), lambda i, info: (i, 0))
    half_block = jax.ShapeDtypeStruct((rows, width // 2), jnp.bfloat16)
    return pl.pallas_call(
        mask_kernel,
        grid_spec=pltpu.PrefetchScalarGridSpec(
            num_scalar_prefetch=1,
            grid=(4,),
            in_specs=[slab(classes), slab(width), whole(classes, width // 2)],
            out_specs=[slab(width)] + [slab(width // 2)] * 3 + [whole(classes, width)],
        ),
        out_shape=[
            jax.ShapeDtypeStruct((rows, width), jnp.bfloat16),
            *[half_block] * 3,
            jax.ShapeDtypeStruct((classes, width), jnp.bfloat16),
        ],
        compiler_params=PARAMS,
        cost_estimate=COST,
    )(info, hot, spectra, wedges)


def weight_kernel(shell_weight, shells, weight):
    spread = spread_pairs()

    def widen(x):
        return jnp.dot(x, spread, preferred_element_type=jnp.float32)

    for j in range(shells.shape[1] // LANES):
        shell = shells[:, pl.ds(j * LANES, LANES)]
        value = jnp.zeros(shell.shape, jnp.float32)
        for k in range(shell_weight.shape[0]):
            value = jnp.where(shell == k, shell_weight[k], value)
        top = value.astype(jnp.bfloat16)
        rest = value - top.astype(jnp.float32)
        middle = rest.astype(jnp.bfloat16)
        low = (rest - middle.astype(jnp.float32)).astype(jnp.bfloat16)
        weight[:, pl.ds(j * 2 * LANES, 2 * LANES)] = (widen(top) + widen(middle)) + widen(low)


def pair_weights(shell_weight, shells):
    return pl.pallas_call(
        weight_kernel,
        in_specs=[SMEM, VMEM],
        out_specs=VMEM,
        out_shape=jax.ShapeDtypeStruct((1, 2 * shells.shape[1]), jnp.float32),
        compiler_params=PARAMS,
        cost_estimate=COST,
    )(shell_weight, shells)


def first_kernel(info, own, sibling, weight, out, own_w, a, other, tiles, sems, out_sems):
    core = info[CORE]
    got_own = pltpu.make_async_copy(own, a.at[0], sems.at[0])
    got_sibling = pltpu.make_async_copy(sibling, other.at[0], sems.at[1])
    got_own.start()
    got_sibling.start()

    def leave(k, owner):
        copy = pltpu.make_async_copy(tiles.at[k], out.at[:, owner], out_sems.at[k])
        copy.start()
        return copy

    def put(k, tile):
        tiles[k] = tile.reshape(tiles.shape[1:])

    got_own.wait()
    a[1] = scaled(a[0], weight[...])
    left_w = pltpu.make_async_copy(a.at[1], own_w, out_sems.at[2])
    left_w.start()
    put(0, gram(a[1], a[0]))
    left_mine = leave(0, core)
    got_sibling.wait()

    @pl.when(core == 1)
    def _():
        other[1] = scaled(other[0], weight[...])

    put(1, gram(other[core], a[1 - core]))
    left_other = leave(1, 1 - core)
    left_w.wait()
    left_mine.wait()
    left_other.wait()


def first_tiles(info, own, sibling, weight):
    rows, width = own.shape
    block = pltpu.VMEM((2, rows, width), jnp.bfloat16)
    return pl.pallas_call(
        first_kernel,
        in_specs=[SMEM, ANY, ANY, VMEM],
        out_specs=[ANY, ANY],
        out_shape=[
            jax.ShapeDtypeStruct((4, 2, rows // 4, rows), jnp.float32),
            jax.ShapeDtypeStruct((rows, width), jnp.bfloat16),
        ],
        scratch_shapes=[
            block,
            block,
            pltpu.VMEM((2, 4, rows // 4, rows), jnp.float32),
            pltpu.SemaphoreType.DMA((2,)),
            pltpu.SemaphoreType.DMA((3,)),
        ],
        compiler_params=PARAMS,
        cost_estimate=COST,
    )(info, own, sibling, weight)


def half_kernel(jobs, info, *refs):
    operands, (weight, energy), outs, (a, b, tiles, sems, out_sems) = refs[:-11], refs[-11:-9], refs[-9:-5], refs[-5:]
    rows, half = b.shape[2:]
    slices = tiles.shape[3]
    core = info[CORE]
    sent = []

    def go(src, dst, n):
        copy = pltpu.make_async_copy(src, dst, out_sems.at[n])
        copy.start()
        sent.append(copy)

    def fetch(k, first_at, half_at):
        first, at = info[first_at] == 1, span(info[half_at], half)

        def pick(n, dst, yes, no):
            for chosen, src in ((first, yes), (jnp.logical_not(first), no)):
                src = src if src.shape[1] == half else src.at[:, at]

                @pl.when(chosen)
                def _(src=src):
                    pltpu.make_async_copy(src, dst, sems.at[k, n]).start()

            return pltpu.make_async_copy(src, dst, sems.at[k, n])

        a_yes, a_no, other_yes, other_no, b_yes, b_no = operands[6 * k : 6 * k + 6]
        got_b = pick(0, b.at[k, 0], b_yes, b_no)
        return got_b, [pick(1, a.at[k, 0], a_yes, a_no), pick(2, a.at[k, 2], other_yes, other_no)]

    got = [fetch(k, job[0], job[3]) for k, job in enumerate(jobs)]
    for k in range(len(jobs)):
        for x in range(4):
            go(energy, outs[x].at[k, pl.ds(2 * slices, energy.shape[0])], 12 * k + 8 + x)
    for k, (_, on_b_at, on_b_other_at, half_at) in enumerate(jobs):
        got_b, got_a = got[k]
        w = weight[:, span(info[half_at], half)]
        got_b.wait()
        b[k, 1] = scaled(b[k, 0], w)
        for n, (on_b, owner) in enumerate(((info[on_b_at], core), (info[on_b_other_at], 1 - core))):
            got_a[n].wait()

            @pl.when(on_b == 0)
            def _(n=n, k=k, w=w):
                a[k, 2 * n + 1] = scaled(a[k, 2 * n], w)

            tiles[k, n] = gram(a[k, 2 * n + 1 - on_b], b[k, on_b]).reshape(tiles.shape[2:])
            at = pl.ds(pl.multiple_of(owner * slices, 8), slices)
            for x in range(4):
                go(tiles.at[k, n, (info[X] + x) % 4], outs[x].at[k, at], 12 * k + 4 * n + x)
    for copy in sent:
        copy.wait()


def half_tiles(jobs, info, *operands):
    rows, classes = operands[0].shape[0], operands[-1].shape[0]
    half = operands[-2].shape[1] // 2

    def kernel(*refs):
        half_kernel(jobs, *refs)

    return pl.pallas_call(
        kernel,
        in_specs=[SMEM] + [ANY] * (len(operands) - 2) + [VMEM] * 2,
        out_specs=[ANY] * 4,
        out_shape=[jax.ShapeDtypeStruct((2, rows // 2 + classes, rows), jnp.float32)] * 4,
        scratch_shapes=[
            pltpu.VMEM((2, 4, rows, half), jnp.bfloat16),
            pltpu.VMEM((2, 2, rows, half), jnp.bfloat16),
            pltpu.VMEM((2, 2, 4, rows // 4, rows), jnp.float32),
            pltpu.SemaphoreType.DMA((2, 3)),
            pltpu.SemaphoreType.DMA((24,)),
        ],
        compiler_params=PARAMS,
        cost_estimate=COST,
    )(info, *operands)


def late_kernel(
    is_mine, info, own, own_w, partner_a, partner_b, a_high, a_low, mine_high, mine_low, diagonal, a_diagonal,
    weight, *rest,
):
    out, a, own_b, partner, sixth_a, sixth_b, tiles, sems, out_sems = rest[-9:]
    half = partner_a.shape[1]
    slices = out.shape[2]
    lower = info[YH] == 0
    high_is_yh = info[HIGH] == info[YH]
    high, yh = info[HIGH], info[YH]

    def pick(n, dst, *choices):
        for chosen, src in choices:

            @pl.when(chosen)
            def _(src=src):
                pltpu.make_async_copy(src, dst, sems.at[n]).start()

        return pltpu.make_async_copy(choices[0][1], dst, sems.at[n])

    always = info[CORE] >= 0
    no = jnp.logical_not
    got_b = pick(
        6,
        sixth_b,
        (lower, diagonal),
        (jnp.logical_and(no(lower), high_is_yh), mine_high),
        (jnp.logical_and(no(lower), no(high_is_yh)), mine_low),
    )
    got_a = pick(
        5,
        sixth_a,
        (no(lower), a_diagonal),
        (jnp.logical_and(lower, high_is_yh), a_high),
        (jnp.logical_and(lower, no(high_is_yh)), a_low),
    )
    got_high = pick(0, a.at[0, :, span(high, half)], (always, a_high))
    got_low = pick(1, a.at[0, :, span(1 - high, half)], (always, a_low))
    got_own = pick(2, own_b, (info[ON_B2] == 1, own_w), (info[ON_B2] == 0, own))
    got_near = pick(3, partner.at[:, span(yh, half)], (always, partner_a))
    got_far = pick(4, partner.at[:, span(1 - yh, half)], (always, partner_b))
    owner = info[CORE] if is_mine else 1 - info[CORE]
    sent = []

    def put(k, tile):
        tiles[k] = tile.reshape(4, slices, tile.shape[1])

    def leave(k):
        copy = pltpu.make_async_copy(tiles.at[k], out.at[pl.ds(owner * 4, 4), k], out_sems.at[k])
        copy.start()
        sent.append(copy)

    got_a.wait()
    got_b.wait()
    w_yh = weight[:, span(yh, half)]

    @pl.when(info[ON_B6] == 1)
    def _():
        sixth_b[...] = scaled(sixth_b[...], w_yh)

    @pl.when(info[ON_B6] == 0)
    def _():
        sixth_a[...] = scaled(sixth_a[...], w_yh)

    put(2, gram(sixth_a[...], sixth_b[...]))
    leave(2)
    got_high.wait()
    got_low.wait()
    a[1] = scaled(a[0], weight[...])
    got_own.wait()
    put(0, gram(a[1 - info[ON_B2]], own_b[...]))
    leave(0)
    got_near.wait()
    got_far.wait()

    @pl.when(info[ON_B5] == 1)
    def _():
        partner[...] = scaled(partner[...], weight[...])

    put(1, gram(a[1 - info[ON_B5]], partner[...]))
    leave(1)
    for copy in sent:
        copy.wait()


def late_tiles(is_mine, info, own, own_w, partner_a, partner_b, a_high, a_low, mine_high, mine_low, diagonal,
               a_diagonal, weight, other=None):
    rows, width = own.shape
    half = width // 2
    arrays = [own, own_w, partner_a, partner_b, a_high, a_low, mine_high, mine_low, diagonal, a_diagonal, weight]
    specs = [SMEM] + [ANY] * 10 + [VMEM]
    aliases = {}
    if other is not None:
        arrays.append(other)
        specs.append(ANY)
        aliases = {len(specs) - 1: 0}
    block = lambda n: pltpu.VMEM((rows, n), jnp.bfloat16)

    def kernel(*refs):
        late_kernel(is_mine, *refs)

    return pl.pallas_call(
        kernel,
        in_specs=specs,
        out_specs=ANY,
        out_shape=jax.ShapeDtypeStruct((8, 3, rows // 4, rows), jnp.float32),
        scratch_shapes=[
            pltpu.VMEM((2, rows, width), jnp.bfloat16),
            block(width),
            block(width),
            block(half),
            block(half),
            pltpu.VMEM((3, 4, rows // 4, rows), jnp.float32),
            pltpu.SemaphoreType.DMA((7,)),
            pltpu.SemaphoreType.DMA((3,)),
        ],
        input_output_aliases=aliases,
        compiler_params=PARAMS,
        cost_estimate=COST,
    )(info, *arrays)


def gather_kernel(info, early, late, from_previous, third_back, third_ahead, from_other, from_diagonal, out):
    yh, z = info[YH], info[Z]

    def put(dyh, dz, value):
        out[(yh + dyh) % 2 * 4 + (z + dz) % 4] = value

    slices = out.shape[1]
    put(0, 0, early[:slices])
    put(0, 1, late[0])
    put(0, 2, third_back[:slices] + third_ahead[:slices])
    put(0, 3, from_previous[0])
    put(1, 0, early[2 * slices : 3 * slices] + from_other[slices : 2 * slices])
    put(1, 1, from_other[:slices])
    put(1, 2, from_previous[2] + from_diagonal[...])
    put(1, 3, from_previous[1])


def gathered(info, *parts):
    slices, rows = parts[1].shape[1:]
    return pl.pallas_call(
        gather_kernel,
        in_specs=[SMEM] + [VMEM] * len(parts),
        out_specs=VMEM,
        out_shape=jax.ShapeDtypeStruct((8, slices, rows), jnp.float32),
    )(info, *parts)


def final_kernel(info, found, swapped, root, out):
    rows = swapped.shape[0]
    core, by_row = info[CORE], info[BY_ROW]

    for is_first in (True, False):

        @pl.when(jnp.logical_and(by_row == 1, (core == 0) == is_first))
        def _(is_first=is_first):
            kept = found[:rows] if is_first else found[rows:]
            pair = (kept, swapped[...]) if is_first else (swapped[...], kept)
            out[...] = jnp.concatenate(pair, 1) / root[...]

    @pl.when(by_row == 0)
    def _():
        out[...] = found[...].T / root[...]


def finished(info, found, swapped, root):
    return pl.pallas_call(
        final_kernel,
        in_specs=[SMEM, VMEM, VMEM, VMEM],
        out_specs=VMEM,
        out_shape=jax.ShapeDtypeStruct(root.shape, jnp.float32),
    )(info, found, swapped, root)


def per_device(spectra, labels, wedges, shells, shell_weight):
    rows, width = spectra.shape
    half, slices = width // 2, rows // 4
    classes = wedges.shape[0]
    blk = lax.axis_index("blk")
    core, z, yh = blk % 2, (blk // 2) % 4, blk // 8
    freq = lax.axis_index("freq")

    def place(dyh, dz):
        return ((yh + dyh) % 2) * 4 + (z + dz) % 4

    def ahead(a, b):
        return ((a - b) % 8 < 4).astype(jnp.int32)

    def columns(block, which):
        return lax.dynamic_slice_in_dim(block, which * half, half, 1)

    low, lower = z < 2, yh == 0
    high = z // 2
    previous_high = ((z + 3) % 4) // 2
    step_y, step_z = (freq // 4 + yh) % 2, (freq % 4 - z) % 4
    same_y = step_y == 0
    inner_z = jnp.logical_or(z == 1, z == 2)
    by_row = jnp.where(
        step_z == 0,
        jnp.logical_or(same_y, yh == 1),
        jnp.where(step_z == 1, False, jnp.where(step_z == 2, jnp.where(same_y, inner_z, lower), True)),
    )
    info = jnp.stack(
        [
            core,
            yh,
            z,
            high,
            ((z + 1) % 4) // 2,
            previous_high,
            ahead(place(0, 1), place(0, 0)),
            jnp.where(low, ahead(place(0, 1), place(0, -1)), ahead(place(0, -1), place(0, 1))),
            ahead(place(0, 1), place(1, 0)),
            jnp.where(lower, ahead(place(0, 1), place(1, -1)), ahead(place(1, -1), place(0, 1))),
            lower.astype(jnp.int32),
            low.astype(jnp.int32),
            jnp.int32(1),
            by_row.astype(jnp.int32),
            freq % 4,
        ]
    ).astype(jnp.int32)

    class_range = jnp.arange(classes, dtype=jnp.int32)
    own_labels = lax.dynamic_slice_in_dim(labels, blk * rows, rows)
    hot = (own_labels[:, None] == class_range[None, :]).astype(jnp.bfloat16)
    own, to_partner, to_next, to_previous, pairs = masked_blocks(info, hot, spectra, wedges)

    following_a = send(to_previous, dz=-1)
    partner_a = send(to_partner, dyh=1)
    previous = send(to_next, dz=1)
    sibling = send(own, dc=1)
    own, shells = together(own, shells)
    weight = pair_weights(shell_weight, shells[None, :])
    q1, own_w = first_tiles(info, own, sibling, weight)
    p1 = summed_along_x(q1)
    own_e, q1 = together(own, q1)
    squares = own_e.astype(jnp.float32) ** 2 * weight
    partial_energy = lax.dot_general(
        pairs.astype(jnp.float32), squares, (((1,), (1,)), ((), ())), precision=lax.Precision.HIGHEST
    )
    to_previous_b, to_partner_b = columns(own_e, 1 - previous_high), columns(own_e, yh)
    following_a, partner_a, previous, p1, partial_energy, to_previous_b, to_partner_b = together(
        following_a, partner_a, previous, p1, partial_energy, to_previous_b, to_partner_b
    )
    following_b = send(to_previous_b, dz=-1)
    partner_b = send(to_partner_b, dyh=1)
    diagonal = send(partner_a, dz=1)
    partner_s = send(partner_a, dc=1)
    third_a_s = send(jnp.where(low, following_a, previous), dc=1)
    half_pair = half_tiles(
        ((LOWER, ONE, CORE, YH), (LOW, ON_B3, ON_B3, HIGH)), info, partner_a, own, partner_s, sibling, own, partner_a,
        following_a, previous, third_a_s, third_a_s, previous, following_a, weight, partial_energy,
    )
    half_parts = [send(half_pair[1], dx=1), send(half_pair[2], dx=2), send(half_pair[3], dx=-1)]
    following_b, partner_b, diagonal, kept, half_parts[0], half_parts[2] = together(
        following_b, partner_b, diagonal, half_pair[0], half_parts[0], half_parts[2]
    )

    following_as = send(following_a, dc=1)
    following_bs = send(following_b, dc=1)
    diagonal_s = send(diagonal, dc=1)
    late = late_tiles(
        True, info, own, own_w, partner_a, partner_b, following_a, following_b, following_a, following_b,
        diagonal, diagonal, weight,
    )
    late, following_as, following_bs, diagonal_s, *half_pair = together(
        late, following_as, following_bs, diagonal_s, kept, *half_parts
    )
    half_pair = half_pair[0] + half_pair[1] + half_pair[2] + half_pair[3]

    own_yl = freq // 4

    def halves(which):
        return [
            lax.dynamic_index_in_dim(p1, which, 0, keepdims=False),
            lax.dynamic_slice_in_dim(half_pair[1], which * slices, slices, 0),
            lax.dynamic_slice_in_dim(half_pair[0], which * slices, slices, 0),
            half_pair[0, 2 * slices :],
        ]

    early = send(jnp.concatenate(halves(1 - own_yl)), dyl=1)
    late = late_tiles(
        False, info, own, own_w, partner_a, partner_b, following_as, following_bs, following_a, following_b,
        diagonal, diagonal_s, weight, late,
    )
    late, early = together(late, early)
    late = lax.all_to_all(late, "freq", 0, 0, tiled=True)

    early = jnp.concatenate(halves(own_yl)) + early
    third, energy = early[slices : 2 * slices], early[3 * slices :]
    third_energy = jnp.concatenate([third, energy])
    back, forth, opposite = send(third_energy, dz=1), send(third_energy, dz=-1), send(energy, dz=2)
    fourth_plane = jnp.concatenate(
        [early[2 * slices : 3 * slices], energy, forth[slices:], opposite, back[slices:]]
    )
    late, fourth_plane = together(late, fourth_plane)
    sixth = jnp.sum(late[:, 2], 0)
    late = jnp.sum(late, 0)

    from_previous = send(late, dz=1)
    from_other = send(jnp.concatenate([late[1], fourth_plane]), dyh=1)
    from_diagonal = send(sixth, dyh=1, dz=-1)
    from_previous, from_other, from_diagonal = together(from_previous, from_other, from_diagonal)
    pieces = gathered(info, early, late, from_previous, back, forth, from_other, from_diagonal)
    found = lax.all_to_all(pieces, "freq", 0, 0, tiled=True).reshape(2 * rows, rows)
    swapped = send(lax.dynamic_slice_in_dim(found, (1 - core) * rows, rows, 0), dc=1)

    energies = jnp.concatenate([fourth_plane[slices:], from_other[2 * slices :]])
    energies_s = send(energies, dc=1)
    column_energy = [
        lax.dynamic_slice_in_dim(e, (step_y * 4 + step_z) * classes, classes, 0) for e in (energies, energies_s)
    ]
    column_energy = jnp.where(
        core == 0, jnp.concatenate(column_energy, 1), jnp.concatenate(column_energy[::-1], 1)
    )
    labels, pieces = together(labels, pieces)
    own_labels = lax.dynamic_slice_in_dim(labels, blk * rows, rows)
    column_labels = lax.dynamic_slice_in_dim(labels, freq * 2 * rows, 2 * rows)
    row_side = jnp.zeros((rows, 2 * rows), jnp.float32)
    column_side = jnp.zeros((rows, 2 * rows), jnp.float32)
    for d in range(classes):
        row_side = jnp.where(column_labels[None, :] == d, energy[d][:, None], row_side)
        column_side = jnp.where(own_labels[:, None] == d, column_energy[d][None, :], column_side)
    root = jnp.sqrt(row_side * column_side + 1e-06)
    found, root = together(found, root)
    return finished(info, found, swapped, root)


def solution(mesh):
    placed = (P("blk", "freq"), P(), P(None, "freq"), P("freq"), P())
    return jax.shard_map(
        per_device, mesh=mesh, in_specs=placed, out_specs=P("blk", "freq"), check_vma=False
    )
```

```python
import jax
import jax.numpy as jnp
from jax import lax
from jax.experimental import pallas as pl
from jax.experimental.pallas import tpu as pltpu
from jax.sharding import PartitionSpec as P

BOTH = ("blk", "freq")
VMEM_BYTES = 54 * 1024 * 1024
LANES = 128
PARAMS = pltpu.CompilerParams(vmem_limit_bytes=VMEM_BYTES)
COST = pl.CostEstimate(flops=1024, bytes_accessed=1024, transcendentals=0)
VMEM = pl.BlockSpec(memory_space=pltpu.VMEM)
SMEM = pl.BlockSpec(memory_space=pltpu.SMEM)
ANY = pl.BlockSpec(memory_space=pl.ANY)


def places():
    return [
        (yh, z, c, f) for yh in range(2) for z in range(4) for c in range(2) for f in range(8)
    ]


def place_index(yh, z, c, f):
    return (((yh % 2) * 4 + z % 4) * 2 + c % 2) * 8 + f % 8


def route(dyh, dz, dc, dyl, dx):
    return [
        (place_index(yh, z, c, f), place_index(yh + dyh, z + dz, c + dc, (f // 4 + dyl) * 4 + (f + dx) % 4))
        for yh, z, c, f in places()
    ]


def send(block, dyh=0, dz=0, dc=0, dyl=0, dx=0):
    return lax.ppermute(block, BOTH, route(dyh, dz, dc, dyl, dx))


def summed_along_x(tiles):
    groups = [list(range(4)), list(range(4, 8))]
    return jnp.sum(lax.all_to_all(tiles, "freq", 0, 0, axis_index_groups=groups, tiled=True), 0)


def together(*arrays):
    return lax.optimization_barrier(arrays)


def scaled(block, weight):
    return (block.astype(jnp.float32) * weight).astype(jnp.bfloat16)


def gram(a, b):
    return lax.dot_general(a, b, (((1,), (1,)), ((), ())), preferred_element_type=jnp.float32)


CORE, YH, Z, HIGH, NEXT_HIGH, PREV_HIGH, ON_B2, ON_B3, ON_B5, ON_B6, LOWER, LOW, ONE, BY_ROW, X = range(15)


def span(which, half):
    return pl.ds(pl.multiple_of(which * half, LANES), half)


def spread_pairs():
    place = lax.broadcasted_iota(jnp.int32, (LANES, 2 * LANES), 0)
    return (lax.broadcasted_iota(jnp.int32, (LANES, 2 * LANES), 1) // 2 == place).astype(jnp.bfloat16)


def mask_kernel(info, hot, spectra, wedges, own, to_partner, to_next, to_previous, pairs):
    half = spectra.shape[1] // 2

    @pl.when(pl.program_id(0) == 0)
    def _():
        spread = spread_pairs()
        for j in range(half // LANES):
            some = wedges[:, pl.ds(j * LANES, LANES)].astype(jnp.float32).astype(jnp.bfloat16)
            wide = jnp.dot(some, spread, preferred_element_type=jnp.float32)
            pairs[:, pl.ds(j * 2 * LANES, 2 * LANES)] = wide.astype(jnp.bfloat16)

    keep = jnp.dot(hot[...], pairs[...], preferred_element_type=jnp.float32).astype(jnp.bfloat16)
    own[...] = spectra[...] * keep
    to_partner[...] = own[:, span(1 - info[YH], half)]
    to_next[...] = own[:, span(info[NEXT_HIGH], half)]
    to_previous[...] = own[:, span(info[PREV_HIGH], half)]


def masked_blocks(info, hot, spectra, wedges):
    rows, width = spectra.shape
    classes = wedges.shape[0]
    part = rows // 4
    whole = lambda *shape: pl.BlockSpec(shape, lambda i, info: (0, 0))
    slab = lambda n: pl.BlockSpec((part, n), lambda i, info: (i, 0))
    half_block = jax.ShapeDtypeStruct((rows, width // 2), jnp.bfloat16)
    return pl.pallas_call(
        mask_kernel,
        grid_spec=pltpu.PrefetchScalarGridSpec(
            num_scalar_prefetch=1,
            grid=(4,),
            in_specs=[slab(classes), slab(width), whole(classes, width // 2)],
            out_specs=[slab(width)] + [slab(width // 2)] * 3 + [whole(classes, width)],
        ),
        out_shape=[
            jax.ShapeDtypeStruct((rows, width), jnp.bfloat16),
            *[half_block] * 3,
            jax.ShapeDtypeStruct((classes, width), jnp.bfloat16),
        ],
        compiler_params=PARAMS,
        cost_estimate=COST,
    )(info, hot, spectra, wedges)


def weight_kernel(shell_weight, shells, weight):
    spread = spread_pairs()

    def widen(x):
        return jnp.dot(x, spread, preferred_element_type=jnp.float32)

    for j in range(shells.shape[1] // LANES):
        shell = shells[:, pl.ds(j * LANES, LANES)]
        value = jnp.zeros(shell.shape, jnp.float32)
        for k in range(shell_weight.shape[0]):
            value = jnp.where(shell == k, shell_weight[k], value)
        top = value.astype(jnp.bfloat16)
        rest = value - top.astype(jnp.float32)
        middle = rest.astype(jnp.bfloat16)
        low = (rest - middle.astype(jnp.float32)).astype(jnp.bfloat16)
        weight[:, pl.ds(j * 2 * LANES, 2 * LANES)] = (widen(top) + widen(middle)) + widen(low)


def pair_weights(shell_weight, shells):
    return pl.pallas_call(
        weight_kernel,
        in_specs=[SMEM, VMEM],
        out_specs=VMEM,
        out_shape=jax.ShapeDtypeStruct((1, 2 * shells.shape[1]), jnp.float32),
        compiler_params=PARAMS,
        cost_estimate=COST,
    )(shell_weight, shells)


def first_kernel(info, own, sibling, weight, out, own_w, a, other, tiles, sems, out_sems):
    core = info[CORE]
    got_own = pltpu.make_async_copy(own, a.at[0], sems.at[0])
    got_sibling = pltpu.make_async_copy(sibling, other.at[0], sems.at[1])
    got_own.start()
    got_sibling.start()

    def leave(k, owner):
        copy = pltpu.make_async_copy(tiles.at[k], out.at[:, owner], out_sems.at[k])
        copy.start()
        return copy

    def put(k, tile):
        tiles[k] = tile.reshape(tiles.shape[1:])

    got_own.wait()
    a[1] = scaled(a[0], weight[...])
    left_w = pltpu.make_async_copy(a.at[1], own_w, out_sems.at[2])
    left_w.start()
    put(0, gram(a[1], a[0]))
    left_mine = leave(0, core)
    got_sibling.wait()

    @pl.when(core == 1)
    def _():
        other[1] = scaled(other[0], weight[...])

    put(1, gram(other[core], a[1 - core]))
    left_other = leave(1, 1 - core)
    left_w.wait()
    left_mine.wait()
    left_other.wait()


def first_tiles(info, own, sibling, weight):
    rows, width = own.shape
    block = pltpu.VMEM((2, rows, width), jnp.bfloat16)
    return pl.pallas_call(
        first_kernel,
        in_specs=[SMEM, ANY, ANY, VMEM],
        out_specs=[ANY, ANY],
        out_shape=[
            jax.ShapeDtypeStruct((4, 2, rows // 4, rows), jnp.float32),
            jax.ShapeDtypeStruct((rows, width), jnp.bfloat16),
        ],
        scratch_shapes=[
            block,
            block,
            pltpu.VMEM((2, 4, rows // 4, rows), jnp.float32),
            pltpu.SemaphoreType.DMA((2,)),
            pltpu.SemaphoreType.DMA((3,)),
        ],
        compiler_params=PARAMS,
        cost_estimate=COST,
    )(info, own, sibling, weight)


def half_kernel(jobs, info, *refs):
    operands, (weight, energy), outs, (a, b, tiles, sems, out_sems) = refs[:-11], refs[-11:-9], refs[-9:-5], refs[-5:]
    rows, half = b.shape[2:]
    slices = tiles.shape[3]
    core = info[CORE]
    sent = []

    def go(src, dst, n):
        copy = pltpu.make_async_copy(src, dst, out_sems.at[n])
        copy.start()
        sent.append(copy)

    def fetch(k, first_at, half_at):
        first, at = info[first_at] == 1, span(info[half_at], half)

        def pick(n, dst, yes, no):
            for chosen, src in ((first, yes), (jnp.logical_not(first), no)):
                src = src if src.shape[1] == half else src.at[:, at]

                @pl.when(chosen)
                def _(src=src):
                    pltpu.make_async_copy(src, dst, sems.at[k, n]).start()

            return pltpu.make_async_copy(src, dst, sems.at[k, n])

        a_yes, a_no, other_yes, other_no, b_yes, b_no = operands[6 * k : 6 * k + 6]
        got_b = pick(0, b.at[k, 0], b_yes, b_no)
        return got_b, [pick(1, a.at[k, 0], a_yes, a_no), pick(2, a.at[k, 2], other_yes, other_no)]

    got = [fetch(k, job[0], job[3]) for k, job in enumerate(jobs)]
    for k in range(len(jobs)):
        for x in range(4):
            go(energy, outs[x].at[k, pl.ds(2 * slices, energy.shape[0])], 12 * k + 8 + x)
    for k, (_, on_b_at, on_b_other_at, half_at) in enumerate(jobs):
        got_b, got_a = got[k]
        w = weight[:, span(info[half_at], half)]
        got_b.wait()
        b[k, 1] = scaled(b[k, 0], w)
        for n, (on_b, owner) in enumerate(((info[on_b_at], core), (info[on_b_other_at], 1 - core))):
            got_a[n].wait()

            @pl.when(on_b == 0)
            def _(n=n, k=k, w=w):
                a[k, 2 * n + 1] = scaled(a[k, 2 * n], w)

            tiles[k, n] = gram(a[k, 2 * n + 1 - on_b], b[k, on_b]).reshape(tiles.shape[2:])
            at = pl.ds(pl.multiple_of(owner * slices, 8), slices)
            for x in range(4):
                go(tiles.at[k, n, (info[X] + x) % 4], outs[x].at[k, at], 12 * k + 4 * n + x)
    for copy in sent:
        copy.wait()


def half_tiles(jobs, info, *operands):
    rows, classes = operands[0].shape[0], operands[-1].shape[0]
    half = operands[-2].shape[1] // 2

    def kernel(*refs):
        half_kernel(jobs, *refs)

    return pl.pallas_call(
        kernel,
        in_specs=[SMEM] + [ANY] * (len(operands) - 2) + [VMEM] * 2,
        out_specs=[ANY] * 4,
        out_shape=[jax.ShapeDtypeStruct((2, rows // 2 + classes, rows), jnp.float32)] * 4,
        scratch_shapes=[
            pltpu.VMEM((2, 4, rows, half), jnp.bfloat16),
            pltpu.VMEM((2, 2, rows, half), jnp.bfloat16),
            pltpu.VMEM((2, 2, 4, rows // 4, rows), jnp.float32),
            pltpu.SemaphoreType.DMA((2, 3)),
            pltpu.SemaphoreType.DMA((24,)),
        ],
        compiler_params=PARAMS,
        cost_estimate=COST,
    )(info, *operands)


def late_kernel(
    is_mine, info, own, own_w, partner_a, partner_b, a_high, a_low, mine_high, mine_low, diagonal, a_diagonal,
    weight, *rest,
):
    out, a, own_b, partner, sixth_a, sixth_b, tiles, sems, out_sems = rest[-9:]
    half = partner_a.shape[1]
    slices = out.shape[2]
    lower = info[YH] == 0
    high_is_yh = info[HIGH] == info[YH]
    high, yh = info[HIGH], info[YH]

    def pick(n, dst, *choices):
        for chosen, src in choices:

            @pl.when(chosen)
            def _(src=src):
                pltpu.make_async_copy(src, dst, sems.at[n]).start()

        return pltpu.make_async_copy(choices[0][1], dst, sems.at[n])

    always = info[CORE] >= 0
    no = jnp.logical_not
    got_b = pick(
        6,
        sixth_b,
        (lower, diagonal),
        (jnp.logical_and(no(lower), high_is_yh), mine_high),
        (jnp.logical_and(no(lower), no(high_is_yh)), mine_low),
    )
    got_a = pick(
        5,
        sixth_a,
        (no(lower), a_diagonal),
        (jnp.logical_and(lower, high_is_yh), a_high),
        (jnp.logical_and(lower, no(high_is_yh)), a_low),
    )
    got_high = pick(0, a.at[0, :, span(high, half)], (always, a_high))
    got_low = pick(1, a.at[0, :, span(1 - high, half)], (always, a_low))
    got_own = pick(2, own_b, (info[ON_B2] == 1, own_w), (info[ON_B2] == 0, own))
    got_near = pick(3, partner.at[:, span(yh, half)], (always, partner_a))
    got_far = pick(4, partner.at[:, span(1 - yh, half)], (always, partner_b))
    owner = info[CORE] if is_mine else 1 - info[CORE]
    sent = []

    def put(k, tile):
        tiles[k] = tile.reshape(4, slices, tile.shape[1])

    def leave(k):
        copy = pltpu.make_async_copy(tiles.at[k], out.at[pl.ds(owner * 4, 4), k], out_sems.at[k])
        copy.start()
        sent.append(copy)

    got_a.wait()
    got_b.wait()
    w_yh = weight[:, span(yh, half)]

    @pl.when(info[ON_B6] == 1)
    def _():
        sixth_b[...] = scaled(sixth_b[...], w_yh)

    @pl.when(info[ON_B6] == 0)
    def _():
        sixth_a[...] = scaled(sixth_a[...], w_yh)

    put(2, gram(sixth_a[...], sixth_b[...]))
    leave(2)
    got_high.wait()
    got_low.wait()
    a[1] = scaled(a[0], weight[...])
    got_own.wait()
    put(0, gram(a[1 - info[ON_B2]], own_b[...]))
    leave(0)
    got_near.wait()
    got_far.wait()

    @pl.when(info[ON_B5] == 1)
    def _():
        partner[...] = scaled(partner[...], weight[...])

    put(1, gram(a[1 - info[ON_B5]], partner[...]))
    leave(1)
    for copy in sent:
        copy.wait()


def late_tiles(is_mine, info, own, own_w, partner_a, partner_b, a_high, a_low, mine_high, mine_low, diagonal,
               a_diagonal, weight, other=None):
    rows, width = own.shape
    half = width // 2
    arrays = [own, own_w, partner_a, partner_b, a_high, a_low, mine_high, mine_low, diagonal, a_diagonal, weight]
    specs = [SMEM] + [ANY] * 10 + [VMEM]
    aliases = {}
    if other is not None:
        arrays.append(other)
        specs.append(ANY)
        aliases = {len(specs) - 1: 0}
    block = lambda n: pltpu.VMEM((rows, n), jnp.bfloat16)

    def kernel(*refs):
        late_kernel(is_mine, *refs)

    return pl.pallas_call(
        kernel,
        in_specs=specs,
        out_specs=ANY,
        out_shape=jax.ShapeDtypeStruct((8, 3, rows // 4, rows), jnp.float32),
        scratch_shapes=[
            pltpu.VMEM((2, rows, width), jnp.bfloat16),
            block(width),
            block(width),
            block(half),
            block(half),
            pltpu.VMEM((3, 4, rows // 4, rows), jnp.float32),
            pltpu.SemaphoreType.DMA((7,)),
            pltpu.SemaphoreType.DMA((3,)),
        ],
        input_output_aliases=aliases,
        compiler_params=PARAMS,
        cost_estimate=COST,
    )(info, *arrays)


def gather_kernel(info, early, late, from_previous, third_back, third_ahead, from_other, from_diagonal, out):
    yh, z = info[YH], info[Z]

    def put(dyh, dz, value):
        out[(yh + dyh) % 2 * 4 + (z + dz) % 4] = value

    slices = out.shape[1]
    put(0, 0, early[:slices])
    put(0, 1, late[0])
    put(0, 2, third_back[:slices] + third_ahead[:slices])
    put(0, 3, from_previous[0])
    put(1, 0, early[2 * slices : 3 * slices] + from_other[slices : 2 * slices])
    put(1, 1, from_other[:slices])
    put(1, 2, from_previous[2] + from_diagonal[...])
    put(1, 3, from_previous[1])


def gathered(info, *parts):
    slices, rows = parts[1].shape[1:]
    return pl.pallas_call(
        gather_kernel,
        in_specs=[SMEM] + [VMEM] * len(parts),
        out_specs=VMEM,
        out_shape=jax.ShapeDtypeStruct((8, slices, rows), jnp.float32),
    )(info, *parts)


def final_kernel(info, found, swapped, root, out):
    rows = swapped.shape[0]
    core, by_row = info[CORE], info[BY_ROW]

    for is_first in (True, False):

        @pl.when(jnp.logical_and(by_row == 1, (core == 0) == is_first))
        def _(is_first=is_first):
            kept = found[:rows] if is_first else found[rows:]
            pair = (kept, swapped[...]) if is_first else (swapped[...], kept)
            out[...] = jnp.concatenate(pair, 1) / root[...]

    @pl.when(by_row == 0)
    def _():
        out[...] = found[...].T / root[...]


def finished(info, found, swapped, root):
    return pl.pallas_call(
        final_kernel,
        in_specs=[SMEM, VMEM, VMEM, VMEM],
        out_specs=VMEM,
        out_shape=jax.ShapeDtypeStruct(root.shape, jnp.float32),
    )(info, found, swapped, root)


def per_device(spectra, labels, wedges, shells, shell_weight):
    rows, width = spectra.shape
    half, slices = width // 2, rows // 4
    classes = wedges.shape[0]
    blk = lax.axis_index("blk")
    core, z, yh = blk % 2, (blk // 2) % 4, blk // 8
    freq = lax.axis_index("freq")

    def place(dyh, dz):
        return ((yh + dyh) % 2) * 4 + (z + dz) % 4

    def ahead(a, b):
        return ((a - b) % 8 < 4).astype(jnp.int32)

    def columns(block, which):
        return lax.dynamic_slice_in_dim(block, which * half, half, 1)

    low, lower = z < 2, yh == 0
    high = z // 2
    previous_high = ((z + 3) % 4) // 2
    step_y, step_z = (freq // 4 + yh) % 2, (freq % 4 - z) % 4
    same_y = step_y == 0
    inner_z = jnp.logical_or(z == 1, z == 2)
    by_row = jnp.where(
        step_z == 0,
        jnp.logical_or(same_y, yh == 1),
        jnp.where(step_z == 1, False, jnp.where(step_z == 2, jnp.where(same_y, inner_z, lower), True)),
    )
    info = jnp.stack(
        [
            core,
            yh,
            z,
            high,
            ((z + 1) % 4) // 2,
            previous_high,
            ahead(place(0, 1), place(0, 0)),
            jnp.where(low, ahead(place(0, 1), place(0, -1)), ahead(place(0, -1), place(0, 1))),
            ahead(place(0, 1), place(1, 0)),
            jnp.where(lower, ahead(place(0, 1), place(1, -1)), ahead(place(1, -1), place(0, 1))),
            lower.astype(jnp.int32),
            low.astype(jnp.int32),
            jnp.int32(1),
            by_row.astype(jnp.int32),
            freq % 4,
        ]
    ).astype(jnp.int32)

    class_range = jnp.arange(classes, dtype=jnp.int32)
    own_labels = lax.dynamic_slice_in_dim(labels, blk * rows, rows)
    hot = (own_labels[:, None] == class_range[None, :]).astype(jnp.bfloat16)
    own, to_partner, to_next, to_previous, pairs = masked_blocks(info, hot, spectra, wedges)

    following_a = send(to_previous, dz=-1)
    partner_a = send(to_partner, dyh=1)
    previous = send(to_next, dz=1)
    sibling = send(own, dc=1)
    own, shells = together(own, shells)
    weight = pair_weights(shell_weight, shells[None, :])
    q1, own_w = first_tiles(info, own, sibling, weight)
    p1 = summed_along_x(q1)
    own_e, q1 = together(own, q1)
    squares = own_e.astype(jnp.float32) ** 2 * weight
    partial_energy = lax.dot_general(
        pairs.astype(jnp.float32), squares, (((1,), (1,)), ((), ())), precision=lax.Precision.HIGHEST
    )
    to_previous_b, to_partner_b = columns(own_e, 1 - previous_high), columns(own_e, yh)
    following_a, partner_a, previous, p1, partial_energy, to_previous_b, to_partner_b = together(
        following_a, partner_a, previous, p1, partial_energy, to_previous_b, to_partner_b
    )
    following_b = send(to_previous_b, dz=-1)
    partner_b = send(to_partner_b, dyh=1)
    diagonal = send(partner_a, dz=1)
    partner_s = send(partner_a, dc=1)
    third_a_s = send(jnp.where(low, following_a, previous), dc=1)
    half_pair = half_tiles(
        ((LOWER, ONE, CORE, YH), (LOW, ON_B3, ON_B3, HIGH)), info, partner_a, own, partner_s, sibling, own, partner_a,
        following_a, previous, third_a_s, third_a_s, previous, following_a, weight, partial_energy,
    )
    half_parts = [send(half_pair[1], dx=1), send(half_pair[2], dx=2), send(half_pair[3], dx=-1)]
    following_b, partner_b, diagonal, kept, half_parts[0], half_parts[2] = together(
        following_b, partner_b, diagonal, half_pair[0], half_parts[0], half_parts[2]
    )

    following_as = send(following_a, dc=1)
    following_bs = send(following_b, dc=1)
    diagonal_s = send(diagonal, dc=1)
    late = late_tiles(
        True, info, own, own_w, partner_a, partner_b, following_a, following_b, following_a, following_b,
        diagonal, diagonal, weight,
    )
    late, following_as, following_bs, diagonal_s, *half_pair = together(
        late, following_as, following_bs, diagonal_s, kept, *half_parts
    )
    half_pair = half_pair[0] + half_pair[1] + half_pair[2] + half_pair[3]

    own_yl = freq // 4

    def halves(which):
        return [
            lax.dynamic_index_in_dim(p1, which, 0, keepdims=False),
            lax.dynamic_slice_in_dim(half_pair[1], which * slices, slices, 0),
            lax.dynamic_slice_in_dim(half_pair[0], which * slices, slices, 0),
            half_pair[0, 2 * slices :],
        ]

    early = send(jnp.concatenate(halves(1 - own_yl)), dyl=1)
    late = late_tiles(
        False, info, own, own_w, partner_a, partner_b, following_as, following_bs, following_a, following_b,
        diagonal, diagonal_s, weight, late,
    )
    late, early = together(late, early)
    late = lax.all_to_all(late, "freq", 0, 0, tiled=True)

    early = jnp.concatenate(halves(own_yl)) + early
    third, energy = early[slices : 2 * slices], early[3 * slices :]
    third_energy = jnp.concatenate([third, energy])
    back, forth, opposite = send(third_energy, dz=1), send(third_energy, dz=-1), send(energy, dz=2)
    fourth_plane = jnp.concatenate(
        [early[2 * slices : 3 * slices], energy, forth[slices:], opposite, back[slices:]]
    )
    late, fourth_plane = together(late, fourth_plane)
    sixth = jnp.sum(late[:, 2], 0)
    late = jnp.sum(late, 0)

    from_previous = send(late, dz=1)
    from_other = send(jnp.concatenate([late[1], fourth_plane]), dyh=1)
    from_diagonal = send(sixth, dyh=1, dz=-1)
    from_previous, from_other, from_diagonal = together(from_previous, from_other, from_diagonal)
    pieces = gathered(info, early, late, from_previous, back, forth, from_other, from_diagonal)
    found = lax.all_to_all(pieces, "freq", 0, 0, tiled=True).reshape(2 * rows, rows)
    swapped = send(lax.dynamic_slice_in_dim(found, (1 - core) * rows, rows, 0), dc=1)

    energies = jnp.concatenate([fourth_plane[slices:], from_other[2 * slices :]])
    energies_s = send(energies, dc=1)
    column_energy = [
        lax.dynamic_slice_in_dim(e, (step_y * 4 + step_z) * classes, classes, 0) for e in (energies, energies_s)
    ]
    column_energy = jnp.where(
        core == 0, jnp.concatenate(column_energy, 1), jnp.concatenate(column_energy[::-1], 1)
    )
    labels, pieces = together(labels, pieces)
    own_labels = lax.dynamic_slice_in_dim(labels, blk * rows, rows)
    column_labels = lax.dynamic_slice_in_dim(labels, freq * 2 * rows, 2 * rows)
    row_side = jnp.zeros((rows, 2 * rows), jnp.float32)
    column_side = jnp.zeros((rows, 2 * rows), jnp.float32)
    for d in range(classes):
        row_side = jnp.where(column_labels[None, :] == d, energy[d][:, None], row_side)
        column_side = jnp.where(own_labels[:, None] == d, column_energy[d][None, :], column_side)
    root = jnp.sqrt(row_side * column_side + 1e-06)
    found, root = together(found, root)
    return finished(info, found, swapped, root)


def solution(mesh):
    placed = (P("blk", "freq"), P(), P(None, "freq"), P("freq"), P())
    return jax.shard_map(
        per_device, mesh=mesh, in_specs=placed, out_specs=P("blk", "freq"), check_vma=False
    )
```

```python
import jax
import jax.numpy as jnp
from jax import lax
from jax.experimental import pallas as pl
from jax.experimental.pallas import tpu as pltpu
from jax.sharding import PartitionSpec as P

BOTH = ("blk", "freq")
VMEM_BYTES = 54 * 1024 * 1024
LANES = 128
PARAMS = pltpu.CompilerParams(vmem_limit_bytes=VMEM_BYTES)
COST = pl.CostEstimate(flops=1024, bytes_accessed=1024, transcendentals=0)
VMEM = pl.BlockSpec(memory_space=pltpu.VMEM)
SMEM = pl.BlockSpec(memory_space=pltpu.SMEM)
ANY = pl.BlockSpec(memory_space=pl.ANY)


def places():
    return [
        (yh, z, c, f) for yh in range(2) for z in range(4) for c in range(2) for f in range(8)
    ]


def place_index(yh, z, c, f):
    return (((yh % 2) * 4 + z % 4) * 2 + c % 2) * 8 + f % 8


def route(dyh, dz, dc, dyl, dx):
    return [
        (place_index(yh, z, c, f), place_index(yh + dyh, z + dz, c + dc, (f // 4 + dyl) * 4 + (f + dx) % 4))
        for yh, z, c, f in places()
    ]


def send(block, dyh=0, dz=0, dc=0, dyl=0, dx=0):
    return lax.ppermute(block, BOTH, route(dyh, dz, dc, dyl, dx))


def summed_along_x(tiles):
    groups = [list(range(4)), list(range(4, 8))]
    return jnp.sum(lax.all_to_all(tiles, "freq", 0, 0, axis_index_groups=groups, tiled=True), 0)


def together(*arrays):
    return lax.optimization_barrier(arrays)


def scaled(block, weight):
    return (block.astype(jnp.float32) * weight).astype(jnp.bfloat16)


def gram(a, b):
    return lax.dot_general(a, b, (((1,), (1,)), ((), ())), preferred_element_type=jnp.float32)


CORE, YH, Z, HIGH, NEXT_HIGH, PREV_HIGH, ON_B2, ON_B3, ON_B5, ON_B6, LOWER, LOW, ONE, BY_ROW, X = range(15)


def span(which, half):
    return pl.ds(pl.multiple_of(which * half, LANES), half)


def spread_pairs():
    place = lax.broadcasted_iota(jnp.int32, (LANES, 2 * LANES), 0)
    return (lax.broadcasted_iota(jnp.int32, (LANES, 2 * LANES), 1) // 2 == place).astype(jnp.bfloat16)


def mask_kernel(info, hot, spectra, wedges, own, to_partner, to_next, to_previous, pairs):
    half = spectra.shape[1] // 2

    @pl.when(pl.program_id(0) == 0)
    def _():
        spread = spread_pairs()
        for j in range(half // LANES):
            some = wedges[:, pl.ds(j * LANES, LANES)].astype(jnp.float32).astype(jnp.bfloat16)
            wide = jnp.dot(some, spread, preferred_element_type=jnp.float32)
            pairs[:, pl.ds(j * 2 * LANES, 2 * LANES)] = wide.astype(jnp.bfloat16)

    keep = jnp.dot(hot[...], pairs[...], preferred_element_type=jnp.float32).astype(jnp.bfloat16)
    own[...] = spectra[...] * keep
    to_partner[...] = own[:, span(1 - info[YH], half)]
    to_next[...] = own[:, span(info[NEXT_HIGH], half)]
    to_previous[...] = own[:, span(info[PREV_HIGH], half)]


def masked_blocks(info, hot, spectra, wedges):
    rows, width = spectra.shape
    classes = wedges.shape[0]
    part = rows // 4
    whole = lambda *shape: pl.BlockSpec(shape, lambda i, info: (0, 0))
    slab = lambda n: pl.BlockSpec((part, n), lambda i, info: (i, 0))
    half_block = jax.ShapeDtypeStruct((rows, width // 2), jnp.bfloat16)
    return pl.pallas_call(
        mask_kernel,
        grid_spec=pltpu.PrefetchScalarGridSpec(
            num_scalar_prefetch=1,
            grid=(4,),
            in_specs=[slab(classes), slab(width), whole(classes, width // 2)],
            out_specs=[slab(width)] + [slab(width // 2)] * 3 + [whole(classes, width)],
        ),
        out_shape=[
            jax.ShapeDtypeStruct((rows, width), jnp.bfloat16),
            *[half_block] * 3,
            jax.ShapeDtypeStruct((classes, width), jnp.bfloat16),
        ],
        compiler_params=PARAMS,
        cost_estimate=COST,
    )(info, hot, spectra, wedges)


def weight_kernel(shell_weight, shells, weight):
    spread = spread_pairs()

    def widen(x):
        return jnp.dot(x, spread, preferred_element_type=jnp.float32)

    for j in range(shells.shape[1] // LANES):
        shell = shells[:, pl.ds(j * LANES, LANES)]
        value = jnp.zeros(shell.shape, jnp.float32)
        for k in range(shell_weight.shape[0]):
            value = jnp.where(shell == k, shell_weight[k], value)
        top = value.astype(jnp.bfloat16)
        rest = value - top.astype(jnp.float32)
        middle = rest.astype(jnp.bfloat16)
        low = (rest - middle.astype(jnp.float32)).astype(jnp.bfloat16)
        weight[:, pl.ds(j * 2 * LANES, 2 * LANES)] = (widen(top) + widen(middle)) + widen(low)


def pair_weights(shell_weight, shells):
    return pl.pallas_call(
        weight_kernel,
        in_specs=[SMEM, VMEM],
        out_specs=VMEM,
        out_shape=jax.ShapeDtypeStruct((1, 2 * shells.shape[1]), jnp.float32),
        compiler_params=PARAMS,
        cost_estimate=COST,
    )(shell_weight, shells)


def first_kernel(info, own, sibling, weight, out, own_w, a, other, tiles, sems, out_sems):
    core = info[CORE]
    got_own = pltpu.make_async_copy(own, a.at[0], sems.at[0])
    got_sibling = pltpu.make_async_copy(sibling, other.at[0], sems.at[1])
    got_own.start()
    got_sibling.start()

    def leave(k, owner):
        copy = pltpu.make_async_copy(tiles.at[k], out.at[:, owner], out_sems.at[k])
        copy.start()
        return copy

    def put(k, tile):
        tiles[k] = tile.reshape(tiles.shape[1:])

    got_own.wait()
    a[1] = scaled(a[0], weight[...])
    left_w = pltpu.make_async_copy(a.at[1], own_w, out_sems.at[2])
    left_w.start()
    put(0, gram(a[1], a[0]))
    left_mine = leave(0, core)
    got_sibling.wait()

    @pl.when(core == 1)
    def _():
        other[1] = scaled(other[0], weight[...])

    put(1, gram(other[core], a[1 - core]))
    left_other = leave(1, 1 - core)
    left_w.wait()
    left_mine.wait()
    left_other.wait()


def first_tiles(info, own, sibling, weight):
    rows, width = own.shape
    block = pltpu.VMEM((2, rows, width), jnp.bfloat16)
    return pl.pallas_call(
        first_kernel,
        in_specs=[SMEM, ANY, ANY, VMEM],
        out_specs=[ANY, ANY],
        out_shape=[
            jax.ShapeDtypeStruct((4, 2, rows // 4, rows), jnp.float32),
            jax.ShapeDtypeStruct((rows, width), jnp.bfloat16),
        ],
        scratch_shapes=[
            block,
            block,
            pltpu.VMEM((2, 4, rows // 4, rows), jnp.float32),
            pltpu.SemaphoreType.DMA((2,)),
            pltpu.SemaphoreType.DMA((3,)),
        ],
        compiler_params=PARAMS,
        cost_estimate=COST,
    )(info, own, sibling, weight)


def half_kernel(jobs, info, *refs):
    operands, (weight, energy), outs, (a, b, tiles, sems, out_sems) = refs[:-11], refs[-11:-9], refs[-9:-5], refs[-5:]
    rows, half = b.shape[2:]
    slices = tiles.shape[3]
    core = info[CORE]
    sent = []

    def go(src, dst, n):
        copy = pltpu.make_async_copy(src, dst, out_sems.at[n])
        copy.start()
        sent.append(copy)

    def fetch(k, first_at, half_at):
        first, at = info[first_at] == 1, span(info[half_at], half)

        def pick(n, dst, yes, no):
            for chosen, src in ((first, yes), (jnp.logical_not(first), no)):
                src = src if src.shape[1] == half else src.at[:, at]

                @pl.when(chosen)
                def _(src=src):
                    pltpu.make_async_copy(src, dst, sems.at[k, n]).start()

            return pltpu.make_async_copy(src, dst, sems.at[k, n])

        a_yes, a_no, other_yes, other_no, b_yes, b_no = operands[6 * k : 6 * k + 6]
        got_b = pick(0, b.at[k, 0], b_yes, b_no)
        return got_b, [pick(1, a.at[k, 0], a_yes, a_no), pick(2, a.at[k, 2], other_yes, other_no)]

    got = [fetch(k, job[0], job[3]) for k, job in enumerate(jobs)]
    for k in range(len(jobs)):
        for x in range(4):
            go(energy, outs[x].at[k, pl.ds(2 * slices, energy.shape[0])], 12 * k + 8 + x)
    for k, (_, on_b_at, on_b_other_at, half_at) in enumerate(jobs):
        got_b, got_a = got[k]
        w = weight[:, span(info[half_at], half)]
        got_b.wait()
        b[k, 1] = scaled(b[k, 0], w)
        for n, (on_b, owner) in enumerate(((info[on_b_at], core), (info[on_b_other_at], 1 - core))):
            got_a[n].wait()

            @pl.when(on_b == 0)
            def _(n=n, k=k, w=w):
                a[k, 2 * n + 1] = scaled(a[k, 2 * n], w)

            tiles[k, n] = gram(a[k, 2 * n + 1 - on_b], b[k, on_b]).reshape(tiles.shape[2:])
            at = pl.ds(pl.multiple_of(owner * slices, 8), slices)
            for x in range(4):
                go(tiles.at[k, n, (info[X] + x) % 4], outs[x].at[k, at], 12 * k + 4 * n + x)
    for copy in sent:
        copy.wait()


def half_tiles(jobs, info, *operands):
    rows, classes = operands[0].shape[0], operands[-1].shape[0]
    half = operands[-2].shape[1] // 2

    def kernel(*refs):
        half_kernel(jobs, *refs)

    return pl.pallas_call(
        kernel,
        in_specs=[SMEM] + [ANY] * (len(operands) - 2) + [VMEM] * 2,
        out_specs=[ANY] * 4,
        out_shape=[jax.ShapeDtypeStruct((2, rows // 2 + classes, rows), jnp.float32)] * 4,
        scratch_shapes=[
            pltpu.VMEM((2, 4, rows, half), jnp.bfloat16),
            pltpu.VMEM((2, 2, rows, half), jnp.bfloat16),
            pltpu.VMEM((2, 2, 4, rows // 4, rows), jnp.float32),
            pltpu.SemaphoreType.DMA((2, 3)),
            pltpu.SemaphoreType.DMA((24,)),
        ],
        compiler_params=PARAMS,
        cost_estimate=COST,
    )(info, *operands)


def late_kernel(
    is_mine, info, own, own_w, partner_a, partner_b, a_high, a_low, mine_high, mine_low, diagonal, a_diagonal,
    weight, *rest,
):
    out, a, own_b, partner, sixth_a, sixth_b, tiles, sems, out_sems = rest[-9:]
    half = partner_a.shape[1]
    slices = out.shape[2]
    lower = info[YH] == 0
    high_is_yh = info[HIGH] == info[YH]
    high, yh = info[HIGH], info[YH]

    def pick(n, dst, *choices):
        for chosen, src in choices:

            @pl.when(chosen)
            def _(src=src):
                pltpu.make_async_copy(src, dst, sems.at[n]).start()

        return pltpu.make_async_copy(choices[0][1], dst, sems.at[n])

    always = info[CORE] >= 0
    no = jnp.logical_not
    got_b = pick(
        6,
        sixth_b,
        (lower, diagonal),
        (jnp.logical_and(no(lower), high_is_yh), mine_high),
        (jnp.logical_and(no(lower), no(high_is_yh)), mine_low),
    )
    got_a = pick(
        5,
        sixth_a,
        (no(lower), a_diagonal),
        (jnp.logical_and(lower, high_is_yh), a_high),
        (jnp.logical_and(lower, no(high_is_yh)), a_low),
    )
    got_high = pick(0, a.at[0, :, span(high, half)], (always, a_high))
    got_low = pick(1, a.at[0, :, span(1 - high, half)], (always, a_low))
    got_own = pick(2, own_b, (info[ON_B2] == 1, own_w), (info[ON_B2] == 0, own))
    got_near = pick(3, partner.at[:, span(yh, half)], (always, partner_a))
    got_far = pick(4, partner.at[:, span(1 - yh, half)], (always, partner_b))
    owner = info[CORE] if is_mine else 1 - info[CORE]
    sent = []

    def put(k, tile):
        tiles[k] = tile.reshape(4, slices, tile.shape[1])

    def leave(k):
        copy = pltpu.make_async_copy(tiles.at[k], out.at[pl.ds(owner * 4, 4), k], out_sems.at[k])
        copy.start()
        sent.append(copy)

    got_a.wait()
    got_b.wait()
    w_yh = weight[:, span(yh, half)]

    @pl.when(info[ON_B6] == 1)
    def _():
        sixth_b[...] = scaled(sixth_b[...], w_yh)

    @pl.when(info[ON_B6] == 0)
    def _():
        sixth_a[...] = scaled(sixth_a[...], w_yh)

    put(2, gram(sixth_a[...], sixth_b[...]))
    leave(2)
    got_high.wait()
    got_low.wait()
    a[1] = scaled(a[0], weight[...])
    got_own.wait()
    put(0, gram(a[1 - info[ON_B2]], own_b[...]))
    leave(0)
    got_near.wait()
    got_far.wait()

    @pl.when(info[ON_B5] == 1)
    def _():
        partner[...] = scaled(partner[...], weight[...])

    put(1, gram(a[1 - info[ON_B5]], partner[...]))
    leave(1)
    for copy in sent:
        copy.wait()


def late_tiles(is_mine, info, own, own_w, partner_a, partner_b, a_high, a_low, mine_high, mine_low, diagonal,
               a_diagonal, weight, other=None):
    rows, width = own.shape
    half = width // 2
    arrays = [own, own_w, partner_a, partner_b, a_high, a_low, mine_high, mine_low, diagonal, a_diagonal, weight]
    specs = [SMEM] + [ANY] * 10 + [VMEM]
    aliases = {}
    if other is not None:
        arrays.append(other)
        specs.append(ANY)
        aliases = {len(specs) - 1: 0}
    block = lambda n: pltpu.VMEM((rows, n), jnp.bfloat16)

    def kernel(*refs):
        late_kernel(is_mine, *refs)

    return pl.pallas_call(
        kernel,
        in_specs=specs,
        out_specs=ANY,
        out_shape=jax.ShapeDtypeStruct((8, 3, rows // 4, rows), jnp.float32),
        scratch_shapes=[
            pltpu.VMEM((2, rows, width), jnp.bfloat16),
            block(width),
            block(width),
            block(half),
            block(half),
            pltpu.VMEM((3, 4, rows // 4, rows), jnp.float32),
            pltpu.SemaphoreType.DMA((7,)),
            pltpu.SemaphoreType.DMA((3,)),
        ],
        input_output_aliases=aliases,
        compiler_params=PARAMS,
        cost_estimate=COST,
    )(info, *arrays)


def gather_kernel(info, early, late, from_previous, third_back, third_ahead, from_other, from_diagonal, out):
    yh, z = info[YH], info[Z]

    def put(dyh, dz, value):
        out[(yh + dyh) % 2 * 4 + (z + dz) % 4] = value

    slices = out.shape[1]
    put(0, 0, early[:slices])
    put(0, 1, late[0])
    put(0, 2, third_back[:slices] + third_ahead[:slices])
    put(0, 3, from_previous[0])
    put(1, 0, early[2 * slices : 3 * slices] + from_other[slices : 2 * slices])
    put(1, 1, from_other[:slices])
    put(1, 2, from_previous[2] + from_diagonal[...])
    put(1, 3, from_previous[1])


def gathered(info, *parts):
    slices, rows = parts[1].shape[1:]
    return pl.pallas_call(
        gather_kernel,
        in_specs=[SMEM] + [VMEM] * len(parts),
        out_specs=VMEM,
        out_shape=jax.ShapeDtypeStruct((8, slices, rows), jnp.float32),
    )(info, *parts)


def final_kernel(info, found, swapped, root, out):
    rows = swapped.shape[0]
    core, by_row = info[CORE], info[BY_ROW]

    for is_first in (True, False):

        @pl.when(jnp.logical_and(by_row == 1, (core == 0) == is_first))
        def _(is_first=is_first):
            kept = found[:rows] if is_first else found[rows:]
            pair = (kept, swapped[...]) if is_first else (swapped[...], kept)
            out[...] = jnp.concatenate(pair, 1) / root[...]

    @pl.when(by_row == 0)
    def _():
        out[...] = found[...].T / root[...]


def finished(info, found, swapped, root):
    return pl.pallas_call(
        final_kernel,
        in_specs=[SMEM, VMEM, VMEM, VMEM],
        out_specs=VMEM,
        out_shape=jax.ShapeDtypeStruct(root.shape, jnp.float32),
    )(info, found, swapped, root)


def per_device(spectra, labels, wedges, shells, shell_weight):
    rows, width = spectra.shape
    half, slices = width // 2, rows // 4
    classes = wedges.shape[0]
    blk = lax.axis_index("blk")
    core, z, yh = blk % 2, (blk // 2) % 4, blk // 8
    freq = lax.axis_index("freq")

    def place(dyh, dz):
        return ((yh + dyh) % 2) * 4 + (z + dz) % 4

    def ahead(a, b):
        return ((a - b) % 8 < 4).astype(jnp.int32)

    def columns(block, which):
        return lax.dynamic_slice_in_dim(block, which * half, half, 1)

    low, lower = z < 2, yh == 0
    high = z // 2
    previous_high = ((z + 3) % 4) // 2
    step_y, step_z = (freq // 4 + yh) % 2, (freq % 4 - z) % 4
    same_y = step_y == 0
    inner_z = jnp.logical_or(z == 1, z == 2)
    by_row = jnp.where(
        step_z == 0,
        jnp.logical_or(same_y, yh == 1),
        jnp.where(step_z == 1, False, jnp.where(step_z == 2, jnp.where(same_y, inner_z, lower), True)),
    )
    info = jnp.stack(
        [
            core,
            yh,
            z,
            high,
            ((z + 1) % 4) // 2,
            previous_high,
            ahead(place(0, 1), place(0, 0)),
            jnp.where(low, ahead(place(0, 1), place(0, -1)), ahead(place(0, -1), place(0, 1))),
            ahead(place(0, 1), place(1, 0)),
            jnp.where(lower, ahead(place(0, 1), place(1, -1)), ahead(place(1, -1), place(0, 1))),
            lower.astype(jnp.int32),
            low.astype(jnp.int32),
            jnp.int32(1),
            by_row.astype(jnp.int32),
            freq % 4,
        ]
    ).astype(jnp.int32)

    class_range = jnp.arange(classes, dtype=jnp.int32)
    own_labels = lax.dynamic_slice_in_dim(labels, blk * rows, rows)
    hot = (own_labels[:, None] == class_range[None, :]).astype(jnp.bfloat16)
    own, to_partner, to_next, to_previous, pairs = masked_blocks(info, hot, spectra, wedges)

    following_a = send(to_previous, dz=-1)
    partner_a = send(to_partner, dyh=1)
    previous = send(to_next, dz=1)
    sibling = send(own, dc=1)
    own, shells = together(own, shells)
    weight = pair_weights(shell_weight, shells[None, :])
    q1, own_w = first_tiles(info, own, sibling, weight)
    p1 = summed_along_x(q1)
    own_e, q1 = together(own, q1)
    squares = own_e.astype(jnp.float32) ** 2 * weight
    partial_energy = lax.dot_general(
        pairs.astype(jnp.float32), squares, (((1,), (1,)), ((), ())), precision=lax.Precision.HIGHEST
    )
    to_previous_b, to_partner_b = columns(own_e, 1 - previous_high), columns(own_e, yh)
    following_a, partner_a, previous, p1, partial_energy, to_previous_b, to_partner_b = together(
        following_a, partner_a, previous, p1, partial_energy, to_previous_b, to_partner_b
    )
    following_b = send(to_previous_b, dz=-1)
    partner_b = send(to_partner_b, dyh=1)
    diagonal = send(partner_a, dz=1)
    partner_s = send(partner_a, dc=1)
    third_a_s = send(jnp.where(low, following_a, previous), dc=1)
    half_pair = half_tiles(
        ((LOWER, ONE, CORE, YH), (LOW, ON_B3, ON_B3, HIGH)), info, partner_a, own, partner_s, sibling, own, partner_a,
        following_a, previous, third_a_s, third_a_s, previous, following_a, weight, partial_energy,
    )
    half_parts = [send(half_pair[1], dx=1), send(half_pair[2], dx=2), send(half_pair[3], dx=-1)]
    following_b, partner_b, diagonal, kept, half_parts[0], half_parts[1] = together(
        following_b, partner_b, diagonal, half_pair[0], half_parts[0], half_parts[1]
    )

    following_as = send(following_a, dc=1)
    following_bs = send(following_b, dc=1)
    diagonal_s = send(diagonal, dc=1)
    late = late_tiles(
        True, info, own, own_w, partner_a, partner_b, following_a, following_b, following_a, following_b,
        diagonal, diagonal, weight,
    )
    late, following_as, following_bs, diagonal_s, *half_pair = together(
        late, following_as, following_bs, diagonal_s, kept, *half_parts
    )
    half_pair = half_pair[0] + half_pair[1] + half_pair[2] + half_pair[3]

    own_yl = freq // 4

    def halves(which):
        return [
            lax.dynamic_index_in_dim(p1, which, 0, keepdims=False),
            lax.dynamic_slice_in_dim(half_pair[1], which * slices, slices, 0),
            lax.dynamic_slice_in_dim(half_pair[0], which * slices, slices, 0),
            half_pair[0, 2 * slices :],
        ]

    early = send(jnp.concatenate(halves(1 - own_yl)), dyl=1)
    late = late_tiles(
        False, info, own, own_w, partner_a, partner_b, following_as, following_bs, following_a, following_b,
        diagonal, diagonal_s, weight, late,
    )
    late, early = together(late, early)
    late = lax.all_to_all(late, "freq", 0, 0, tiled=True)

    early = jnp.concatenate(halves(own_yl)) + early
    third, energy = early[slices : 2 * slices], early[3 * slices :]
    third_energy = jnp.concatenate([third, energy])
    back, forth, opposite = send(third_energy, dz=1), send(third_energy, dz=-1), send(energy, dz=2)
    fourth_plane = jnp.concatenate(
        [early[2 * slices : 3 * slices], energy, forth[slices:], opposite, back[slices:]]
    )
    late, fourth_plane = together(late, fourth_plane)
    sixth = jnp.sum(late[:, 2], 0)
    late = jnp.sum(late, 0)

    from_previous = send(late, dz=1)
    from_other = send(jnp.concatenate([late[1], fourth_plane]), dyh=1)
    from_diagonal = send(sixth, dyh=1, dz=-1)
    from_previous, from_other, from_diagonal = together(from_previous, from_other, from_diagonal)
    pieces = gathered(info, early, late, from_previous, back, forth, from_other, from_diagonal)
    found = lax.all_to_all(pieces, "freq", 0, 0, tiled=True).reshape(2 * rows, rows)
    swapped = send(lax.dynamic_slice_in_dim(found, (1 - core) * rows, rows, 0), dc=1)

    energies = jnp.concatenate([fourth_plane[slices:], from_other[2 * slices :]])
    energies_s = send(energies, dc=1)
    column_energy = [
        lax.dynamic_slice_in_dim(e, (step_y * 4 + step_z) * classes, classes, 0) for e in (energies, energies_s)
    ]
    column_energy = jnp.where(
        core == 0, jnp.concatenate(column_energy, 1), jnp.concatenate(column_energy[::-1], 1)
    )
    labels, pieces = together(labels, pieces)
    own_labels = lax.dynamic_slice_in_dim(labels, blk * rows, rows)
    column_labels = lax.dynamic_slice_in_dim(labels, freq * 2 * rows, 2 * rows)
    row_side = jnp.zeros((rows, 2 * rows), jnp.float32)
    column_side = jnp.zeros((rows, 2 * rows), jnp.float32)
    for d in range(classes):
        row_side = jnp.where(column_labels[None, :] == d, energy[d][:, None], row_side)
        column_side = jnp.where(own_labels[:, None] == d, column_energy[d][None, :], column_side)
    root = jnp.sqrt(row_side * column_side + 1e-06)
    found, root = together(found, root)
    return finished(info, found, swapped, root)


def solution(mesh):
    placed = (P("blk", "freq"), P(), P(None, "freq"), P("freq"), P())
    return jax.shard_map(
        per_device, mesh=mesh, in_specs=placed, out_specs=P("blk", "freq"), check_vma=False
    )
```
